256 devices in a mesh: dp: 8 (over y, z_lo), resp: 8 (over x, core), tensor: 4 (over z_hi).
Axes of the slice: x: 4, y: 4, z: 8 (z_hi: 4, z_lo: 2; z = z_hi * 2 + z_lo), core: 2. Of those that a mesh axis runs over, the one named last changes fastest.
Arguments:
- prompt_k: bfloat16 [32768, 512], P(('dp', 'resp', 'tensor')), parts along dimension 0, may hold values from -4 to 4
- prompt_v: bfloat16 [32768, 512], P(('dp', 'resp', 'tensor')), parts along dimension 0, may hold values from -6 to 6
- resp_q: bfloat16 [16384, 2560], P(('dp', 'resp'), 'tensor'), parts along dimension 0, may hold values from -8 to 8
- resp_k: bfloat16 [16384, 512], P(('dp', 'resp'), 'tensor'), parts along dimension 0, may hold values from -6 to 6
- resp_v: bfloat16 [16384, 512], P(('dp', 'resp'), 'tensor'), parts along dimension 0, may hold values from -6 to 6
- resp_grad: bfloat16 [16384, 2560], P(('dp', 'resp'), 'tensor'), parts along dimension 0, may hold values from -6 to 6
- lengths: int32 [64], P(('dp', 'resp')), parts along dimension 0, may hold values from 1 to 256, 1280 in all
Outputs:
- grad_q: float32 [16384, 2560], P(('dp', 'resp'), 'tensor'), parts along dimension 0
- grad_rk: float32 [16384, 512], P(('dp', 'resp'), 'tensor'), parts along dimension 0
- grad_rv: float32 [16384, 512], P(('dp', 'resp'), 'tensor'), parts along dimension 0
- grad_pk: float32 [32768, 512], P(('dp', 'resp', 'tensor')), parts along dimension 0
- grad_pv: float32 [32768, 512], P(('dp', 'resp', 'tensor')), parts along dimension 0
The draws below stay inside these ranges and needn't reach their ends.
There are 8 independent parts, one for each index of `dp`. The reference program is written for one: setup_inputs(seed, part) draws one part's arguments, and reference() takes and returns one part's arrays. A program takes and returns all parts, laid end to end along the dimension named above; each array names one. Nothing has to cross between parts.
Inputs may be any that keep to these rules, and one draw needn't show every extreme that they name: The lengths of one prompt group sum to 1280; the longest fills its buffer.
All inputs are finite; a program needn't handle non-finite values.
Results may differ from the reference program's by a relative error of at most 0.005.
Values may be sent and summed in bfloat16 or wider, within the bound.
A program may use at most 64 MiB of HBM per device.

```python
import math
import jax
import jax.numpy as jnp
import numpy as np
from jax import lax

HEADS = 20
KV_HEADS = 4
HD = 128
RMAX = 256
PROMPT = 4096
RESP_ROWS = 2048
LIVE_TOTAL = 1280
N_RESP = 8


def draw_prompt_k(key, part):
    key = jax.random.fold_in(key, 11)
    values = jnp.clip(jax.random.normal(key, (PROMPT, KV_HEADS * HD), jnp.float32), -4.0, 4.0)
    return values.astype(jnp.bfloat16)


def draw_resp_q(key, part):
    key = jax.random.fold_in(key, 12)
    values = 2.0 * jnp.clip(jax.random.normal(key, (RESP_ROWS, HEADS * HD), jnp.float32), -4.0, 4.0)
    return values.astype(jnp.bfloat16)


def block_scale(key, extent, pieces, low, top_value):
    def one(axis_at, blocks):
        draws = jax.random.uniform(jax.random.fold_in(jax.random.fold_in(key, 6), axis_at), (blocks,), jnp.float32, low / len(pieces), top_value / len(pieces))
        return jnp.repeat(jnp.exp(draws), extent[axis_at] // blocks).reshape((-1,) + (1,) * (len(extent) - axis_at - 1))

    loudness = one(*pieces[0])
    for cut in pieces[1:]:
        loudness = loudness * one(*cut)
    return loudness


def split_up(number_of, total, most, lean):
    portions = [(1 << 20) // math.isqrt(standing ** lean) + 1 for standing in range(2, number_of + 1)]
    rest, counts = total - most - (number_of - 1), [1] * (number_of - 1)
    while rest > 0:
        free = [i for i in range(number_of - 1) if counts[i] < most]
        mass, budget = sum([portions[i] for i in free]), rest
        for i in free:
            more = min(most - counts[i], max(1, budget * portions[i] // mass), rest)
            counts[i] = counts[i] + more
            rest = rest - more
    return np.array([most] + counts)


def uneven_parts(stream_key, count, total, limit, lean):
    if count == 2:
        one = jax.random.randint(stream_key, (), max(1, total - limit), min(limit, total - 1) + 1)
        return jnp.stack([one, total - one])
    tallies = jnp.asarray(split_up(count, total, limit, lean), jnp.int32)
    twos = (count - 1) // 2
    source_of, receiver = tallies[1:1 + 2 * twos:2], tallies[2:2 + 2 * twos:2]
    margin = jnp.minimum(source_of - 1, limit - receiver)
    shifted = jax.random.randint(jax.random.fold_in(stream_key, 1), (twos,), 0, 1 << 20) % (margin + 1)
    tallies = tallies.at[1:1 + 2 * twos:2].set(source_of - shifted).at[2:2 + 2 * twos:2].set(receiver + shifted)
    return tallies[jax.random.permutation(jax.random.fold_in(stream_key, 2), count)]


def normal_values(key, shape, deviation, most, cuts=(), held_as=jnp.bfloat16):
    loudness = block_scale(key, shape, cuts, -0.22, 0.18) if cuts else 1.0
    values = jax.random.normal(key, shape, jnp.float32) * deviation * loudness
    return jnp.minimum(jnp.maximum(values, -most), most).astype(held_as)


def setup_inputs(seed: int = 0, part: int = 0) -> dict:
    seeds = jax.random.split(jax.random.key(seed), 8)
    part_keys = jax.random.split(jax.random.fold_in(seeds[7], part), 8)
    prompt_k = draw_prompt_k(jax.random.fold_in(jax.random.fold_in(seeds[7], part), 71), part)
    prompt_v = normal_values(part_keys[1], (PROMPT, KV_HEADS * HD), 1.0, 6.0, ((0, 32),))
    resp_q = draw_resp_q(jax.random.fold_in(jax.random.fold_in(seeds[7], part), 71), part)
    resp_k = normal_values(part_keys[3], (RESP_ROWS, KV_HEADS * HD), 1.0, 6.0, ((0, 8), (1, 4)))
    resp_v = normal_values(part_keys[4], (RESP_ROWS, KV_HEADS * HD), 1.0, 6.0, ((0, 8), (1, 4)))
    resp_grad = normal_values(part_keys[5], (RESP_ROWS, HEADS * HD), 1.0, 6.0, ((0, 8), (1, 4)))
    lengths = uneven_parts(part_keys[6], N_RESP, LIVE_TOTAL, RMAX, 1).astype(jnp.int32)
    return {"prompt_k": prompt_k, "prompt_v": prompt_v, "resp_q": resp_q, "resp_k": resp_k, "resp_v": resp_v, "resp_grad": resp_grad, "lengths": lengths}


very_negative = -1e30


def reference(prompt_k, prompt_v, resp_q, resp_k, resp_v, resp_grad, lengths):
    score_scale = HD ** -0.5
    group_size = HEADS // KV_HEADS
    prompt_keys = prompt_k.reshape(PROMPT, KV_HEADS, HD)
    prompt_vals = prompt_v.reshape(PROMPT, KV_HEADS, HD)
    positions = jnp.arange(RMAX, dtype=jnp.int32)
    allowed = jnp.concatenate([jnp.ones((RMAX, PROMPT), dtype=bool), positions[:, None] >= positions[None, :]], axis=1)

    def per_response(sums_now, which):
        first_row = (which * RMAX).astype(jnp.int32)
        queries = lax.dynamic_slice_in_dim(resp_q, first_row, RMAX, 0).reshape(RMAX, KV_HEADS, group_size, HD)
        own_keys = lax.dynamic_slice_in_dim(resp_k, first_row, RMAX, 0).reshape(RMAX, KV_HEADS, HD)
        own_vals = lax.dynamic_slice_in_dim(resp_v, first_row, RMAX, 0).reshape(RMAX, KV_HEADS, HD)
        grad_rows = lax.dynamic_slice_in_dim(resp_grad, first_row, RMAX, 0).reshape(RMAX, KV_HEADS, group_size, HD)
        is_live = positions < lengths[which]
        grad_rows = jnp.where(is_live[:, None, None, None], grad_rows, jnp.zeros_like(grad_rows))
        key_rows = jnp.concatenate([prompt_keys, own_keys], axis=0).astype(jnp.float32)
        val_rows = jnp.concatenate([prompt_vals, own_vals], axis=0).astype(jnp.float32)
        query_full = queries.astype(jnp.float32)
        grad_full = grad_rows.astype(jnp.float32)
        scores = jnp.einsum("qhgd,khd->hgqk", query_full, key_rows) * score_scale
        scores = jnp.where(allowed[None, None], scores, very_negative)
        peak_score = jnp.max(scores, axis=3, keepdims=True)
        weights_raw = jnp.exp(scores - peak_score)
        prob = weights_raw / jnp.sum(weights_raw, axis=3, keepdims=True)
        grad_prob = jnp.einsum("qhgd,khd->hgqk", grad_full, val_rows)
        grad_mean = jnp.sum(prob * grad_prob, axis=3, keepdims=True)
        dscore = prob * (grad_prob - grad_mean)
        prob_half = lax.optimization_barrier(prob.astype(jnp.bfloat16)).astype(jnp.float32)
        dscore_half = lax.optimization_barrier(dscore.astype(jnp.bfloat16)).astype(jnp.float32)
        grad_query = jnp.einsum("hgqk,khd->qhgd", dscore_half, key_rows) * score_scale
        grad_key = jnp.einsum("hgqk,qhgd->khd", dscore_half, query_full) * score_scale
        grad_val = jnp.einsum("hgqk,qhgd->khd", prob_half, grad_full)
        new_sums = (sums_now[0] + grad_key[:PROMPT].reshape(PROMPT, KV_HEADS * HD),
                    sums_now[1] + grad_val[:PROMPT].reshape(PROMPT, KV_HEADS * HD))
        return new_sums, (grad_query.reshape(RMAX, HEADS * HD),
                          grad_key[PROMPT:].reshape(RMAX, KV_HEADS * HD),
                          grad_val[PROMPT:].reshape(RMAX, KV_HEADS * HD))

    zero_rows = jnp.zeros((PROMPT, KV_HEADS * HD), jnp.float32)
    prompt_sums, per_rows = lax.scan(per_response, (zero_rows, zero_rows), jnp.arange(N_RESP, dtype=jnp.int32))
    grad_q = per_rows[0].reshape(RESP_ROWS, HEADS * HD)
    grad_rk = per_rows[1].reshape(RESP_ROWS, KV_HEADS * HD)
    grad_rv = per_rows[2].reshape(RESP_ROWS, KV_HEADS * HD)
    return (grad_q, grad_rk, grad_rv, prompt_sums[0], prompt_sums[1])
```

```python
import jax
import jax.numpy as jnp
from jax import lax
from jax.experimental import pallas as pl
from jax.experimental.pallas import tpu as pltpu
from jax.sharding import PartitionSpec as P

HD = 128
SCALE = HD**-0.5
LOG2E = 1.4426950408889634
NEG = -1e30
ROWS = 256
CHUNK = 256

CONTRACT_LAST = (((1,), (1,)), ((), ()))
PLAIN = (((1,), (0,)), ((), ()))


def dot(a, b, dims):
    return lax.dot_general(a, b, dims, preferred_element_type=jnp.float32)


MESH = pl.DeviceIdType.MESH
QUARTER = 128
ROUNDS = 4
TURN = (0, 1, 3, 2)
SPREAD, AHEAD, BEHIND, FAR_K, FAR_V = range(5)

FIRST = ("b0o", "b0t", "d0o", "d0t", "b1o", "b1t", "d1o", "d1t", "b2o", "b2t", "d2o", "d2t", "b3o", "b3t", "d3t", "d3o")
SECOND = ("d3o", "d3t", "b3o", "b3t", "d2o", "d2t", "b2o", "b2t", "d1o", "d1t", "d0o", "d0t", "b1o", "b1t", "b0t", "b0o")


def code(name):
    return (int(name[1]) * 2 + (name[0] == "d")) * 2 + (name[2] == "t")


def pick(step, order):
    chosen = code(order[0])
    for at, name in enumerate(order[1:], 1):
        chosen = jnp.where(step == at, code(name), chosen)
    return chosen // 2, chosen % 2


def attend(base, group, count, keys, vals, causal, qs, lives, peak, denom, weighted, peaks, exps, gprobs):
    for h in range(count):
        at, g = base + h, group + h
        scores = dot(keys, qs[g], CONTRACT_LAST) * (SCALE * LOG2E)
        if causal is not None:
            scores = jnp.where(causal, scores, NEG)
        gprob = dot(vals, lives[g], CONTRACT_LAST)
        scores = scores.reshape(CHUNK // 8, 8, ROWS)
        old = peak[g]
        new = jnp.maximum(old, jnp.max(scores, axis=0))
        raw = jnp.exp2(scores - new[None])
        shrink = jnp.exp2(old - new)
        peak[g] = new
        denom[g] = denom[g] * shrink + jnp.sum(raw, axis=0)
        weighted[g] = weighted[g] * shrink + jnp.sum(raw * gprob.reshape(raw.shape), axis=0)
        peaks[at] = new
        exps[at] = raw.reshape(CHUNK, ROWS)
        gprobs[at] = gprob


def join_sums(group, count, peak, denom, weighted, out):
    for h in range(count):
        top = jnp.max(peak[group + h], axis=0, keepdims=True)
        share = jnp.exp2(peak[group + h] - top)
        out[0, h : h + 1] = top
        out[1, h : h + 1] = jnp.sum(denom[group + h] * share, axis=0, keepdims=True)
        out[2, h : h + 1] = jnp.sum(weighted[group + h] * share, axis=0, keepdims=True)


def finish_stats(group, count, one, two, peak, weighted):
    for h in range(count):
        row = slice(h, h + 1)
        top = jnp.maximum(one[0, row], two[0, row])
        share_one, share_two = jnp.exp2(one[0, row] - top), jnp.exp2(two[0, row] - top)
        total = one[1, row] * share_one + two[1, row] * share_two
        mean = (one[2, row] * share_one + two[2, row] * share_two) / total
        peak[group + h] = jnp.broadcast_to(top + jnp.log2(total), (8, ROWS))
        weighted[group + h] = jnp.broadcast_to(mean, (8, ROWS))


def grads(base, group, count, keys, qs, lives, peak, weighted, peaks, exps, gprobs, dq):
    keys_t = keys.T
    probs, dscores = [], []
    for h in range(count):
        at, g = base + h, group + h
        factor = jnp.exp2(peaks[at] - peak[g])
        prob = exps[at].reshape(CHUNK // 8, 8, ROWS) * factor[None]
        dscore = prob * (gprobs[at].reshape(CHUNK // 8, 8, ROWS) - weighted[g][None])
        probs.append(prob.reshape(CHUNK, ROWS).astype(jnp.bfloat16))
        dscore = dscore.reshape(CHUNK, ROWS).astype(jnp.bfloat16)
        dscores.append(dscore)
        dq[g] += dot(keys_t, dscore, PLAIN)
    rows = pl.ds(group, count)
    grad_v = dot(jnp.concatenate(probs, axis=1), lives[rows].reshape(count * ROWS, HD), PLAIN)
    grad_k = dot(jnp.concatenate(dscores, axis=1), qs[rows].reshape(count * ROWS, HD), PLAIN)
    return grad_k, grad_v


def kernel(lengths, q_hbm, pk_hbm, pv_hbm, rk_hbm, rv_hbm, g_hbm, dq_hbm, drk_hbm, drv_hbm, dpk_hbm, dpv_hbm,
           q, pk, pv, rk, rv, g, dq_out, drk, drv, dpk, dpv,
           qs, lives, peak, denom, weighted, peaks, exps, gprobs, dq, dq_send, dq_in,
           stat_out, stat_in, packed, kv, own, half_out, half_in, ring_out, ring_in, z_out, z_in,
           local_s, swap_s, swap_r, stat_s, stat_r, dq_s, dq_r, get_s, get_r, half_s, half_r, ring_s, ring_r, z_s, z_r):
    heads = q.shape[1] // HD
    resp, tensor = lax.axis_index("resp"), lax.axis_index("tensor")
    chip, core = resp // 2, resp % 2
    up = {"resp": (chip + 1) % 4 * 2 + core}
    down = {"resp": (chip + 3) % 4 * 2 + core}
    twin = {"resp": chip * 2 + 1 - core}

    def along(turn):
        return {"tensor": (tensor + turn) % 4}

    def columns(index):
        return pl.ds(pl.multiple_of(index * HD, HD), HD)

    barrier = pltpu.get_barrier_semaphore()
    for other in (up, down, twin, along(1), along(2), along(3)):
        pl.semaphore_signal(barrier, inc=1, device_id=other, device_id_type=MESH)
    moves_in = [
        pltpu.make_async_copy(src, dst, local_s.at[i])
        for i, (src, dst) in enumerate(
            ((pk_hbm, pk), (pv_hbm, pv), (q_hbm, q), (g_hbm, g), (rk_hbm, rk), (rv_hbm, rv))
        )
    ]
    for move in moves_in:
        move.start()

    def send(src, dst, sems, at, to):
        return pltpu.make_async_remote_copy(
            src_ref=src, dst_ref=dst, send_sem=sems[0].at[at], recv_sem=sems[1].at[at],
            device_id=to, device_id_type=MESH,
        )

    def get(n, kind):
        b, d = 2 * n, 2 * n + 1
        if kind == SPREAD:
            ends = [(packed.at[n, part], kv.at[d, 0, part], along(TURN[n])) for part in range(2)]
        elif kind == AHEAD:
            ends = [(kv.at[d, 0, part], kv.at[b, 0, part], up) for part in range(2)]
        elif kind == BEHIND:
            ends = [(kv.at[d, 0, part], kv.at[b, 1, part], down) for part in range(2)]
        elif kind == FAR_K:
            ends = [(kv.at[b, 0, 0], kv.at[d, 1, 0], up)]
        else:
            ends = [(kv.at[b, 1, 1], kv.at[d, 1, 1], down)]
        return [send(src, dst, (get_s, get_r), (n, kind, i), to) for i, (src, dst, to) in enumerate(ends)]

    def start(copies):
        for copy in copies:
            copy.start()

    def received(copies):
        for copy in copies:
            copy.wait_recv()

    def begin(n):
        if n:
            received(get(n, SPREAD))
        start(get(n, AHEAD))
        start(get(n, BEHIND))

    def forward(n):
        received(get(n, AHEAD))
        start(get(n, FAR_K))
        received(get(n, BEHIND))
        start(get(n, FAR_V))

    def swap():
        return [
            send(ref.at[h], ref.at[heads + h], (swap_s, swap_r), (i, h), twin)
            for h in range(heads)
            for i, ref in enumerate((qs, lives))
        ]

    positions = lax.broadcasted_iota(jnp.int32, (ROWS, HD), 0)
    alive = positions < lengths[0]
    moves_in[0].wait()
    moves_in[1].wait()
    kv[1, 0, 0] = pk[:, columns(tensor)]
    kv[1, 0, 1] = pv[:, columns(tensor)]
    for n in range(1, ROUNDS):
        cols = columns((tensor + TURN[n]) % 4)
        packed[n, 0] = pk[:, cols]
        packed[n, 1] = pv[:, cols]
    pl.semaphore_wait(barrier, 6)
    begin(0)
    for n in range(1, ROUNDS):
        start(get(n, SPREAD))
    moves_in[2].wait()
    moves_in[3].wait()
    for h in range(heads):
        cols = slice(h * HD, (h + 1) * HD)
        qs[h] = q[:, cols]
        lives[h] = jnp.where(alive, g[:, cols], jnp.zeros((), jnp.bfloat16))
    start(swap())
    moves_in[4].wait()
    moves_in[5].wait()
    peak[...] = jnp.full(peak.shape, NEG, jnp.float32)
    denom[...] = jnp.zeros(denom.shape, jnp.float32)
    weighted[...] = jnp.zeros(weighted.shape, jnp.float32)
    dq[...] = jnp.zeros(dq.shape, jnp.float32)
    causal = lax.broadcasted_iota(jnp.int32, (CHUNK, ROWS), 0) <= lax.broadcasted_iota(jnp.int32, (CHUNK, ROWS), 1)
    sums = (qs, lives, peak, denom, weighted, peaks, exps, gprobs)
    steps = len(FIRST)
    attend(steps * heads, 0, heads, rk[...], rv[...], causal, *sums)

    before = {
        "b0o": (lambda: forward(0),),
        "b0t": (lambda: received(swap()),),
        "d0o": (lambda: received(get(0, FAR_K) + get(0, FAR_V)),),
        "d1o": (lambda: received(get(1, FAR_K) + get(1, FAR_V)),),
        "d2o": (lambda: received(get(2, FAR_K) + get(2, FAR_V)),),
        "d3t": (lambda: received(get(3, FAR_K) + get(3, FAR_V)),),
    }
    after = {
        "b0o": (lambda: begin(1),),
        "d0o": (lambda: forward(1),),
        "d0t": (lambda: begin(2),),
        "d1o": (lambda: forward(2), lambda: begin(3)),
        "b2t": (lambda: forward(3),),
    }

    def serve(step, order, table):
        for name, jobs in table.items():
            @pl.when(step == order.index(name))
            def _():
                for job in jobs:
                    job()

    def first(step, carry):
        chunk, half = pick(step, FIRST)
        serve(step, FIRST, before)
        keys = kv[chunk, :, 0].reshape(CHUNK, HD)
        vals = kv[chunk, :, 1].reshape(CHUNK, HD)
        attend((chunk * 2 + half) * heads, half * heads, heads, keys, vals, None, *sums)
        serve(step, FIRST, after)

        @pl.when(step == steps - 2)
        def _():
            join_sums(heads, heads, peak, denom, weighted, stat_out.at[1])
            tell(1).start()

        return carry

    def tell(half):
        return send(stat_out.at[half], stat_in.at[1 - half], (stat_s, stat_r), 1 - half, twin)

    lax.fori_loop(0, steps, first, 0)
    join_sums(0, heads, peak, denom, weighted, stat_out.at[0])
    tell(0).start()
    tell(1).wait_recv()
    finish_stats(0, heads, stat_out.at[0], stat_in.at[0], peak, weighted)

    def to_half(n, part):
        return send(half_out.at[n, part], half_in.at[n, part], (half_s, half_r), (n, part), (up, down)[part])

    def to_ring(n, way):
        return [
            send(ring_out.at[n, way, part], ring_in.at[n, way, part], (ring_s, ring_r), (n, way, part), (up, down)[way])
            for part in range(2)
        ]

    def to_holder(n):
        return [
            send(z_out.at[n, part], z_in.at[n, part], (z_s, z_r), (n, part), along(4 - TURN[n])) for part in range(2)
        ]

    def to_owner(h):
        return send(dq_send.at[h], dq_in.at[h], (dq_s, dq_r), h, twin)

    def wide(ref):
        return ref.astype(jnp.float32)

    def halves(n):
        half_out[n] = own[2 * n + 1, 1].astype(jnp.bfloat16)
        to_half(n, 0).start()
        to_half(n, 1).start()

    def relay(n):
        for way in range(2):
            to_half(n, way).wait_recv()
            part = own[2 * n, 1 - way]
            ring_out[n, way, way] = (part[way] + wide(half_in[n, way])).astype(jnp.bfloat16)
            ring_out[n, way, 1 - way] = part[1 - way].astype(jnp.bfloat16)
            start(to_ring(n, way))

    def total(n):
        received(to_ring(n, 0) + to_ring(n, 1))
        return own[2 * n + 1, 0] + wide(ring_in[n, 0]) + wide(ring_in[n, 1])

    def hand_over(n):
        z_out[n] = total(n).astype(jnp.bfloat16)
        start(to_holder(n))

    def learn():
        tell(0).wait_recv()
        finish_stats(heads, heads, stat_out.at[1], stat_in.at[1], peak, weighted)

    def return_queries():
        for h in range(heads):
            dq_send[h] = dq[heads + h].astype(jnp.bfloat16)
            to_owner(h).start()

    services = {
        "d3o": (learn,),
        "d3t": (lambda: halves(3),),
        "d2o": (lambda: relay(3),),
        "d2t": (lambda: halves(2),),
        "b2t": (lambda: hand_over(3),),
        "d1o": (lambda: relay(2),),
        "d1t": (lambda: halves(1),),
        "d0t": (lambda: halves(0), lambda: hand_over(2)),
        "b1t": (lambda: relay(1),),
        "b0t": (return_queries,),
        "b0o": (lambda: relay(0),),
    }

    def second(step, carry):
        chunk, half = pick(step, SECOND)
        keys = kv[chunk, :, 0].reshape(CHUNK, HD)
        grad_k, grad_v = grads(
            (chunk * 2 + half) * heads, half * heads, heads, keys, qs, lives, peak, weighted, peaks, exps, gprobs, dq
        )
        grad_k = (grad_k * SCALE).reshape(2, QUARTER, HD)
        grad_v = grad_v.reshape(2, QUARTER, HD)
        fresh = step % 2 == 0
        own[chunk, :, 0] = grad_k + jnp.where(fresh, 0.0, own[chunk, :, 0])
        own[chunk, :, 1] = grad_v + jnp.where(fresh, 0.0, own[chunk, :, 1])
        serve(step, SECOND, services)
        return carry

    lax.fori_loop(0, steps, second, 0)
    grad_k, grad_v = grads(steps * heads, 0, heads, rk[...], qs, lives, peak, weighted, peaks, exps, gprobs, dq)
    drk[...] = grad_k * SCALE
    drv[...] = grad_v
    hand_over(1)
    moves_out = [
        pltpu.make_async_copy(src, dst, local_s.at[6 + i])
        for i, (src, dst) in enumerate((
            (drk, drk_hbm), (drv, drv_hbm), (dq_out, dq_hbm), (dpk, dpk_hbm), (dpv, dpv_hbm)
        ))
    ]
    moves_out[0].start()
    moves_out[1].start()
    for h in range(heads):
        to_owner(h).wait_recv()
        dq_out[:, h * HD : (h + 1) * HD] = (dq[h] + wide(dq_in[h])).T * SCALE
    moves_out[2].start()
    sums_now = total(0)
    dpk[:, columns(tensor)] = sums_now[0]
    dpv[:, columns(tensor)] = sums_now[1]
    for n in reversed(range(1, ROUNDS)):
        received(to_holder(n))
        cols = columns((tensor + TURN[n]) % 4)
        dpk[:, cols] = wide(z_in[n, 0])
        dpv[:, cols] = wide(z_in[n, 1])
    moves_out[3].start()
    moves_out[4].start()
    sent = swap() + [tell(0), tell(1)] + [to_owner(h) for h in range(heads)]
    for n in range(ROUNDS):
        for kind in range(SPREAD if n else AHEAD, FAR_V + 1):
            sent += get(n, kind)
        sent += [to_half(n, 0), to_half(n, 1)] + to_ring(n, 0) + to_ring(n, 1)
        if n:
            sent += to_holder(n)
    for copy in sent:
        copy.wait_send()
    for move in moves_out:
        move.wait()


def copy_kernel(*refs):
    sems = refs[-1]
    count = (len(refs) - 1) // 3
    ins, outs, rooms = refs[:count], refs[count : 2 * count], refs[2 * count : 3 * count]
    here = [pltpu.make_async_copy(ins[i], rooms[i], sems.at[0, i]) for i in range(count)]
    away = [pltpu.make_async_copy(rooms[i], outs[i], sems.at[1, i]) for i in range(count)]
    for move in here:
        move.start()
    for i in range(count):
        here[i].wait()
        away[i].start()
    for move in away:
        move.wait()


def local(prompt_k, prompt_v, resp_q, resp_k, resp_v, resp_grad, lengths):
    heads = resp_q.shape[1] // HD
    blocks = (len(FIRST) + 1) * heads
    anywhere = pl.BlockSpec(memory_space=pl.ANY)
    f32, bf16 = jnp.float32, jnp.bfloat16
    stat = pltpu.VMEM((2 * heads, 8, ROWS), f32)
    piece = (2, QUARTER, HD)

    def sems(*shape):
        return [pltpu.SemaphoreType.DMA(shape)] * 2

    outs = tuple(jax.ShapeDtypeStruct(x.shape, f32) for x in (resp_q, resp_k, resp_v, prompt_k, prompt_v))
    flops = 10 * blocks * CHUNK * ROWS * HD
    results = pl.pallas_call(
        kernel,
        out_shape=outs,
        in_specs=[pl.BlockSpec(memory_space=pltpu.SMEM)] + [anywhere] * 6,
        out_specs=[anywhere] * 5,
        scratch_shapes=[
            *(pltpu.VMEM(x.shape, bf16) for x in (resp_q, prompt_k, prompt_v, resp_k, resp_v, resp_grad)),
            *(pltpu.VMEM(x.shape, f32) for x in outs),
            pltpu.VMEM((2 * heads, ROWS, HD), bf16),
            pltpu.VMEM((2 * heads, ROWS, HD), bf16),
            stat,
            stat,
            stat,
            pltpu.VMEM((blocks, 8, ROWS), f32),
            pltpu.VMEM((blocks, CHUNK, ROWS), f32),
            pltpu.VMEM((blocks, CHUNK, ROWS), f32),
            pltpu.VMEM((2 * heads, HD, ROWS), f32),
            pltpu.VMEM((heads, HD, ROWS), bf16),
            pltpu.VMEM((heads, HD, ROWS), bf16),
            pltpu.VMEM((2, 3, 8, ROWS), f32),
            pltpu.VMEM((2, 3, 8, ROWS), f32),
            pltpu.VMEM((ROUNDS,) + piece, bf16),
            pltpu.VMEM((2 * ROUNDS, 2) + piece, bf16),
            pltpu.VMEM((2 * ROUNDS, 2) + piece, f32),
            pltpu.VMEM((ROUNDS,) + piece, bf16),
            pltpu.VMEM((ROUNDS,) + piece, bf16),
            pltpu.VMEM((ROUNDS, 2) + piece, bf16),
            pltpu.VMEM((ROUNDS, 2) + piece, bf16),
            pltpu.VMEM((ROUNDS,) + piece, bf16),
            pltpu.VMEM((ROUNDS,) + piece, bf16),
            pltpu.SemaphoreType.DMA((11,)),
            *sems(2, heads),
            *sems(2),
            *sems(heads),
            *sems(ROUNDS, 5, 2),
            *sems(ROUNDS, 2),
            *sems(ROUNDS, 2, 2),
            *sems(ROUNDS, 2),
        ],
        compiler_params=pltpu.CompilerParams(
            vmem_limit_bytes=61 * 1024 * 1024, collective_id=0, has_side_effects=True
        ),
        cost_estimate=pl.CostEstimate(flops=flops, bytes_accessed=3 << 20, transcendentals=0),
    )(lengths, resp_q, prompt_k, prompt_v, resp_k, resp_v, resp_grad)
    return pl.pallas_call(
        copy_kernel,
        out_shape=outs,
        in_specs=[anywhere] * 5,
        out_specs=[anywhere] * 5,
        scratch_shapes=[pltpu.VMEM(x.shape, f32) for x in outs] + [pltpu.SemaphoreType.DMA((2, 5))],
        compiler_params=pltpu.CompilerParams(vmem_limit_bytes=61 * 1024 * 1024),
    )(*results)


def solution(mesh):
    rows = P(("dp", "resp", "tensor"), None)
    both = P(("dp", "resp"), "tensor")
    return jax.shard_map(
        local,
        mesh=mesh,
        in_specs=(rows, rows, both, both, both, both, P(("dp", "resp"))),
        out_specs=(both, both, both, rows, rows),
        check_vma=False,
    )
```

```python
import jax
import jax.numpy as jnp
from jax import lax
from jax.experimental import pallas as pl
from jax.experimental.pallas import tpu as pltpu
from jax.sharding import PartitionSpec as P

HD = 128
SCALE = HD**-0.5
LOG2E = 1.4426950408889634
NEG = -1e30
ROWS = 256
CHUNK = 256

CONTRACT_LAST = (((1,), (1,)), ((), ()))
PLAIN = (((1,), (0,)), ((), ()))


def dot(a, b, dims):
    return lax.dot_general(a, b, dims, preferred_element_type=jnp.float32)


MESH = pl.DeviceIdType.MESH
QUARTER = 128
ROUNDS = 4
TURN = (0, 1, 3, 2)
SPREAD, AHEAD, BEHIND, FAR_K, FAR_V = range(5)

FIRST = ("b0o", "b0t", "c0o", "c0t", "c1o", "c1t", "b1o", "b1t", "b2o", "b2t", "b3t", "d0t", "b3o", "d1t", "d0o", "d1o")
SECOND = ("d1o", "d0o", "d1t", "d0t", "b3o", "b3t", "b2o", "b2t", "b1o", "b1t", "b0o", "b0t", "c1t", "c1o", "c0t", "c0o")
BASE = {"b": 0, "c": 4, "d": 6}


def code(name):
    return (BASE[name[0]] + int(name[1])) * 2 + (name[2] == "t")


def place(letter, n):
    return BASE[letter] + n // 2, n % 2


def pick(step, order):
    chosen = code(order[0])
    for at, name in enumerate(order[1:], 1):
        chosen = jnp.where(step == at, code(name), chosen)
    return chosen // 2, chosen % 2


def attend(base, group, count, keys, vals, causal, qs, lives, peak, denom, weighted, peaks, exps, gprobs):
    for h in range(count):
        at, g = base + h, group + h
        scores = dot(keys, qs[g], CONTRACT_LAST) * (SCALE * LOG2E)
        if causal is not None:
            scores = jnp.where(causal, scores, NEG)
        gprob = dot(vals, lives[g], CONTRACT_LAST)
        scores = scores.reshape(CHUNK // 8, 8, ROWS)
        old = peak[g]
        new = jnp.maximum(old, jnp.max(scores, axis=0))
        raw = jnp.exp2(scores - new[None])
        shrink = jnp.exp2(old - new)
        peak[g] = new
        denom[g] = denom[g] * shrink + jnp.sum(raw, axis=0)
        weighted[g] = weighted[g] * shrink + jnp.sum(raw * gprob.reshape(raw.shape), axis=0)
        peaks[at] = new
        exps[at] = raw.reshape(CHUNK, ROWS)
        gprobs[at] = gprob


def join_sums(group, count, peak, denom, weighted, out):
    for h in range(count):
        top = jnp.max(peak[group + h], axis=0, keepdims=True)
        share = jnp.exp2(peak[group + h] - top)
        out[0, h : h + 1] = top
        out[1, h : h + 1] = jnp.sum(denom[group + h] * share, axis=0, keepdims=True)
        out[2, h : h + 1] = jnp.sum(weighted[group + h] * share, axis=0, keepdims=True)


def finish_stats(group, count, one, two, peak, weighted):
    for h in range(count):
        row = slice(h, h + 1)
        top = jnp.maximum(one[0, row], two[0, row])
        share_one, share_two = jnp.exp2(one[0, row] - top), jnp.exp2(two[0, row] - top)
        total = one[1, row] * share_one + two[1, row] * share_two
        mean = (one[2, row] * share_one + two[2, row] * share_two) / total
        peak[group + h] = jnp.broadcast_to(top + jnp.log2(total), (8, ROWS))
        weighted[group + h] = jnp.broadcast_to(mean, (8, ROWS))


def grads(base, group, count, keys, qs, lives, peak, weighted, peaks, exps, gprobs, dq):
    keys_t = keys.T
    probs, dscores = [], []
    for h in range(count):
        at, g = base + h, group + h
        factor = jnp.exp2(peaks[at] - peak[g])
        prob = exps[at].reshape(CHUNK // 8, 8, ROWS) * factor[None]
        dscore = prob * (gprobs[at].reshape(CHUNK // 8, 8, ROWS) - weighted[g][None])
        probs.append(prob.reshape(CHUNK, ROWS).astype(jnp.bfloat16))
        dscore = dscore.reshape(CHUNK, ROWS).astype(jnp.bfloat16)
        dscores.append(dscore)
        dq[g] += dot(keys_t, dscore, PLAIN)
    rows = pl.ds(group, count)
    grad_v = dot(jnp.concatenate(probs, axis=1), lives[rows].reshape(count * ROWS, HD), PLAIN)
    grad_k = dot(jnp.concatenate(dscores, axis=1), qs[rows].reshape(count * ROWS, HD), PLAIN)
    return grad_k, grad_v


def kernel(lengths, q_hbm, pk_hbm, pv_hbm, rk_hbm, rv_hbm, g_hbm, dq_hbm, drk_hbm, drv_hbm, dpk_hbm, dpv_hbm,
           q, pk, pv, rk, rv, g, dq_out, drk, drv, dpk, dpv,
           qs, lives, peak, denom, weighted, peaks, exps, gprobs, dq, dq_send, dq_in,
           stat_out, stat_in, packed, kv, own, half_out, half_in, ring_out, ring_in, z_out, z_in,
           local_s, swap_s, swap_r, stat_s, stat_r, dq_s, dq_r, get_s, get_r, half_s, half_r, ring_s, ring_r, z_s, z_r):
    heads = q.shape[1] // HD
    resp, tensor = lax.axis_index("resp"), lax.axis_index("tensor")
    chip, core = resp // 2, resp % 2
    up = {"resp": (chip + 1) % 4 * 2 + core}
    down = {"resp": (chip + 3) % 4 * 2 + core}
    twin = {"resp": chip * 2 + 1 - core}

    def along(turn):
        return {"tensor": (tensor + turn) % 4}

    def columns(index):
        return pl.ds(pl.multiple_of(index * HD, HD), HD)

    barrier = pltpu.get_barrier_semaphore()
    for other in (up, down, twin, along(1), along(2), along(3)):
        pl.semaphore_signal(barrier, inc=1, device_id=other, device_id_type=MESH)
    moves_in = [
        pltpu.make_async_copy(src, dst, local_s.at[i])
        for i, (src, dst) in enumerate(
            ((pk_hbm, pk), (pv_hbm, pv), (q_hbm, q), (g_hbm, g), (rk_hbm, rk), (rv_hbm, rv))
        )
    ]
    for move in moves_in:
        move.start()

    def send(src, dst, sems, at, to):
        return pltpu.make_async_remote_copy(
            src_ref=src, dst_ref=dst, send_sem=sems[0].at[at], recv_sem=sems[1].at[at],
            device_id=to, device_id_type=MESH,
        )

    def get(n, kind):
        mine, far = kv.at[*place("c", n)], kv.at[*place("d", n)]
        if kind == SPREAD:
            ends = [(packed.at[n, part], mine.at[part], along(TURN[n])) for part in range(2)]
        elif kind == AHEAD:
            ends = [(mine.at[part], kv.at[n, 0, part], up) for part in range(2)]
        elif kind == BEHIND:
            ends = [(mine.at[part], kv.at[n, 1, part], down) for part in range(2)]
        elif kind == FAR_K:
            ends = [(kv.at[n, 0, 0], far.at[0], up)]
        else:
            ends = [(kv.at[n, 1, 1], far.at[1], down)]
        return [send(src, dst, (get_s, get_r), (n, kind, i), to) for i, (src, dst, to) in enumerate(ends)]

    def start(copies):
        for copy in copies:
            copy.start()

    def received(copies):
        for copy in copies:
            copy.wait_recv()

    def begin(n):
        if n:
            received(get(n, SPREAD))
        start(get(n, AHEAD))
        start(get(n, BEHIND))

    def forward(n):
        received(get(n, AHEAD))
        start(get(n, FAR_K))
        received(get(n, BEHIND))
        start(get(n, FAR_V))

    def swap():
        return [
            send(ref.at[h], ref.at[heads + h], (swap_s, swap_r), (i, h), twin)
            for h in range(heads)
            for i, ref in enumerate((qs, lives))
        ]

    positions = lax.broadcasted_iota(jnp.int32, (ROWS, HD), 0)
    alive = positions < lengths[0]
    moves_in[0].wait()
    moves_in[1].wait()
    kv[4, 0, 0] = pk[:, columns(tensor)]
    kv[4, 0, 1] = pv[:, columns(tensor)]
    for n in range(1, ROUNDS):
        cols = columns((tensor + TURN[n]) % 4)
        packed[n, 0] = pk[:, cols]
        packed[n, 1] = pv[:, cols]
    pl.semaphore_wait(barrier, 6)
    begin(0)
    for n in range(1, ROUNDS):
        start(get(n, SPREAD))
    moves_in[2].wait()
    moves_in[3].wait()
    for h in range(heads):
        cols = slice(h * HD, (h + 1) * HD)
        qs[h] = q[:, cols]
        lives[h] = jnp.where(alive, g[:, cols], jnp.zeros((), jnp.bfloat16))
    start(swap())
    moves_in[4].wait()
    moves_in[5].wait()
    peak[...] = jnp.full(peak.shape, NEG, jnp.float32)
    denom[...] = jnp.zeros(denom.shape, jnp.float32)
    weighted[...] = jnp.zeros(weighted.shape, jnp.float32)
    dq[...] = jnp.zeros(dq.shape, jnp.float32)
    own[...] = jnp.zeros(own.shape, jnp.float32)
    causal = lax.broadcasted_iota(jnp.int32, (CHUNK, ROWS), 0) <= lax.broadcasted_iota(jnp.int32, (CHUNK, ROWS), 1)
    sums = (qs, lives, peak, denom, weighted, peaks, exps, gprobs)
    steps = len(FIRST)
    attend(steps * heads, 0, heads, rk[...], rv[...], causal, *sums)

    def far_received(*rounds):
        for n in rounds:
            received(get(n, FAR_K) + get(n, FAR_V))

    before = {
        "b0o": (lambda: forward(0),),
        "b0t": (lambda: received(swap()),),
        "d0t": (lambda: far_received(0, 1),),
        "d1t": (lambda: far_received(2, 3),),
    }
    after = {
        "b0o": (lambda: begin(1), lambda: begin(2)),
        "c0t": (lambda: begin(3),),
        "c1t": (lambda: forward(1), lambda: forward(2)),
        "b2t": (lambda: forward(3),),
    }

    def serve(step, order, table):
        for name, jobs in table.items():
            @pl.when(step == order.index(name))
            def _():
                for job in jobs:
                    job()

    def first(step, carry):
        chunk, half = pick(step, FIRST)
        serve(step, FIRST, before)
        keys = kv[chunk, :, 0].reshape(CHUNK, HD)
        vals = kv[chunk, :, 1].reshape(CHUNK, HD)
        attend((chunk * 2 + half) * heads, half * heads, heads, keys, vals, None, *sums)
        serve(step, FIRST, after)

        @pl.when(step == FIRST.index("d1t"))
        def _():
            join_sums(heads, heads, peak, denom, weighted, stat_out.at[1])
            tell(1).start()

        return carry

    def tell(half):
        return send(stat_out.at[half], stat_in.at[1 - half], (stat_s, stat_r), 1 - half, twin)

    lax.fori_loop(0, steps, first, 0)
    join_sums(0, heads, peak, denom, weighted, stat_out.at[0])
    tell(0).start()
    tell(1).wait_recv()
    finish_stats(0, heads, stat_out.at[0], stat_in.at[0], peak, weighted)

    def to_half(n, part):
        return send(half_out.at[n, part], half_in.at[n, part], (half_s, half_r), (n, part), (up, down)[part])

    def to_ring(n, way):
        return [
            send(ring_out.at[n, way, part], ring_in.at[n, way, part], (ring_s, ring_r), (n, way, part), (up, down)[way])
            for part in range(2)
        ]

    def to_holder(n):
        return [
            send(z_out.at[n, part], z_in.at[n, part], (z_s, z_r), (n, part), along(4 - TURN[n])) for part in range(2)
        ]

    def to_owner(h):
        return send(dq_send.at[h], dq_in.at[h], (dq_s, dq_r), h, twin)

    def wide(ref):
        return ref.astype(jnp.float32)

    def halves(n):
        half_out[n] = own[place("d", n)].astype(jnp.bfloat16)
        to_half(n, 0).start()
        to_half(n, 1).start()

    def relay(n):
        for way in range(2):
            to_half(n, way).wait_recv()
            part = own[n, 1 - way]
            ring_out[n, way, way] = (part[way] + wide(half_in[n, way])).astype(jnp.bfloat16)
            ring_out[n, way, 1 - way] = part[1 - way].astype(jnp.bfloat16)
            start(to_ring(n, way))

    def total(n):
        received(to_ring(n, 0) + to_ring(n, 1))
        return own[place("c", n)] + wide(ring_in[n, 0]) + wide(ring_in[n, 1])

    def hand_over(n):
        z_out[n] = total(n).astype(jnp.bfloat16)
        start(to_holder(n))

    def learn():
        tell(0).wait_recv()
        finish_stats(heads, heads, stat_out.at[1], stat_in.at[1], peak, weighted)

    def return_queries():
        for h in range(heads):
            dq_send[h] = dq[heads + h].astype(jnp.bfloat16)
            to_owner(h).start()

    services = {
        "d0o": (learn,),
        "d1t": (lambda: halves(3), lambda: halves(2)),
        "d0t": (lambda: halves(1), lambda: halves(0)),
        "b2t": (lambda: relay(3), lambda: relay(2)),
        "b1t": (lambda: relay(1),),
        "b0t": (lambda: relay(0),),
        "c1o": (lambda: hand_over(3), lambda: hand_over(2)),
        "c0t": (return_queries,),
        "c0o": (lambda: hand_over(1),),
    }

    def second(step, carry):
        chunk, half = pick(step, SECOND)
        keys = kv[chunk, :, 0].reshape(CHUNK, HD)
        grad_k, grad_v = grads(
            (chunk * 2 + half) * heads, half * heads, heads, keys, qs, lives, peak, weighted, peaks, exps, gprobs, dq
        )
        grad_k = (grad_k * SCALE).reshape(2, QUARTER, HD)
        grad_v = grad_v.reshape(2, QUARTER, HD)
        own[chunk, :, 0] += grad_k
        own[chunk, :, 1] += grad_v
        serve(step, SECOND, services)
        return carry

    lax.fori_loop(0, steps, second, 0)
    grad_k, grad_v = grads(steps * heads, 0, heads, rk[...], qs, lives, peak, weighted, peaks, exps, gprobs, dq)
    drk[...] = grad_k * SCALE
    drv[...] = grad_v
    moves_out = [
        pltpu.make_async_copy(src, dst, local_s.at[6 + i])
        for i, (src, dst) in enumerate((
            (drk, drk_hbm), (drv, drv_hbm), (dq_out, dq_hbm), (dpk, dpk_hbm), (dpv, dpv_hbm)
        ))
    ]
    moves_out[0].start()
    moves_out[1].start()
    for h in range(heads):
        to_owner(h).wait_recv()
        dq_out[:, h * HD : (h + 1) * HD] = (dq[h] + wide(dq_in[h])).T * SCALE
    moves_out[2].start()
    sums_now = total(0)
    dpk[:, columns(tensor)] = sums_now[0]
    dpv[:, columns(tensor)] = sums_now[1]
    for n in reversed(range(1, ROUNDS)):
        received(to_holder(n))
        cols = columns((tensor + TURN[n]) % 4)
        dpk[:, cols] = wide(z_in[n, 0])
        dpv[:, cols] = wide(z_in[n, 1])
    moves_out[3].start()
    moves_out[4].start()
    sent = swap() + [tell(0), tell(1)] + [to_owner(h) for h in range(heads)]
    for n in range(ROUNDS):
        for kind in range(SPREAD if n else AHEAD, FAR_V + 1):
            sent += get(n, kind)
        sent += [to_half(n, 0), to_half(n, 1)] + to_ring(n, 0) + to_ring(n, 1)
        if n:
            sent += to_holder(n)
    for copy in sent:
        copy.wait_send()
    for move in moves_out:
        move.wait()


def copy_kernel(*refs):
    sems = refs[-1]
    count = (len(refs) - 1) // 3
    ins, outs, rooms = refs[:count], refs[count : 2 * count], refs[2 * count : 3 * count]
    here = [pltpu.make_async_copy(ins[i], rooms[i], sems.at[0, i]) for i in range(count)]
    away = [pltpu.make_async_copy(rooms[i], outs[i], sems.at[1, i]) for i in range(count)]
    for move in here:
        move.start()
    for i in range(count):
        here[i].wait()
        away[i].start()
    for move in away:
        move.wait()


def local(prompt_k, prompt_v, resp_q, resp_k, resp_v, resp_grad, lengths):
    heads = resp_q.shape[1] // HD
    blocks = (len(FIRST) + 1) * heads
    anywhere = pl.BlockSpec(memory_space=pl.ANY)
    f32, bf16 = jnp.float32, jnp.bfloat16
    stat = pltpu.VMEM((2 * heads, 8, ROWS), f32)
    piece = (2, QUARTER, HD)

    def sems(*shape):
        return [pltpu.SemaphoreType.DMA(shape)] * 2

    outs = tuple(jax.ShapeDtypeStruct(x.shape, f32) for x in (resp_q, resp_k, resp_v, prompt_k, prompt_v))
    flops = 10 * blocks * CHUNK * ROWS * HD
    results = pl.pallas_call(
        kernel,
        out_shape=outs,
        in_specs=[pl.BlockSpec(memory_space=pltpu.SMEM)] + [anywhere] * 6,
        out_specs=[anywhere] * 5,
        scratch_shapes=[
            *(pltpu.VMEM(x.shape, bf16) for x in (resp_q, prompt_k, prompt_v, resp_k, resp_v, resp_grad)),
            *(pltpu.VMEM(x.shape, f32) for x in outs),
            pltpu.VMEM((2 * heads, ROWS, HD), bf16),
            pltpu.VMEM((2 * heads, ROWS, HD), bf16),
            stat,
            stat,
            stat,
            pltpu.VMEM((blocks, 8, ROWS), f32),
            pltpu.VMEM((blocks, CHUNK, ROWS), f32),
            pltpu.VMEM((blocks, CHUNK, ROWS), f32),
            pltpu.VMEM((2 * heads, HD, ROWS), f32),
            pltpu.VMEM((heads, HD, ROWS), bf16),
            pltpu.VMEM((heads, HD, ROWS), bf16),
            pltpu.VMEM((2, 3, 8, ROWS), f32),
            pltpu.VMEM((2, 3, 8, ROWS), f32),
            pltpu.VMEM((ROUNDS,) + piece, bf16),
            pltpu.VMEM((2 * ROUNDS, 2) + piece, bf16),
            pltpu.VMEM((2 * ROUNDS, 2) + piece, f32),
            pltpu.VMEM((ROUNDS,) + piece, bf16),
            pltpu.VMEM((ROUNDS,) + piece, bf16),
            pltpu.VMEM((ROUNDS, 2) + piece, bf16),
            pltpu.VMEM((ROUNDS, 2) + piece, bf16),
            pltpu.VMEM((ROUNDS,) + piece, bf16),
            pltpu.VMEM((ROUNDS,) + piece, bf16),
            pltpu.SemaphoreType.DMA((11,)),
            *sems(2, heads),
            *sems(2),
            *sems(heads),
            *sems(ROUNDS, 5, 2),
            *sems(ROUNDS, 2),
            *sems(ROUNDS, 2, 2),
            *sems(ROUNDS, 2),
        ],
        compiler_params=pltpu.CompilerParams(
            vmem_limit_bytes=61 * 1024 * 1024, collective_id=0, has_side_effects=True
        ),
        cost_estimate=pl.CostEstimate(flops=flops, bytes_accessed=3 << 20, transcendentals=0),
    )(lengths, resp_q, prompt_k, prompt_v, resp_k, resp_v, resp_grad)
    return pl.pallas_call(
        copy_kernel,
        out_shape=outs,
        in_specs=[anywhere] * 5,
        out_specs=[anywhere] * 5,
        scratch_shapes=[pltpu.VMEM(x.shape, f32) for x in outs] + [pltpu.SemaphoreType.DMA((2, 5))],
        compiler_params=pltpu.CompilerParams(vmem_limit_bytes=61 * 1024 * 1024),
    )(*results)


def solution(mesh):
    rows = P(("dp", "resp", "tensor"), None)
    both = P(("dp", "resp"), "tensor")
    return jax.shard_map(
        local,
        mesh=mesh,
        in_specs=(rows, rows, both, both, both, both, P(("dp", "resp"))),
        out_specs=(both, both, both, rows, rows),
        check_vma=False,
    )
```

```python
import jax
import jax.numpy as jnp
from jax import lax
from jax.experimental import pallas as pl
from jax.experimental.pallas import tpu as pltpu
from jax.sharding import PartitionSpec as P

HD = 128
SCALE = HD**-0.5
LOG2E = 1.4426950408889634
NEG = -1e30
ROWS = 256
CHUNK = 256

CONTRACT_LAST = (((1,), (1,)), ((), ()))
PLAIN = (((1,), (0,)), ((), ()))


def dot(a, b, dims):
    return lax.dot_general(a, b, dims, preferred_element_type=jnp.float32)


MESH = pl.DeviceIdType.MESH
QUARTER = 128
ROUNDS = 4
TURN = (0, 1, 3, 2)
SPREAD, AHEAD, BEHIND, FAR_K, FAR_V, RELAY = range(6)

BASE = {"b": 0, "c": 4, "d": 6}
FIRST = ("b0", "c0", "c1", "b1", "b2", "d0")
LATE = ("b3", "d1")
SECOND = ("d1", "d0", "b3", "b2", "c1", "b1", "b0", "c0")


def code(name):
    return BASE[name[0]] + int(name[1])


def pick(step, values):
    chosen = values[0]
    for at, value in enumerate(values[1:], 1):
        chosen = jnp.where(step == at, value, chosen)
    return chosen


def place(letter, n):
    return BASE[letter] + n // 2, n % 2


def attend(base, group, count, keys, vals, causal, qs, lives, peak, denom, weighted, peaks, exps, gprobs):
    for h in range(count):
        at, g = base + h, group + h
        scores = dot(keys, qs[g], CONTRACT_LAST) * (SCALE * LOG2E)
        if causal is not None:
            scores = jnp.where(causal, scores, NEG)
        gprob = dot(vals, lives[g], CONTRACT_LAST)
        scores = scores.reshape(CHUNK // 8, 8, ROWS)
        old = peak[g]
        new = jnp.maximum(old, jnp.max(scores, axis=0))
        raw = jnp.exp2(scores - new[None])
        shrink = jnp.exp2(old - new)
        peak[g] = new
        denom[g] = denom[g] * shrink + jnp.sum(raw, axis=0)
        weighted[g] = weighted[g] * shrink + jnp.sum(raw * gprob.reshape(raw.shape), axis=0)
        peaks[at] = new
        exps[at] = raw.reshape(CHUNK, ROWS)
        gprobs[at] = gprob


def join_sums(group, count, peak, denom, weighted, out):
    for h in range(count):
        top = jnp.max(peak[group + h], axis=0, keepdims=True)
        share = jnp.exp2(peak[group + h] - top)
        out[0, h : h + 1] = top
        out[1, h : h + 1] = jnp.sum(denom[group + h] * share, axis=0, keepdims=True)
        out[2, h : h + 1] = jnp.sum(weighted[group + h] * share, axis=0, keepdims=True)


def finish_stats(group, count, one, two, peak, weighted):
    for h in range(count):
        row = slice(h, h + 1)
        top = jnp.maximum(one[0, row], two[0, row])
        share_one, share_two = jnp.exp2(one[0, row] - top), jnp.exp2(two[0, row] - top)
        total = one[1, row] * share_one + two[1, row] * share_two
        mean = (one[2, row] * share_one + two[2, row] * share_two) / total
        peak[group + h] = jnp.broadcast_to(top + jnp.log2(total), (8, ROWS))
        weighted[group + h] = jnp.broadcast_to(mean, (8, ROWS))


def grads(base, group, count, keys, qs, lives, peak, weighted, peaks, exps, gprobs, dq):
    keys_t = keys.T
    probs, dscores = [], []
    for h in range(count):
        at, g = base + h, group + h
        factor = jnp.exp2(peaks[at] - peak[g])
        prob = exps[at].reshape(CHUNK // 8, 8, ROWS) * factor[None]
        dscore = prob * (gprobs[at].reshape(CHUNK // 8, 8, ROWS) - weighted[g][None])
        probs.append(prob.reshape(CHUNK, ROWS).astype(jnp.bfloat16))
        dscore = dscore.reshape(CHUNK, ROWS).astype(jnp.bfloat16)
        dscores.append(dscore)
        dq[g] += dot(keys_t, dscore, PLAIN)
    rows = pl.ds(group, count)
    grad_v = dot(jnp.concatenate(probs, axis=1), lives[rows].reshape(count * ROWS, HD), PLAIN)
    grad_k = dot(jnp.concatenate(dscores, axis=1), qs[rows].reshape(count * ROWS, HD), PLAIN)
    return grad_k, grad_v


def kernel(lengths, q_hbm, pk_hbm, pv_hbm, rk_hbm, rv_hbm, g_hbm, dq_hbm, drk_hbm, drv_hbm, dpk_hbm, dpv_hbm,
           q, pk, pv, rk, rv, g, dq_out, drk, drv, dpk, dpv,
           qs, lives, peak, denom, weighted, peaks, exps, gprobs, dq, dq_send, dq_in,
           stat_out, stat_in, packed, passing, returning, kv, own, half_out, half_in, ring_out, ring_in, z_out, z_in,
           local_s, swap_s, swap_r, stat_s, stat_r, dq_s, dq_r, get_s, get_r, half_s, half_r, ring_s, ring_r, z_s, z_r):
    heads = q.shape[1] // HD
    resp, tensor = lax.axis_index("resp"), lax.axis_index("tensor")
    chip, core = resp // 2, resp % 2
    up = {"resp": (chip + 1) % 4 * 2 + core}
    down = {"resp": (chip + 3) % 4 * 2 + core}
    twin = {"resp": chip * 2 + 1 - core}

    def along(turn):
        return {"tensor": (tensor + turn) % 4}

    def columns(index):
        return pl.ds(pl.multiple_of(index * HD, HD), HD)

    barrier = pltpu.get_barrier_semaphore()
    for other in (up, down, twin, along(1), along(3)):
        pl.semaphore_signal(barrier, inc=1, device_id=other, device_id_type=MESH)
    moves_in = [
        pltpu.make_async_copy(src, dst, local_s.at[i])
        for i, (src, dst) in enumerate(
            ((pk_hbm, pk), (pv_hbm, pv), (q_hbm, q), (g_hbm, g), (rk_hbm, rk), (rv_hbm, rv))
        )
    ]
    for move in moves_in:
        move.start()

    def send(src, dst, sems, at, to):
        return pltpu.make_async_remote_copy(
            src_ref=src, dst_ref=dst, send_sem=sems[0].at[at], recv_sem=sems[1].at[at],
            device_id=to, device_id_type=MESH,
        )

    def get(n, kind):
        mine, far = kv.at[*place("c", n)], kv.at[*place("d", n)]
        if kind == RELAY:
            ends = [(packed.at[n, part], passing.at[part], along((1, 3)[part])) for part in range(2)]
        elif kind == SPREAD and n == 3:
            ends = [(passing.at[part], mine.at[part], along((1, 3)[part])) for part in range(2)]
        elif kind == SPREAD:
            ends = [(packed.at[n, part], mine.at[part], along(TURN[n])) for part in range(2)]
        elif kind == AHEAD:
            ends = [(mine.at[part], kv.at[n, 0, part], up) for part in range(2)]
        elif kind == BEHIND:
            ends = [(mine.at[part], kv.at[n, 1, part], down) for part in range(2)]
        elif kind == FAR_K:
            ends = [(kv.at[n, 0, 0], far.at[0], up)]
        else:
            ends = [(kv.at[n, 1, 1], far.at[1], down)]
        return [send(src, dst, (get_s, get_r), (n, kind, i), to) for i, (src, dst, to) in enumerate(ends)]

    def start(copies):
        for copy in copies:
            copy.start()

    def received(copies):
        for copy in copies:
            copy.wait_recv()

    def begin(n):
        if n:
            received(get(n, SPREAD))
        start(get(n, AHEAD))
        start(get(n, BEHIND))

    def forward(n):
        received(get(n, AHEAD))
        start(get(n, FAR_K))
        received(get(n, BEHIND))
        start(get(n, FAR_V))

    def relay_out():
        for first_hop, second_hop in zip(get(3, RELAY), get(3, SPREAD)):
            first_hop.wait_recv()
            second_hop.start()

    def swap():
        return [
            send(ref.at[h], ref.at[heads + h], (swap_s, swap_r), (i, h), twin)
            for h in range(heads)
            for i, ref in enumerate((qs, lives))
        ]

    positions = lax.broadcasted_iota(jnp.int32, (ROWS, HD), 0)
    alive = positions < lengths[0]
    moves_in[0].wait()
    moves_in[1].wait()
    kv[4, 0, 0] = pk[:, columns(tensor)]
    kv[4, 0, 1] = pv[:, columns(tensor)]
    for n in range(1, ROUNDS):
        cols = columns((tensor + TURN[n]) % 4)
        packed[n, 0] = pk[:, cols]
        packed[n, 1] = pv[:, cols]
    pl.semaphore_wait(barrier, 5)
    begin(0)
    start(get(1, SPREAD))
    start(get(2, SPREAD))
    start(get(3, RELAY))
    moves_in[2].wait()
    moves_in[3].wait()
    for h in range(heads):
        cols = slice(h * HD, (h + 1) * HD)
        qs[h] = q[:, cols]
        lives[h] = jnp.where(alive, g[:, cols], jnp.zeros((), jnp.bfloat16))
    start(swap())
    moves_in[4].wait()
    moves_in[5].wait()
    peak[...] = jnp.full(peak.shape, NEG, jnp.float32)
    denom[...] = jnp.zeros(denom.shape, jnp.float32)
    weighted[...] = jnp.zeros(weighted.shape, jnp.float32)
    dq[...] = jnp.zeros(dq.shape, jnp.float32)
    causal = lax.broadcasted_iota(jnp.int32, (CHUNK, ROWS), 0) <= lax.broadcasted_iota(jnp.int32, (CHUNK, ROWS), 1)
    sums = (qs, lives, peak, denom, weighted, peaks, exps, gprobs)
    steps = len(SECOND)
    attend(2 * steps * heads, 0, heads, rk[...], rv[...], causal, *sums)

    def far_received(*rounds):
        for n in rounds:
            received(get(n, FAR_K) + get(n, FAR_V))

    before = {
        "b0": (lambda: forward(0), lambda: received(swap())),
        "d0": (lambda: far_received(0, 1),),
    }
    after = {
        "b0": (lambda: begin(1), lambda: begin(2), relay_out),
        "c0": (lambda: begin(3),),
        "c1": (lambda: forward(1), lambda: forward(2)),
        "b2": (lambda: forward(3),),
    }

    def serve(step, order, table):
        for name, jobs in table.items():
            @pl.when(step == order.index(name))
            def _():
                for job in jobs:
                    job()

    def tell(half):
        return send(stat_out.at[half], stat_in.at[1 - half], (stat_s, stat_r), 1 - half, twin)

    def take(chunk, half):
        keys = kv[chunk, :, 0].reshape(CHUNK, HD)
        vals = kv[chunk, :, 1].reshape(CHUNK, HD)
        attend((chunk * 2 + half) * heads, half * heads, heads, keys, vals, None, *sums)

    def first(step, carry):
        chunk = pick(step, [code(name) for name in FIRST])
        serve(step, FIRST, before)
        take(chunk, 0)
        take(chunk, 1)
        serve(step, FIRST, after)
        return carry

    lax.fori_loop(0, len(FIRST), first, 0)
    far_received(2, 3)
    for name in LATE:
        take(code(name), 1)
    join_sums(heads, heads, peak, denom, weighted, stat_out.at[1])
    tell(1).start()
    for name in LATE:
        take(code(name), 0)
    join_sums(0, heads, peak, denom, weighted, stat_out.at[0])
    tell(0).start()
    for n in range(ROUNDS):
        for kind in range(SPREAD if n else AHEAD, FAR_V + 1):
            for copy in get(n, kind):
                copy.wait_send()
    for copy in get(3, RELAY) + swap():
        copy.wait_send()
    tell(1).wait_recv()
    finish_stats(0, heads, stat_out.at[0], stat_in.at[0], peak, weighted)
    tell(0).wait_recv()
    finish_stats(heads, heads, stat_out.at[1], stat_in.at[1], peak, weighted)

    def to_half(n, part):
        return send(half_out.at[n, part], half_in.at[n, part], (half_s, half_r), (n, part), (up, down)[part])

    def to_ring(n, way):
        return [
            send(ring_out.at[n, way, part], ring_in.at[n, way, part], (ring_s, ring_r), (n, way, part), (up, down)[way])
            for part in range(2)
        ]

    def to_holder(n):
        if n == 3:
            ends = [(returning.at[part], along((1, 3)[part])) for part in range(2)]
        else:
            ends = [(z_out.at[n, part], along(4 - TURN[n])) for part in range(2)]
        return [send(src, z_in.at[n, part], (z_s, z_r), (n, part), to) for part, (src, to) in enumerate(ends)]

    def to_relay():
        return [
            send(z_out.at[3, part], returning.at[part], (z_s, z_r), (0, part), along((1, 3)[part])) for part in range(2)
        ]

    def relay_back():
        for first_hop, second_hop in zip(to_relay(), to_holder(3)):
            first_hop.wait_recv()
            second_hop.start()

    def to_owner(h):
        return send(dq_send.at[h], dq_in.at[h], (dq_s, dq_r), h, twin)

    def wide(ref):
        return ref.astype(jnp.float32)

    def halves(n):
        half_out[n] = own[place("d", n)].astype(jnp.bfloat16)
        to_half(n, 0).start()
        to_half(n, 1).start()

    def relay(n):
        for way in range(2):
            to_half(n, way).wait_recv()
            part = own[n, 1 - way]
            ring_out[n, way, way] = (part[way] + wide(half_in[n, way])).astype(jnp.bfloat16)
            ring_out[n, way, 1 - way] = part[1 - way].astype(jnp.bfloat16)
            start(to_ring(n, way))

    def total(n):
        received(to_ring(n, 0) + to_ring(n, 1))
        return own[place("c", n)] + wide(ring_in[n, 0]) + wide(ring_in[n, 1])

    def hand_over(n):
        z_out[n] = total(n).astype(jnp.bfloat16)
        start(to_relay() if n == 3 else to_holder(n))

    def return_queries():
        for h in range(heads):
            dq_send[h] = dq[heads + h].astype(jnp.bfloat16)
            to_owner(h).start()

    services = {
        "d1": (lambda: halves(3), lambda: halves(2)),
        "d0": (lambda: halves(1), lambda: halves(0)),
        "b2": (lambda: relay(3), lambda: relay(2)),
        "b1": (lambda: relay(1), lambda: hand_over(3)),
        "b0": (lambda: relay(0), lambda: hand_over(2)),
        "c0": (return_queries, relay_back, lambda: hand_over(1)),
    }

    def second(step, carry):
        chunk = pick(step, [code(name) for name in SECOND])
        keys = kv[chunk, :, 0].reshape(CHUNK, HD)
        grad_k, grad_v = grads(
            chunk * 2 * heads, 0, 2 * heads, keys, qs, lives, peak, weighted, peaks, exps, gprobs, dq
        )
        own[chunk, :, 0] = (grad_k * SCALE).reshape(2, QUARTER, HD)
        own[chunk, :, 1] = grad_v.reshape(2, QUARTER, HD)
        serve(step, SECOND, services)
        return carry

    lax.fori_loop(0, steps, second, 0)
    grad_k, grad_v = grads(2 * steps * heads, 0, heads, rk[...], qs, lives, peak, weighted, peaks, exps, gprobs, dq)
    drk[...] = grad_k * SCALE
    drv[...] = grad_v
    moves_out = [
        pltpu.make_async_copy(src, dst, local_s.at[6 + i])
        for i, (src, dst) in enumerate((
            (drk, drk_hbm), (drv, drv_hbm), (dq_out, dq_hbm), (dpk, dpk_hbm), (dpv, dpv_hbm)
        ))
    ]
    moves_out[0].start()
    moves_out[1].start()
    for h in range(heads):
        to_owner(h).wait_recv()
        dq_out[:, h * HD : (h + 1) * HD] = (dq[h] + wide(dq_in[h])).T * SCALE
    moves_out[2].start()
    sums_now = total(0)
    dpk[:, columns(tensor)] = sums_now[0]
    dpv[:, columns(tensor)] = sums_now[1]
    for n in reversed(range(1, ROUNDS)):
        received(to_holder(n))
        cols = columns((tensor + TURN[n]) % 4)
        dpk[:, cols] = wide(z_in[n, 0])
        dpv[:, cols] = wide(z_in[n, 1])
    moves_out[3].start()
    moves_out[4].start()
    sent = to_relay() + [tell(0), tell(1)] + [to_owner(h) for h in range(heads)]
    for n in range(ROUNDS):
        sent += [to_half(n, 0), to_half(n, 1)] + to_ring(n, 0) + to_ring(n, 1)
        if n:
            sent += to_holder(n)
    for copy in sent:
        copy.wait_send()
    for move in moves_out:
        move.wait()


def copy_kernel(*refs):
    sems = refs[-1]
    count = (len(refs) - 1) // 3
    ins, outs, rooms = refs[:count], refs[count : 2 * count], refs[2 * count : 3 * count]
    here = [pltpu.make_async_copy(ins[i], rooms[i], sems.at[0, i]) for i in range(count)]
    away = [pltpu.make_async_copy(rooms[i], outs[i], sems.at[1, i]) for i in range(count)]
    for move in here:
        move.start()
    for i in range(count):
        here[i].wait()
        away[i].start()
    for move in away:
        move.wait()


def local(prompt_k, prompt_v, resp_q, resp_k, resp_v, resp_grad, lengths):
    heads = resp_q.shape[1] // HD
    blocks = (2 * len(SECOND) + 1) * heads
    anywhere = pl.BlockSpec(memory_space=pl.ANY)
    f32, bf16 = jnp.float32, jnp.bfloat16
    stat = pltpu.VMEM((2 * heads, 8, ROWS), f32)
    piece = (2, QUARTER, HD)

    def sems(*shape):
        return [pltpu.SemaphoreType.DMA(shape)] * 2

    outs = tuple(jax.ShapeDtypeStruct(x.shape, f32) for x in (resp_q, resp_k, resp_v, prompt_k, prompt_v))
    flops = 10 * blocks * CHUNK * ROWS * HD
    results = pl.pallas_call(
        kernel,
        out_shape=outs,
        in_specs=[pl.BlockSpec(memory_space=pltpu.SMEM)] + [anywhere] * 6,
        out_specs=[anywhere] * 5,
        scratch_shapes=[
            *(pltpu.VMEM(x.shape, bf16) for x in (resp_q, prompt_k, prompt_v, resp_k, resp_v, resp_grad)),
            *(pltpu.VMEM(x.shape, f32) for x in outs),
            pltpu.VMEM((2 * heads, ROWS, HD), bf16),
            pltpu.VMEM((2 * heads, ROWS, HD), bf16),
            stat,
            stat,
            stat,
            pltpu.VMEM((blocks, 8, ROWS), f32),
            pltpu.VMEM((blocks, CHUNK, ROWS), f32),
            pltpu.VMEM((blocks, CHUNK, ROWS), f32),
            pltpu.VMEM((2 * heads, HD, ROWS), f32),
            pltpu.VMEM((heads, HD, ROWS), bf16),
            pltpu.VMEM((heads, HD, ROWS), bf16),
            pltpu.VMEM((2, 3, 8, ROWS), f32),
            pltpu.VMEM((2, 3, 8, ROWS), f32),
            pltpu.VMEM((ROUNDS,) + piece, bf16),
            pltpu.VMEM(piece, bf16),
            pltpu.VMEM(piece, bf16),
            pltpu.VMEM((2 * ROUNDS, 2) + piece, bf16),
            pltpu.VMEM((2 * ROUNDS, 2) + piece, f32),
            pltpu.VMEM((ROUNDS,) + piece, bf16),
            pltpu.VMEM((ROUNDS,) + piece, bf16),
            pltpu.VMEM((ROUNDS, 2) + piece, bf16),
            pltpu.VMEM((ROUNDS, 2) + piece, bf16),
            pltpu.VMEM((ROUNDS,) + piece, bf16),
            pltpu.VMEM((ROUNDS,) + piece, bf16),
            pltpu.SemaphoreType.DMA((11,)),
            *sems(2, heads),
            *sems(2),
            *sems(heads),
            *sems(ROUNDS, 6, 2),
            *sems(ROUNDS, 2),
            *sems(ROUNDS, 2, 2),
            *sems(ROUNDS, 2),
        ],
        compiler_params=pltpu.CompilerParams(
            vmem_limit_bytes=61 * 1024 * 1024, collective_id=0, has_side_effects=True
        ),
        cost_estimate=pl.CostEstimate(flops=flops, bytes_accessed=3 << 20, transcendentals=0),
    )(lengths, resp_q, prompt_k, prompt_v, resp_k, resp_v, resp_grad)
    return pl.pallas_call(
        copy_kernel,
        out_shape=outs,
        in_specs=[anywhere] * 5,
        out_specs=[anywhere] * 5,
        scratch_shapes=[pltpu.VMEM(x.shape, f32) for x in outs] + [pltpu.SemaphoreType.DMA((2, 5))],
        compiler_params=pltpu.CompilerParams(vmem_limit_bytes=61 * 1024 * 1024),
    )(*results)


def solution(mesh):
    rows = P(("dp", "resp", "tensor"), None)
    both = P(("dp", "resp"), "tensor")
    return jax.shard_map(
        local,
        mesh=mesh,
        in_specs=(rows, rows, both, both, both, both, P(("dp", "resp"))),
        out_specs=(both, both, both, rows, rows),
        check_vma=False,
    )
```

```python
import jax
import jax.numpy as jnp
from jax import lax
from jax.experimental import pallas as pl
from jax.experimental.pallas import tpu as pltpu
from jax.sharding import PartitionSpec as P

HD = 128
SCALE = HD**-0.5
LOG2E = 1.4426950408889634
NEG = -1e30
ROWS = 256
CHUNK = 256

CONTRACT_LAST = (((1,), (1,)), ((), ()))
PLAIN = (((1,), (0,)), ((), ()))


def dot(a, b, dims):
    return lax.dot_general(a, b, dims, preferred_element_type=jnp.float32)


MESH = pl.DeviceIdType.MESH
QUARTER = 128
ROUNDS = 4
TURN = (0, 1, 3, 2)
SPREAD, AHEAD, BEHIND, FAR_K, FAR_V, RELAY = range(6)

BASE = {"b": 0, "c": 4, "d": 6}
FIRST = (("b0o", "c0o"), ("b0t", "c0t"), ("c1o", "c1t"), ("b1o", "b1t"), ("b2o", "b2t"), ("d0o", "d0t"))
LATE = ("b3", "d1")
SECOND = ("d1", "d0", "b3", "b2", "c1", "b1", "b0", "c0")


def code(name):
    return BASE[name[0]] + int(name[1])


def pick(step, values):
    chosen = values[0]
    for at, value in enumerate(values[1:], 1):
        chosen = jnp.where(step == at, value, chosen)
    return chosen


def place(letter, n):
    return BASE[letter] + n // 2, n % 2


def attend(base, group, count, keys, vals, causal, qs, lives, peak, denom, weighted, peaks, exps, gprobs):
    for h in range(count):
        at, g = base + h, group + h
        scores = dot(keys, qs[g], CONTRACT_LAST) * (SCALE * LOG2E)
        if causal is not None:
            scores = jnp.where(causal, scores, NEG)
        gprob = dot(vals, lives[g], CONTRACT_LAST)
        scores = scores.reshape(CHUNK // 8, 8, ROWS)
        old = peak[g]
        new = jnp.maximum(old, jnp.max(scores, axis=0))
        raw = jnp.exp2(scores - new[None])
        shrink = jnp.exp2(old - new)
        peak[g] = new
        denom[g] = denom[g] * shrink + jnp.sum(raw, axis=0)
        weighted[g] = weighted[g] * shrink + jnp.sum(raw * gprob.reshape(raw.shape), axis=0)
        peaks[at] = new
        exps[at] = raw.reshape(CHUNK, ROWS)
        gprobs[at] = gprob


def join_sums(group, count, peak, denom, weighted, out):
    for h in range(count):
        top = jnp.max(peak[group + h], axis=0, keepdims=True)
        share = jnp.exp2(peak[group + h] - top)
        out[0, h : h + 1] = top
        out[1, h : h + 1] = jnp.sum(denom[group + h] * share, axis=0, keepdims=True)
        out[2, h : h + 1] = jnp.sum(weighted[group + h] * share, axis=0, keepdims=True)


def finish_stats(group, count, one, two, peak, weighted):
    for h in range(count):
        row = slice(h, h + 1)
        top = jnp.maximum(one[0, row], two[0, row])
        share_one, share_two = jnp.exp2(one[0, row] - top), jnp.exp2(two[0, row] - top)
        total = one[1, row] * share_one + two[1, row] * share_two
        mean = (one[2, row] * share_one + two[2, row] * share_two) / total
        peak[group + h] = jnp.broadcast_to(top + jnp.log2(total), (8, ROWS))
        weighted[group + h] = jnp.broadcast_to(mean, (8, ROWS))


def grads(base, group, count, keys, qs, lives, peak, weighted, peaks, exps, gprobs, dq):
    keys_t = keys.T
    probs, dscores = [], []
    for h in range(count):
        at, g = base + h, group + h
        factor = jnp.exp2(peaks[at] - peak[g])
        prob = exps[at].reshape(CHUNK // 8, 8, ROWS) * factor[None]
        dscore = prob * (gprobs[at].reshape(CHUNK // 8, 8, ROWS) - weighted[g][None])
        probs.append(prob.reshape(CHUNK, ROWS).astype(jnp.bfloat16))
        dscore = dscore.reshape(CHUNK, ROWS).astype(jnp.bfloat16)
        dscores.append(dscore)
        dq[g] += dot(keys_t, dscore, PLAIN)
    rows = pl.ds(group, count)
    grad_v = dot(jnp.concatenate(probs, axis=1), lives[rows].reshape(count * ROWS, HD), PLAIN)
    grad_k = dot(jnp.concatenate(dscores, axis=1), qs[rows].reshape(count * ROWS, HD), PLAIN)
    return grad_k, grad_v


def kernel(lengths, q_hbm, pk_hbm, pv_hbm, rk_hbm, rv_hbm, g_hbm, dq_hbm, drk_hbm, drv_hbm, dpk_hbm, dpv_hbm,
           q, pk, pv, rk, rv, g, dq_out, drk, drv, dpk, dpv,
           qs, lives, peak, denom, weighted, peaks, exps, gprobs, dq, dq_send, dq_in,
           stat_out, stat_in, packed, passing, returning, kv, own, half_out, half_in, ring_out, ring_in, z_out, z_in,
           local_s, swap_s, swap_r, stat_s, stat_r, dq_s, dq_r, get_s, get_r, half_s, half_r, ring_s, ring_r, z_s, z_r):
    heads = q.shape[1] // HD
    resp, tensor = lax.axis_index("resp"), lax.axis_index("tensor")
    chip, core = resp // 2, resp % 2
    up = {"resp": (chip + 1) % 4 * 2 + core}
    down = {"resp": (chip + 3) % 4 * 2 + core}
    twin = {"resp": chip * 2 + 1 - core}

    def along(turn):
        return {"tensor": (tensor + turn) % 4}

    def columns(index):
        return pl.ds(pl.multiple_of(index * HD, HD), HD)

    barrier = pltpu.get_barrier_semaphore()
    for other in (up, down, twin, along(1), along(3)):
        pl.semaphore_signal(barrier, inc=1, device_id=other, device_id_type=MESH)
    moves_in = [
        pltpu.make_async_copy(src, dst, local_s.at[i])
        for i, (src, dst) in enumerate(
            ((pk_hbm, pk), (pv_hbm, pv), (q_hbm, q), (g_hbm, g), (rk_hbm, rk), (rv_hbm, rv))
        )
    ]
    for move in moves_in:
        move.start()

    def send(src, dst, sems, at, to):
        return pltpu.make_async_remote_copy(
            src_ref=src, dst_ref=dst, send_sem=sems[0].at[at], recv_sem=sems[1].at[at],
            device_id=to, device_id_type=MESH,
        )

    def get(n, kind):
        mine, far = kv.at[*place("c", n)], kv.at[*place("d", n)]
        if kind == RELAY:
            ends = [(packed.at[n, part], passing.at[part], along((1, 3)[part])) for part in range(2)]
        elif kind == SPREAD and n == 3:
            ends = [(passing.at[part], mine.at[part], along((1, 3)[part])) for part in range(2)]
        elif kind == SPREAD:
            ends = [(packed.at[n], mine, along(TURN[n]))]
        elif kind == AHEAD:
            ends = [(mine, kv.at[n, 0], up)]
        elif kind == BEHIND:
            ends = [(mine, kv.at[n, 1], down)]
        elif kind == FAR_K:
            ends = [(kv.at[n, 0, 0], far.at[0], up)]
        else:
            ends = [(kv.at[n, 1, 1], far.at[1], down)]
        return [send(src, dst, (get_s, get_r), (n, kind, i), to) for i, (src, dst, to) in enumerate(ends)]

    def start(copies):
        for copy in copies:
            copy.start()

    def received(copies):
        for copy in copies:
            copy.wait_recv()

    def begin(n):
        if n:
            received(get(n, SPREAD))
        start(get(n, AHEAD))
        start(get(n, BEHIND))

    def forward(n):
        received(get(n, AHEAD))
        start(get(n, FAR_K))
        received(get(n, BEHIND))
        start(get(n, FAR_V))

    def relay_out():
        for first_hop, second_hop in zip(get(3, RELAY), get(3, SPREAD)):
            first_hop.wait_recv()
            second_hop.start()

    def swap():
        here, there = pl.ds(0, heads), pl.ds(heads, heads)
        return [send(ref.at[here], ref.at[there], (swap_s, swap_r), i, twin) for i, ref in enumerate((qs, lives))]

    positions = lax.broadcasted_iota(jnp.int32, (ROWS, HD), 0)
    alive = positions < lengths[0]
    moves_in[0].wait()
    moves_in[1].wait()
    kv[4, 0, 0] = pk[:, columns(tensor)]
    kv[4, 0, 1] = pv[:, columns(tensor)]
    for n in range(1, ROUNDS):
        cols = columns((tensor + TURN[n]) % 4)
        packed[n, 0] = pk[:, cols]
        packed[n, 1] = pv[:, cols]
    pl.semaphore_wait(barrier, 5)
    begin(0)
    start(get(1, SPREAD))
    start(get(2, SPREAD))
    start(get(3, RELAY))
    moves_in[2].wait()
    moves_in[3].wait()
    for h in range(heads):
        cols = slice(h * HD, (h + 1) * HD)
        qs[h] = q[:, cols]
        lives[h] = jnp.where(alive, g[:, cols], jnp.zeros((), jnp.bfloat16))
    start(swap())
    moves_in[4].wait()
    moves_in[5].wait()
    peak[...] = jnp.full(peak.shape, NEG, jnp.float32)
    denom[...] = jnp.zeros(denom.shape, jnp.float32)
    weighted[...] = jnp.zeros(weighted.shape, jnp.float32)
    dq[...] = jnp.zeros(dq.shape, jnp.float32)
    causal = lax.broadcasted_iota(jnp.int32, (CHUNK, ROWS), 0) <= lax.broadcasted_iota(jnp.int32, (CHUNK, ROWS), 1)
    sums = (qs, lives, peak, denom, weighted, peaks, exps, gprobs)
    steps = len(SECOND)
    attend(2 * steps * heads, 0, heads, rk[...], rv[...], causal, *sums)

    def far_received(*rounds):
        for n in rounds:
            received(get(n, FAR_K) + get(n, FAR_V))

    before = {
        "b0o": (lambda: forward(0), lambda: begin(1), lambda: begin(2)),
        "b0t": (lambda: received(swap()),),
        "d0o": (lambda: far_received(0, 1),),
    }
    after = {
        "b0o": (relay_out,),
        "b0t": (lambda: begin(3),),
        "c1o": (lambda: forward(1), lambda: forward(2)),
        "b2o": (lambda: forward(3),),
    }

    def serve(step, order, table):
        for name, jobs in table.items():
            @pl.when(step == order.index(name))
            def _():
                for job in jobs:
                    job()

    def tell(half):
        return send(stat_out.at[half], stat_in.at[1 - half], (stat_s, stat_r), 1 - half, twin)

    def take(chunk, half):
        keys = kv[chunk, :, 0].reshape(CHUNK, HD)
        vals = kv[chunk, :, 1].reshape(CHUNK, HD)
        attend((chunk * 2 + half) * heads, half * heads, heads, keys, vals, None, *sums)

    def first(step, carry):
        leads = [pair[0] for pair in FIRST]
        serve(step, leads, before)
        for at in range(2):
            take(pick(step, [code(pair[at]) for pair in FIRST]), pick(step, [int(pair[at][2] == "t") for pair in FIRST]))
        serve(step, leads, after)
        return carry

    lax.fori_loop(0, len(FIRST), first, 0)
    far_received(2, 3)
    for name in LATE:
        take(code(name), 1)
    join_sums(heads, heads, peak, denom, weighted, stat_out.at[1])
    tell(1).start()
    for name in LATE:
        take(code(name), 0)
    join_sums(0, heads, peak, denom, weighted, stat_out.at[0])
    tell(0).start()
    for n in range(ROUNDS):
        for kind in range(SPREAD if n else AHEAD, FAR_V + 1):
            for copy in get(n, kind):
                copy.wait_send()
    for copy in get(3, RELAY) + swap():
        copy.wait_send()
    tell(1).wait_recv()
    finish_stats(0, heads, stat_out.at[0], stat_in.at[0], peak, weighted)
    tell(0).wait_recv()
    finish_stats(heads, heads, stat_out.at[1], stat_in.at[1], peak, weighted)

    def to_half(n, part):
        return send(half_out.at[n, part], half_in.at[n, part], (half_s, half_r), (n, part), (up, down)[part])

    def to_ring(n, way):
        return send(ring_out.at[n, way], ring_in.at[n, way], (ring_s, ring_r), (n, way), (up, down)[way])

    def to_holder(n):
        if n == 3:
            ends = [(returning.at[part], along((1, 3)[part])) for part in range(2)]
        else:
            return [send(z_out.at[n], z_in.at[n], (z_s, z_r), (n, 0), along(4 - TURN[n]))]
        return [send(src, z_in.at[n, part], (z_s, z_r), (n, part), to) for part, (src, to) in enumerate(ends)]

    def to_relay():
        return [
            send(z_out.at[3, part], returning.at[part], (z_s, z_r), (0, part), along((1, 3)[part])) for part in range(2)
        ]

    def relay_back():
        for first_hop, second_hop in zip(to_relay(), to_holder(3)):
            first_hop.wait_recv()
            second_hop.start()

    def to_owner():
        return send(dq_send, dq_in, (dq_s, dq_r), 0, twin)

    def wide(ref):
        return ref.astype(jnp.float32)

    def halves(n):
        half_out[n] = own[place("d", n)].astype(jnp.bfloat16)
        to_half(n, 0).start()
        to_half(n, 1).start()

    def relay(n):
        for way in range(2):
            to_half(n, way).wait_recv()
            part = own[n, 1 - way]
            ring_out[n, way, way] = (part[way] + wide(half_in[n, way])).astype(jnp.bfloat16)
            ring_out[n, way, 1 - way] = part[1 - way].astype(jnp.bfloat16)
            to_ring(n, way).start()

    def total(n):
        received([to_ring(n, 0), to_ring(n, 1)])
        return own[place("c", n)] + wide(ring_in[n, 0]) + wide(ring_in[n, 1])

    def hand_over(n):
        z_out[n] = total(n).astype(jnp.bfloat16)
        start(to_relay() if n == 3 else to_holder(n))

    def return_queries():
        for h in range(heads):
            dq_send[h] = dq[heads + h].astype(jnp.bfloat16)
        to_owner().start()

    services = {
        "d1": (lambda: halves(3), lambda: halves(2)),
        "d0": (lambda: halves(1), lambda: halves(0)),
        "b2": (lambda: relay(3), lambda: relay(2)),
        "b1": (lambda: relay(1), lambda: hand_over(3)),
        "b0": (lambda: relay(0), lambda: hand_over(2)),
        "c0": (return_queries, relay_back, lambda: hand_over(1)),
    }

    def second(step, carry):
        chunk = pick(step, [code(name) for name in SECOND])
        keys = kv[chunk, :, 0].reshape(CHUNK, HD)
        grad_k, grad_v = grads(
            chunk * 2 * heads, 0, 2 * heads, keys, qs, lives, peak, weighted, peaks, exps, gprobs, dq
        )
        own[chunk, :, 0] = (grad_k * SCALE).reshape(2, QUARTER, HD)
        own[chunk, :, 1] = grad_v.reshape(2, QUARTER, HD)
        serve(step, SECOND, services)
        return carry

    lax.fori_loop(0, steps, second, 0)
    grad_k, grad_v = grads(2 * steps * heads, 0, heads, rk[...], qs, lives, peak, weighted, peaks, exps, gprobs, dq)
    drk[...] = grad_k * SCALE
    drv[...] = grad_v
    moves_out = [
        pltpu.make_async_copy(src, dst, local_s.at[6 + i])
        for i, (src, dst) in enumerate((
            (drk, drk_hbm), (drv, drv_hbm), (dq_out, dq_hbm), (dpk, dpk_hbm), (dpv, dpv_hbm)
        ))
    ]
    moves_out[0].start()
    moves_out[1].start()
    to_owner().wait_recv()
    for h in range(heads):
        dq_out[:, h * HD : (h + 1) * HD] = (dq[h] + wide(dq_in[h])).T * SCALE
    moves_out[2].start()
    sums_now = total(0)
    dpk[:, columns(tensor)] = sums_now[0]
    dpv[:, columns(tensor)] = sums_now[1]
    for n in reversed(range(1, ROUNDS)):
        received(to_holder(n))
        cols = columns((tensor + TURN[n]) % 4)
        dpk[:, cols] = wide(z_in[n, 0])
        dpv[:, cols] = wide(z_in[n, 1])
    moves_out[3].start()
    moves_out[4].start()
    sent = to_relay() + [tell(0), tell(1), to_owner()]
    for n in range(ROUNDS):
        sent += [to_half(n, 0), to_half(n, 1), to_ring(n, 0), to_ring(n, 1)]
        if n:
            sent += to_holder(n)
    for copy in sent:
        copy.wait_send()
    for move in moves_out:
        move.wait()


def copy_kernel(*refs):
    sems = refs[-1]
    count = (len(refs) - 1) // 3
    ins, outs, rooms = refs[:count], refs[count : 2 * count], refs[2 * count : 3 * count]
    here = [pltpu.make_async_copy(ins[i], rooms[i], sems.at[0, i]) for i in range(count)]
    away = [pltpu.make_async_copy(rooms[i], outs[i], sems.at[1, i]) for i in range(count)]
    for move in here:
        move.start()
    for i in range(count):
        here[i].wait()
        away[i].start()
    for move in away:
        move.wait()


def local(prompt_k, prompt_v, resp_q, resp_k, resp_v, resp_grad, lengths):
    heads = resp_q.shape[1] // HD
    blocks = (2 * len(SECOND) + 1) * heads
    anywhere = pl.BlockSpec(memory_space=pl.ANY)
    f32, bf16 = jnp.float32, jnp.bfloat16
    stat = pltpu.VMEM((2 * heads, 8, ROWS), f32)
    piece = (2, QUARTER, HD)

    def sems(*shape):
        return [pltpu.SemaphoreType.DMA(shape)] * 2

    outs = tuple(jax.ShapeDtypeStruct(x.shape, f32) for x in (resp_q, resp_k, resp_v, prompt_k, prompt_v))
    flops = 10 * blocks * CHUNK * ROWS * HD
    results = pl.pallas_call(
        kernel,
        out_shape=outs,
        in_specs=[pl.BlockSpec(memory_space=pltpu.SMEM)] + [anywhere] * 6,
        out_specs=[anywhere] * 5,
        scratch_shapes=[
            *(pltpu.VMEM(x.shape, bf16) for x in (resp_q, prompt_k, prompt_v, resp_k, resp_v, resp_grad)),
            *(pltpu.VMEM(x.shape, f32) for x in outs),
            pltpu.VMEM((2 * heads, ROWS, HD), bf16),
            pltpu.VMEM((2 * heads, ROWS, HD), bf16),
            stat,
            stat,
            stat,
            pltpu.VMEM((blocks, 8, ROWS), f32),
            pltpu.VMEM((blocks, CHUNK, ROWS), f32),
            pltpu.VMEM((blocks, CHUNK, ROWS), f32),
            pltpu.VMEM((2 * heads, HD, ROWS), f32),
            pltpu.VMEM((heads, HD, ROWS), bf16),
            pltpu.VMEM((heads, HD, ROWS), bf16),
            pltpu.VMEM((2, 3, 8, ROWS), f32),
            pltpu.VMEM((2, 3, 8, ROWS), f32),
            pltpu.VMEM((ROUNDS,) + piece, bf16),
            pltpu.VMEM(piece, bf16),
            pltpu.VMEM(piece, bf16),
            pltpu.VMEM((2 * ROUNDS, 2) + piece, bf16),
            pltpu.VMEM((2 * ROUNDS, 2) + piece, f32),
            pltpu.VMEM((ROUNDS,) + piece, bf16),
            pltpu.VMEM((ROUNDS,) + piece, bf16),
            pltpu.VMEM((ROUNDS, 2) + piece, bf16),
            pltpu.VMEM((ROUNDS, 2) + piece, bf16),
            pltpu.VMEM((ROUNDS,) + piece, bf16),
            pltpu.VMEM((ROUNDS,) + piece, bf16),
            pltpu.SemaphoreType.DMA((11,)),
            *sems(2),
            *sems(2),
            *sems(1),
            *sems(ROUNDS, 6, 2),
            *sems(ROUNDS, 2),
            *sems(ROUNDS, 2),
            *sems(ROUNDS, 2),
        ],
        compiler_params=pltpu.CompilerParams(
            vmem_limit_bytes=61 * 1024 * 1024, collective_id=0, has_side_effects=True
        ),
        cost_estimate=pl.CostEstimate(flops=flops, bytes_accessed=3 << 20, transcendentals=0),
    )(lengths, resp_q, prompt_k, prompt_v, resp_k, resp_v, resp_grad)
    return pl.pallas_call(
        copy_kernel,
        out_shape=outs,
        in_specs=[anywhere] * 5,
        out_specs=[anywhere] * 5,
        scratch_shapes=[pltpu.VMEM(x.shape, f32) for x in outs] + [pltpu.SemaphoreType.DMA((2, 5))],
        compiler_params=pltpu.CompilerParams(vmem_limit_bytes=61 * 1024 * 1024),
    )(*results)


def solution(mesh):
    rows = P(("dp", "resp", "tensor"), None)
    both = P(("dp", "resp"), "tensor")
    return jax.shard_map(
        local,
        mesh=mesh,
        in_specs=(rows, rows, both, both, both, both, P(("dp", "resp"))),
        out_specs=(both, both, both, rows, rows),
        check_vma=False,
    )
```

```python
import jax
import jax.numpy as jnp
from jax import lax
from jax.experimental import pallas as pl
from jax.experimental.pallas import tpu as pltpu
from jax.sharding import PartitionSpec as P

HD = 128
SCALE = HD**-0.5
LOG2E = 1.4426950408889634
NEG = -1e30
ROWS = 256
CHUNK = 256

CONTRACT_LAST = (((1,), (1,)), ((), ()))
PLAIN = (((1,), (0,)), ((), ()))


def dot(a, b, dims):
    return lax.dot_general(a, b, dims, preferred_element_type=jnp.float32)


MESH = pl.DeviceIdType.MESH
QUARTER = 128
ROUNDS = 4
TURN = (0, 1, 3, 2)
SPREAD, AHEAD, BEHIND, FAR_K, FAR_V, RELAY = range(6)

CHUNKS = ("b0", "b1", "b2", "b3", "e0", "m", "f", "e3")
FIRST = ("b0", "e0", "m", "b1", "b2", "f")
SECOND = ("e3", "f", "b3", "b2", "b1", "m", "e0", "b0")
OWN = (("e0", 0), ("m", 0), ("m", 1), ("e3", 0))
FAR = (("e0", 1), ("f", 0), ("f", 1), ("e3", 1))


def place(where, n):
    return CHUNKS.index(where[n][0]), where[n][1]


def pick(step, values):
    chosen = values[0]
    for at, value in enumerate(values[1:], 1):
        chosen = jnp.where(step == at, value, chosen)
    return chosen


def attend(base, group, count, keys, vals, causal, qs, lives, peak, denom, weighted, peaks, exps, gprobs):
    for h in range(count):
        at, g = base + h, group + h
        scores = dot(keys, qs[g], CONTRACT_LAST) * (SCALE * LOG2E)
        if causal is not None:
            scores = jnp.where(causal, scores, NEG)
        gprob = dot(vals, lives[g], CONTRACT_LAST)
        scores = scores.reshape(CHUNK // 8, 8, ROWS)
        old = peak[g]
        new = jnp.maximum(old, jnp.max(scores, axis=0))
        raw = jnp.exp2(scores - new[None])
        shrink = jnp.exp2(old - new)
        peak[g] = new
        denom[g] = denom[g] * shrink + jnp.sum(raw, axis=0)
        weighted[g] = weighted[g] * shrink + jnp.sum(raw * gprob.reshape(raw.shape), axis=0)
        peaks[at] = new
        exps[at] = raw.reshape(CHUNK, ROWS)
        gprobs[at] = gprob


def join_sums(group, count, peak, denom, weighted, out):
    for h in range(count):
        top = jnp.max(peak[group + h], axis=0, keepdims=True)
        share = jnp.exp2(peak[group + h] - top)
        out[0, h : h + 1] = top
        out[1, h : h + 1] = jnp.sum(denom[group + h] * share, axis=0, keepdims=True)
        out[2, h : h + 1] = jnp.sum(weighted[group + h] * share, axis=0, keepdims=True)


def finish_stats(group, count, one, two, peak, weighted):
    for h in range(count):
        row = slice(h, h + 1)
        top = jnp.maximum(one[0, row], two[0, row])
        share_one, share_two = jnp.exp2(one[0, row] - top), jnp.exp2(two[0, row] - top)
        total = one[1, row] * share_one + two[1, row] * share_two
        mean = (one[2, row] * share_one + two[2, row] * share_two) / total
        peak[group + h] = jnp.broadcast_to(top + jnp.log2(total), (8, ROWS))
        weighted[group + h] = jnp.broadcast_to(mean, (8, ROWS))


def grads(base, group, count, keys, qs, lives, peak, weighted, peaks, exps, gprobs, dq):
    keys_t = keys.T
    probs, dscores = [], []
    for h in range(count):
        at, g = base + h, group + h
        factor = jnp.exp2(peaks[at] - peak[g])
        prob = exps[at].reshape(CHUNK // 8, 8, ROWS) * factor[None]
        dscore = prob * (gprobs[at].reshape(CHUNK // 8, 8, ROWS) - weighted[g][None])
        probs.append(prob.reshape(CHUNK, ROWS).astype(jnp.bfloat16))
        dscore = dscore.reshape(CHUNK, ROWS).astype(jnp.bfloat16)
        dscores.append(dscore)
        dq[g] += dot(keys_t, dscore, PLAIN)
    rows = pl.ds(group, count)
    grad_v = dot(jnp.concatenate(probs, axis=1), lives[rows].reshape(count * ROWS, HD), PLAIN)
    grad_k = dot(jnp.concatenate(dscores, axis=1), qs[rows].reshape(count * ROWS, HD), PLAIN)
    return grad_k, grad_v


def kernel(lengths, q_hbm, pk_hbm, pv_hbm, rk_hbm, rv_hbm, g_hbm, dq_hbm, drk_hbm, drv_hbm, dpk_hbm, dpv_hbm,
           q, pk, pv, rk, rv, g, dq_out, drk, drv, dpk, dpv,
           qs, lives, peak, denom, weighted, peaks, exps, gprobs, dq, dq_send, dq_in,
           stat_out, stat_in, packed, passing, returning, kv, own, half_out, half_in, ring_out, ring_in, z_out, z_in,
           local_s, swap_s, swap_r, stat_s, stat_r, dq_s, dq_r, get_s, get_r, half_s, half_r, ring_s, ring_r, z_s, z_r):
    heads = q.shape[1] // HD
    resp, tensor = lax.axis_index("resp"), lax.axis_index("tensor")
    chip, core = resp // 2, resp % 2
    up = {"resp": (chip + 1) % 4 * 2 + core}
    down = {"resp": (chip + 3) % 4 * 2 + core}
    twin = {"resp": chip * 2 + 1 - core}

    def along(turn):
        return {"tensor": (tensor + turn) % 4}

    def columns(index):
        return pl.ds(pl.multiple_of(index * HD, HD), HD)

    barrier = pltpu.get_barrier_semaphore()
    for other in (up, down, twin, along(1), along(3)):
        pl.semaphore_signal(barrier, inc=1, device_id=other, device_id_type=MESH)
    moves_in = [
        pltpu.make_async_copy(src, dst, local_s.at[i])
        for i, (src, dst) in enumerate(
            ((pk_hbm, pk), (pv_hbm, pv), (q_hbm, q), (g_hbm, g), (rk_hbm, rk), (rv_hbm, rv))
        )
    ]
    for move in moves_in:
        move.start()

    def send(src, dst, sems, at, to):
        return pltpu.make_async_remote_copy(
            src_ref=src, dst_ref=dst, send_sem=sems[0].at[at], recv_sem=sems[1].at[at],
            device_id=to, device_id_type=MESH,
        )

    def get(n, kind):
        mine, far = kv.at[*place(OWN, n)], kv.at[*place(FAR, n)]
        if kind == RELAY:
            ends = [(packed.at[n, part], passing.at[part], along((1, 3)[part])) for part in range(2)]
        elif kind == SPREAD and n == 3:
            ends = [(passing.at[part], mine.at[part], along((1, 3)[part])) for part in range(2)]
        elif kind == SPREAD:
            ends = [(packed.at[n], mine, along(TURN[n]))]
        elif kind == AHEAD:
            ends = [(mine, kv.at[n, 0], up)]
        elif kind == BEHIND:
            ends = [(mine, kv.at[n, 1], down)]
        elif kind == FAR_K:
            ends = [(kv.at[n, 0, 0], far.at[0], up)]
        else:
            ends = [(kv.at[n, 1, 1], far.at[1], down)]
        return [send(src, dst, (get_s, get_r), (n, kind, i), to) for i, (src, dst, to) in enumerate(ends)]

    def start(copies):
        for copy in copies:
            copy.start()

    def received(copies):
        for copy in copies:
            copy.wait_recv()

    def begin(n):
        if n:
            received(get(n, SPREAD))
        start(get(n, AHEAD))
        start(get(n, BEHIND))

    def forward(n):
        received(get(n, AHEAD))
        start(get(n, FAR_K))
        received(get(n, BEHIND))
        start(get(n, FAR_V))

    def relay_out():
        for first_hop, second_hop in zip(get(3, RELAY), get(3, SPREAD)):
            first_hop.wait_recv()
            second_hop.start()

    def swap():
        here, there = pl.ds(0, heads), pl.ds(heads, heads)
        return [send(ref.at[here], ref.at[there], (swap_s, swap_r), i, twin) for i, ref in enumerate((qs, lives))]

    positions = lax.broadcasted_iota(jnp.int32, (ROWS, HD), 0)
    alive = positions < lengths[0]
    moves_in[0].wait()
    moves_in[1].wait()
    kv[4, 0, 0] = pk[:, columns(tensor)]
    kv[4, 0, 1] = pv[:, columns(tensor)]
    for n in range(1, ROUNDS):
        cols = columns((tensor + TURN[n]) % 4)
        packed[n, 0] = pk[:, cols]
        packed[n, 1] = pv[:, cols]
    pl.semaphore_wait(barrier, 5)
    begin(0)
    start(get(1, SPREAD))
    start(get(2, SPREAD))
    start(get(3, RELAY))
    moves_in[2].wait()
    moves_in[3].wait()
    for h in range(heads):
        cols = slice(h * HD, (h + 1) * HD)
        qs[h] = q[:, cols]
        lives[h] = jnp.where(alive, g[:, cols], jnp.zeros((), jnp.bfloat16))
    start(swap())
    moves_in[4].wait()
    moves_in[5].wait()
    peak[...] = jnp.full(peak.shape, NEG, jnp.float32)
    denom[...] = jnp.zeros(denom.shape, jnp.float32)
    weighted[...] = jnp.zeros(weighted.shape, jnp.float32)
    dq[...] = jnp.zeros(dq.shape, jnp.float32)
    causal = lax.broadcasted_iota(jnp.int32, (CHUNK, ROWS), 0) <= lax.broadcasted_iota(jnp.int32, (CHUNK, ROWS), 1)
    sums = (qs, lives, peak, denom, weighted, peaks, exps, gprobs)
    steps = len(SECOND)
    attend(2 * steps * heads, 0, heads, rk[...], rv[...], causal, *sums)

    def far_received(*rounds):
        for n in rounds:
            received(get(n, FAR_K) + get(n, FAR_V))

    before = {
        "b0": (lambda: forward(0), lambda: received(swap())),
        "e0": (lambda: far_received(0),),
        "m": (relay_out, lambda: begin(1), lambda: begin(2)),
        "b1": (lambda: forward(1), lambda: forward(2)),
        "b2": (lambda: begin(3),),
        "f": (lambda: far_received(1, 2),),
    }

    def serve(step, order, table):
        for name, jobs in table.items():
            @pl.when(step == order.index(name))
            def _():
                for job in jobs:
                    job()

    def tell(half):
        return send(stat_out.at[half], stat_in.at[1 - half], (stat_s, stat_r), 1 - half, twin)

    def take(chunk, half):
        keys = kv[chunk, :, 0].reshape(CHUNK, HD)
        vals = kv[chunk, :, 1].reshape(CHUNK, HD)
        attend((chunk * 2 + half) * heads, half * heads, heads, keys, vals, None, *sums)

    def first(step, carry):
        chunk = pick(step, [CHUNKS.index(name) for name in FIRST])
        serve(step, FIRST, before)
        take(chunk, 0)
        take(chunk, 1)
        return carry

    lax.fori_loop(0, len(FIRST), first, 0)
    forward(3)
    take(CHUNKS.index("b3"), 1)
    take(CHUNKS.index("b3"), 0)
    far_received(3)
    take(CHUNKS.index("e3"), 1)
    join_sums(heads, heads, peak, denom, weighted, stat_out.at[1])
    tell(1).start()
    take(CHUNKS.index("e3"), 0)
    join_sums(0, heads, peak, denom, weighted, stat_out.at[0])
    tell(0).start()
    for n in range(ROUNDS):
        for kind in range(SPREAD if n else AHEAD, FAR_V + 1):
            for copy in get(n, kind):
                copy.wait_send()
    for copy in get(3, RELAY) + swap():
        copy.wait_send()
    tell(1).wait_recv()
    finish_stats(0, heads, stat_out.at[0], stat_in.at[0], peak, weighted)
    tell(0).wait_recv()
    finish_stats(heads, heads, stat_out.at[1], stat_in.at[1], peak, weighted)

    def to_half(n, part):
        return send(half_out.at[n, part], half_in.at[n, part], (half_s, half_r), (n, part), (up, down)[part])

    def to_ring(n, way):
        return send(ring_out.at[n, way], ring_in.at[n, way], (ring_s, ring_r), (n, way), (up, down)[way])

    def to_holder(n):
        if n == 3:
            ends = [(returning.at[part], along((1, 3)[part])) for part in range(2)]
        else:
            return [send(z_out.at[n], z_in.at[n], (z_s, z_r), (n, 0), along(4 - TURN[n]))]
        return [send(src, z_in.at[n, part], (z_s, z_r), (n, part), to) for part, (src, to) in enumerate(ends)]

    def to_relay():
        return [
            send(z_out.at[3, part], returning.at[part], (z_s, z_r), (0, part), along((1, 3)[part])) for part in range(2)
        ]

    def relay_back():
        for first_hop, second_hop in zip(to_relay(), to_holder(3)):
            first_hop.wait_recv()
            second_hop.start()

    def to_owner():
        return send(dq_send, dq_in, (dq_s, dq_r), 0, twin)

    def wide(ref):
        return ref.astype(jnp.float32)

    def halves(n):
        half_out[n] = own[place(FAR, n)].astype(jnp.bfloat16)
        to_half(n, 0).start()
        to_half(n, 1).start()

    def relay(n):
        for way in range(2):
            to_half(n, way).wait_recv()
            part = own[n, 1 - way]
            ring_out[n, way, way] = (part[way] + wide(half_in[n, way])).astype(jnp.bfloat16)
            ring_out[n, way, 1 - way] = part[1 - way].astype(jnp.bfloat16)
            to_ring(n, way).start()

    def total(n):
        received([to_ring(n, 0), to_ring(n, 1)])
        return own[place(OWN, n)] + wide(ring_in[n, 0]) + wide(ring_in[n, 1])

    def hand_over(n):
        z_out[n] = total(n).astype(jnp.bfloat16)
        start(to_relay() if n == 3 else to_holder(n))

    def return_queries():
        for h in range(heads):
            dq_send[h] = dq[heads + h].astype(jnp.bfloat16)
        to_owner().start()

    services = {
        "e3": (lambda: halves(3),),
        "f": (lambda: halves(2), lambda: halves(1)),
        "b3": (lambda: relay(3),),
        "b2": (lambda: relay(2),),
        "b1": (lambda: relay(1), lambda: hand_over(3)),
        "m": (lambda: hand_over(2),),
        "e0": (lambda: halves(0), lambda: hand_over(1)),
        "b0": (return_queries, relay_back),
    }

    def second(step, carry):
        chunk = pick(step, [CHUNKS.index(name) for name in SECOND])
        keys = kv[chunk, :, 0].reshape(CHUNK, HD)
        grad_k, grad_v = grads(
            chunk * 2 * heads, 0, 2 * heads, keys, qs, lives, peak, weighted, peaks, exps, gprobs, dq
        )
        own[chunk, :, 0] = (grad_k * SCALE).reshape(2, QUARTER, HD)
        own[chunk, :, 1] = grad_v.reshape(2, QUARTER, HD)
        serve(step, SECOND, services)
        return carry

    lax.fori_loop(0, steps, second, 0)
    grad_k, grad_v = grads(2 * steps * heads, 0, heads, rk[...], qs, lives, peak, weighted, peaks, exps, gprobs, dq)
    drk[...] = grad_k * SCALE
    drv[...] = grad_v
    relay(0)
    moves_out = [
        pltpu.make_async_copy(src, dst, local_s.at[6 + i])
        for i, (src, dst) in enumerate((
            (drk, drk_hbm), (drv, drv_hbm), (dq_out, dq_hbm), (dpk, dpk_hbm), (dpv, dpv_hbm)
        ))
    ]
    moves_out[0].start()
    moves_out[1].start()
    to_owner().wait_recv()
    for h in range(heads):
        dq_out[:, h * HD : (h + 1) * HD] = (dq[h] + wide(dq_in[h])).T * SCALE
    moves_out[2].start()
    sums_now = total(0)
    dpk[:, columns(tensor)] = sums_now[0]
    dpv[:, columns(tensor)] = sums_now[1]
    for n in reversed(range(1, ROUNDS)):
        received(to_holder(n))
        cols = columns((tensor + TURN[n]) % 4)
        dpk[:, cols] = wide(z_in[n, 0])
        dpv[:, cols] = wide(z_in[n, 1])
    moves_out[3].start()
    moves_out[4].start()
    sent = to_relay() + [tell(0), tell(1), to_owner()]
    for n in range(ROUNDS):
        sent += [to_half(n, 0), to_half(n, 1), to_ring(n, 0), to_ring(n, 1)]
        if n:
            sent += to_holder(n)
    for copy in sent:
        copy.wait_send()
    for move in moves_out:
        move.wait()


def copy_kernel(*refs):
    sems = refs[-1]
    count = (len(refs) - 1) // 3
    ins, outs, rooms = refs[:count], refs[count : 2 * count], refs[2 * count : 3 * count]
    here = [pltpu.make_async_copy(ins[i], rooms[i], sems.at[0, i]) for i in range(count)]
    away = [pltpu.make_async_copy(rooms[i], outs[i], sems.at[1, i]) for i in range(count)]
    for move in here:
        move.start()
    for i in range(count):
        here[i].wait()
        away[i].start()
    for move in away:
        move.wait()


def local(prompt_k, prompt_v, resp_q, resp_k, resp_v, resp_grad, lengths):
    heads = resp_q.shape[1] // HD
    blocks = (2 * len(SECOND) + 1) * heads
    anywhere = pl.BlockSpec(memory_space=pl.ANY)
    f32, bf16 = jnp.float32, jnp.bfloat16
    stat = pltpu.VMEM((2 * heads, 8, ROWS), f32)
    piece = (2, QUARTER, HD)

    def sems(*shape):
        return [pltpu.SemaphoreType.DMA(shape)] * 2

    outs = tuple(jax.ShapeDtypeStruct(x.shape, f32) for x in (resp_q, resp_k, resp_v, prompt_k, prompt_v))
    flops = 10 * blocks * CHUNK * ROWS * HD
    results = pl.pallas_call(
        kernel,
        out_shape=outs,
        in_specs=[pl.BlockSpec(memory_space=pltpu.SMEM)] + [anywhere] * 6,
        out_specs=[anywhere] * 5,
        scratch_shapes=[
            *(pltpu.VMEM(x.shape, bf16) for x in (resp_q, prompt_k, prompt_v, resp_k, resp_v, resp_grad)),
            *(pltpu.VMEM(x.shape, f32) for x in outs),
            pltpu.VMEM((2 * heads, ROWS, HD), bf16),
            pltpu.VMEM((2 * heads, ROWS, HD), bf16),
            stat,
            stat,
            stat,
            pltpu.VMEM((blocks, 8, ROWS), f32),
            pltpu.VMEM((blocks, CHUNK, ROWS), f32),
            pltpu.VMEM((blocks, CHUNK, ROWS), f32),
            pltpu.VMEM((2 * heads, HD, ROWS), f32),
            pltpu.VMEM((heads, HD, ROWS), bf16),
            pltpu.VMEM((heads, HD, ROWS), bf16),
            pltpu.VMEM((2, 3, 8, ROWS), f32),
            pltpu.VMEM((2, 3, 8, ROWS), f32),
            pltpu.VMEM((ROUNDS,) + piece, bf16),
            pltpu.VMEM(piece, bf16),
            pltpu.VMEM(piece, bf16),
            pltpu.VMEM((2 * ROUNDS, 2) + piece, bf16),
            pltpu.VMEM((2 * ROUNDS, 2) + piece, f32),
            pltpu.VMEM((ROUNDS,) + piece, bf16),
            pltpu.VMEM((ROUNDS,) + piece, bf16),
            pltpu.VMEM((ROUNDS, 2) + piece, bf16),
            pltpu.VMEM((ROUNDS, 2) + piece, bf16),
            pltpu.VMEM((ROUNDS,) + piece, bf16),
            pltpu.VMEM((ROUNDS,) + piece, bf16),
            pltpu.SemaphoreType.DMA((11,)),
            *sems(2),
            *sems(2),
            *sems(1),
            *sems(ROUNDS, 6, 2),
            *sems(ROUNDS, 2),
            *sems(ROUNDS, 2),
            *sems(ROUNDS, 2),
        ],
        compiler_params=pltpu.CompilerParams(
            vmem_limit_bytes=61 * 1024 * 1024, collective_id=0, has_side_effects=True
        ),
        cost_estimate=pl.CostEstimate(flops=flops, bytes_accessed=3 << 20, transcendentals=0),
    )(lengths, resp_q, prompt_k, prompt_v, resp_k, resp_v, resp_grad)
    return pl.pallas_call(
        copy_kernel,
        out_shape=outs,
        in_specs=[anywhere] * 5,
        out_specs=[anywhere] * 5,
        scratch_shapes=[pltpu.VMEM(x.shape, f32) for x in outs] + [pltpu.SemaphoreType.DMA((2, 5))],
        compiler_params=pltpu.CompilerParams(vmem_limit_bytes=61 * 1024 * 1024),
    )(*results)


def solution(mesh):
    rows = P(("dp", "resp", "tensor"), None)
    both = P(("dp", "resp"), "tensor")
    return jax.shard_map(
        local,
        mesh=mesh,
        in_specs=(rows, rows, both, both, both, both, P(("dp", "resp"))),
        out_specs=(both, both, both, rows, rows),
        check_vma=False,
    )
```

```python
import jax
import jax.numpy as jnp
from jax import lax
from jax.experimental import pallas as pl
from jax.experimental.pallas import tpu as pltpu
from jax.sharding import PartitionSpec as P

HD = 128
SCALE = HD**-0.5
LOG2E = 1.4426950408889634
NEG = -1e30
ROWS = 256
CHUNK = 256

CONTRACT_LAST = (((1,), (1,)), ((), ()))
PLAIN = (((1,), (0,)), ((), ()))


def dot(a, b, dims):
    return lax.dot_general(a, b, dims, preferred_element_type=jnp.float32)


MESH = pl.DeviceIdType.MESH
QUARTER = 128
ROUNDS = 4
TURN = (0, 1, 3, 2)
SPREAD, AHEAD, BEHIND, FAR_K, FAR_V, RELAY = range(6)

CHUNKS = ("b0", "b1", "b2", "b3", "e0", "m", "f", "e3")
FIRST = ("b0", "e0", "m", "b1", "b2", "f")
SECOND = ("e3", "f", "b3", "b2", "b1", "m", "e0", "b0")
OWN = (("e0", 0), ("m", 0), ("m", 1), ("e3", 0))
FAR = (("e0", 1), ("f", 0), ("f", 1), ("e3", 1))


def place(where, n):
    return CHUNKS.index(where[n][0]), where[n][1]


def pick(step, values):
    chosen = values[0]
    for at, value in enumerate(values[1:], 1):
        chosen = jnp.where(step == at, value, chosen)
    return chosen


def attend(base, group, count, keys, vals, causal, qs, lives, peak, denom, weighted, peaks, exps, gprobs):
    for h in range(count):
        at, g = base + h, group + h
        scores = dot(keys, qs[g], CONTRACT_LAST) * (SCALE * LOG2E)
        if causal is not None:
            scores = jnp.where(causal, scores, NEG)
        gprob = dot(vals, lives[g], CONTRACT_LAST)
        scores = scores.reshape(CHUNK // 8, 8, ROWS)
        old = peak[g]
        new = jnp.maximum(old, jnp.max(scores, axis=0))
        raw = jnp.exp2(scores - new[None])
        shrink = jnp.exp2(old - new)
        peak[g] = new
        denom[g] = denom[g] * shrink + jnp.sum(raw, axis=0)
        weighted[g] = weighted[g] * shrink + jnp.sum(raw * gprob.reshape(raw.shape), axis=0)
        peaks[at] = new
        exps[at] = raw.reshape(CHUNK, ROWS)
        gprobs[at] = gprob


def join_sums(group, count, peak, denom, weighted, out):
    for h in range(count):
        top = jnp.max(peak[group + h], axis=0, keepdims=True)
        share = jnp.exp2(peak[group + h] - top)
        out[0, h : h + 1] = top
        out[1, h : h + 1] = jnp.sum(denom[group + h] * share, axis=0, keepdims=True)
        out[2, h : h + 1] = jnp.sum(weighted[group + h] * share, axis=0, keepdims=True)


def finish_stats(group, count, one, two, peak, weighted):
    for h in range(count):
        row = slice(h, h + 1)
        top = jnp.maximum(one[0, row], two[0, row])
        share_one, share_two = jnp.exp2(one[0, row] - top), jnp.exp2(two[0, row] - top)
        total = one[1, row] * share_one + two[1, row] * share_two
        mean = (one[2, row] * share_one + two[2, row] * share_two) / total
        peak[group + h] = jnp.broadcast_to(top + jnp.log2(total), (8, ROWS))
        weighted[group + h] = jnp.broadcast_to(mean, (8, ROWS))


def grads(base, group, count, keys, qs, lives, peak, weighted, peaks, exps, gprobs, dq):
    keys_t = keys.T
    probs, dscores = [], []
    for h in range(count):
        at, g = base + h, group + h
        factor = jnp.exp2(peaks[at] - peak[g])
        prob = exps[at].reshape(CHUNK // 8, 8, ROWS) * factor[None]
        dscore = prob * (gprobs[at].reshape(CHUNK // 8, 8, ROWS) - weighted[g][None])
        probs.append(prob.reshape(CHUNK, ROWS).astype(jnp.bfloat16))
        dscore = dscore.reshape(CHUNK, ROWS).astype(jnp.bfloat16)
        dscores.append(dscore)
        dq[g] += dot(keys_t, dscore, PLAIN)
    rows = pl.ds(group, count)
    grad_v = dot(jnp.concatenate(probs, axis=1), lives[rows].reshape(count * ROWS, HD), PLAIN)
    grad_k = dot(jnp.concatenate(dscores, axis=1), qs[rows].reshape(count * ROWS, HD), PLAIN)
    return grad_k, grad_v


def kernel(lengths, q_hbm, pk_hbm, pv_hbm, rk_hbm, rv_hbm, g_hbm, dq_hbm, drk_hbm, drv_hbm, dpk_hbm, dpv_hbm,
           q, pk, pv, rk, rv, g, dq_out, drk, drv, dpk, dpv,
           qs, lives, peak, denom, weighted, peaks, exps, gprobs, dq, dq_send, dq_in,
           stat_out, stat_in, packed, passing, returning, kv, own, half_out, half_in, ring_out, ring_in, z_out, z_in,
           local_s, swap_s, swap_r, stat_s, stat_r, dq_s, dq_r, get_s, get_r, half_s, half_r, ring_s, ring_r, z_s, z_r):
    heads = q.shape[1] // HD
    resp, tensor = lax.axis_index("resp"), lax.axis_index("tensor")
    chip, core = resp // 2, resp % 2
    up = {"resp": (chip + 1) % 4 * 2 + core}
    down = {"resp": (chip + 3) % 4 * 2 + core}
    twin = {"resp": chip * 2 + 1 - core}

    def along(turn):
        return {"tensor": (tensor + turn) % 4}

    def columns(index):
        return pl.ds(pl.multiple_of(index * HD, HD), HD)

    barrier = pltpu.get_barrier_semaphore()
    for other in (up, down, twin, along(1), along(3)):
        pl.semaphore_signal(barrier, inc=1, device_id=other, device_id_type=MESH)
    moves_in = [
        pltpu.make_async_copy(src, dst, local_s.at[i])
        for i, (src, dst) in enumerate(
            ((pk_hbm, pk), (pv_hbm, pv), (q_hbm, q), (g_hbm, g), (rk_hbm, rk), (rv_hbm, rv))
        )
    ]
    for move in moves_in:
        move.start()

    def send(src, dst, sems, at, to):
        return pltpu.make_async_remote_copy(
            src_ref=src, dst_ref=dst, send_sem=sems[0].at[at], recv_sem=sems[1].at[at],
            device_id=to, device_id_type=MESH,
        )

    def get(n, kind):
        mine, far = kv.at[*place(OWN, n)], kv.at[*place(FAR, n)]
        if kind == RELAY:
            ends = [(packed.at[n, part], passing.at[part], along((1, 3)[part])) for part in range(2)]
        elif kind == SPREAD and n == 3:
            ends = [(passing.at[part], mine.at[part], along((1, 3)[part])) for part in range(2)]
        elif kind == SPREAD:
            ends = [(packed.at[n, part], mine.at[part], along(TURN[n])) for part in range(2)]
        elif kind == AHEAD:
            ends = [(mine.at[part], kv.at[n, 0, part], up) for part in range(2)]
        elif kind == BEHIND:
            ends = [(mine.at[part], kv.at[n, 1, part], down) for part in range(2)]
        elif kind == FAR_K:
            ends = [(kv.at[n, 0, 0], far.at[0], up)]
        else:
            ends = [(kv.at[n, 1, 1], far.at[1], down)]
        return [send(src, dst, (get_s, get_r), (n, kind, i), to) for i, (src, dst, to) in enumerate(ends)]

    def start(copies):
        for copy in copies:
            copy.start()

    def received(copies):
        for copy in copies:
            copy.wait_recv()

    def begin(n, part):
        if n:
            get(n, SPREAD)[part].wait_recv()
        get(n, AHEAD)[part].start()
        get(n, BEHIND)[part].start()

    def forward(n, part):
        get(n, (AHEAD, BEHIND)[part])[part].wait_recv()
        start(get(n, (FAR_K, FAR_V)[part]))

    def near_received(n):
        get(n, AHEAD)[1].wait_recv()
        get(n, BEHIND)[0].wait_recv()

    def relay_out():
        for first_hop, second_hop in zip(get(3, RELAY), get(3, SPREAD)):
            first_hop.wait_recv()
            second_hop.start()

    def swap():
        here, there = pl.ds(0, heads), pl.ds(heads, heads)
        return [send(ref.at[here], ref.at[there], (swap_s, swap_r), i, twin) for i, ref in enumerate((qs, lives))]

    positions = lax.broadcasted_iota(jnp.int32, (ROWS, HD), 0)
    alive = positions < lengths[0]
    moves_in[0].wait()
    moves_in[1].wait()
    kv[4, 0, 0] = pk[:, columns(tensor)]
    kv[4, 0, 1] = pv[:, columns(tensor)]
    for n in range(1, ROUNDS):
        cols = columns((tensor + TURN[n]) % 4)
        packed[n, 0] = pk[:, cols]
        packed[n, 1] = pv[:, cols]
    pl.semaphore_wait(barrier, 5)
    for part in range(2):
        get(1, SPREAD)[part].start()
        get(2, SPREAD)[part].start()
        begin(0, part)
    start(get(3, RELAY))
    moves_in[2].wait()
    moves_in[3].wait()
    for h in range(heads):
        cols = slice(h * HD, (h + 1) * HD)
        qs[h] = q[:, cols]
        lives[h] = jnp.where(alive, g[:, cols], jnp.zeros((), jnp.bfloat16))
    start(swap())
    moves_in[4].wait()
    moves_in[5].wait()
    peak[...] = jnp.full(peak.shape, NEG, jnp.float32)
    denom[...] = jnp.zeros(denom.shape, jnp.float32)
    weighted[...] = jnp.zeros(weighted.shape, jnp.float32)
    dq[...] = jnp.zeros(dq.shape, jnp.float32)
    causal = lax.broadcasted_iota(jnp.int32, (CHUNK, ROWS), 0) <= lax.broadcasted_iota(jnp.int32, (CHUNK, ROWS), 1)
    sums = (qs, lives, peak, denom, weighted, peaks, exps, gprobs)
    steps = len(SECOND)
    attend(2 * steps * heads, 0, heads, rk[...], rv[...], causal, *sums)

    def far_received(*rounds):
        for n in rounds:
            received(get(n, FAR_K) + get(n, FAR_V))

    before = {
        "b0": (lambda: forward(0, 0), lambda: forward(0, 1), lambda: near_received(0), lambda: received(swap())),
        "e0": (lambda: begin(1, 0), lambda: begin(2, 0), lambda: far_received(0)),
        "m": (lambda: begin(1, 1), lambda: begin(2, 1), relay_out),
        "b1": (
            lambda: forward(1, 0), lambda: forward(2, 0), lambda: forward(1, 1), lambda: forward(2, 1),
            lambda: near_received(1),
        ),
        "b2": (lambda: near_received(2),),
        "f": (lambda: begin(3, 0), lambda: begin(3, 1), lambda: far_received(1, 2)),
    }

    def serve(step, order, table):
        for name, jobs in table.items():
            @pl.when(step == order.index(name))
            def _():
                for job in jobs:
                    job()

    def tell(half):
        return send(stat_out.at[half], stat_in.at[1 - half], (stat_s, stat_r), 1 - half, twin)

    def take(chunk, half):
        keys = kv[chunk, :, 0].reshape(CHUNK, HD)
        vals = kv[chunk, :, 1].reshape(CHUNK, HD)
        attend((chunk * 2 + half) * heads, half * heads, heads, keys, vals, None, *sums)

    def first(step, carry):
        chunk = pick(step, [CHUNKS.index(name) for name in FIRST])
        serve(step, FIRST, before)
        take(chunk, 0)
        take(chunk, 1)
        return carry

    lax.fori_loop(0, len(FIRST), first, 0)
    forward(3, 0)
    forward(3, 1)
    near_received(3)
    take(CHUNKS.index("b3"), 1)
    take(CHUNKS.index("b3"), 0)
    far_received(3)
    take(CHUNKS.index("e3"), 1)
    join_sums(heads, heads, peak, denom, weighted, stat_out.at[1])
    tell(1).start()
    take(CHUNKS.index("e3"), 0)
    join_sums(0, heads, peak, denom, weighted, stat_out.at[0])
    tell(0).start()
    for n in range(ROUNDS):
        for kind in range(SPREAD if n else AHEAD, FAR_V + 1):
            for copy in get(n, kind):
                copy.wait_send()
    for copy in get(3, RELAY) + swap():
        copy.wait_send()
    tell(1).wait_recv()
    finish_stats(0, heads, stat_out.at[0], stat_in.at[0], peak, weighted)
    tell(0).wait_recv()
    finish_stats(heads, heads, stat_out.at[1], stat_in.at[1], peak, weighted)

    def to_half(n, part):
        return send(half_out.at[n, part], half_in.at[n, part], (half_s, half_r), (n, part), (up, down)[part])

    def to_ring(n, way):
        return send(ring_out.at[n, way], ring_in.at[n, way], (ring_s, ring_r), (n, way), (up, down)[way])

    def to_holder(n):
        if n == 3:
            ends = [(returning.at[part], along((1, 3)[part])) for part in range(2)]
        else:
            return [send(z_out.at[n], z_in.at[n], (z_s, z_r), (n, 0), along(4 - TURN[n]))]
        return [send(src, z_in.at[n, part], (z_s, z_r), (n, part), to) for part, (src, to) in enumerate(ends)]

    def to_relay():
        return [
            send(z_out.at[3, part], returning.at[part], (z_s, z_r), (0, part), along((1, 3)[part])) for part in range(2)
        ]

    def relay_back():
        for first_hop, second_hop in zip(to_relay(), to_holder(3)):
            first_hop.wait_recv()
            second_hop.start()

    def to_owner():
        return send(dq_send, dq_in, (dq_s, dq_r), 0, twin)

    def wide(ref):
        return ref.astype(jnp.float32)

    def halves(n):
        half_out[n] = own[place(FAR, n)].astype(jnp.bfloat16)
        to_half(n, 0).start()
        to_half(n, 1).start()

    def relay(n):
        for way in range(2):
            to_half(n, way).wait_recv()
            part = own[n, 1 - way]
            ring_out[n, way, way] = (part[way] + wide(half_in[n, way])).astype(jnp.bfloat16)
            ring_out[n, way, 1 - way] = part[1 - way].astype(jnp.bfloat16)
            to_ring(n, way).start()

    def total(n):
        received([to_ring(n, 0), to_ring(n, 1)])
        return own[place(OWN, n)] + wide(ring_in[n, 0]) + wide(ring_in[n, 1])

    def hand_over(n):
        z_out[n] = total(n).astype(jnp.bfloat16)
        start(to_relay() if n == 3 else to_holder(n))

    def return_queries():
        for h in range(heads):
            dq_send[h] = dq[heads + h].astype(jnp.bfloat16)
        to_owner().start()

    services = {
        "e3": (lambda: halves(3),),
        "f": (lambda: halves(2), lambda: halves(1)),
        "b3": (lambda: relay(3),),
        "b2": (lambda: relay(2),),
        "b1": (lambda: relay(1),),
        "e0": (lambda: halves(0), lambda: hand_over(3)),
        "b0": (return_queries,),
    }

    def second(step, carry):
        chunk = pick(step, [CHUNKS.index(name) for name in SECOND])
        keys = kv[chunk, :, 0].reshape(CHUNK, HD)
        grad_k, grad_v = grads(
            chunk * 2 * heads, 0, 2 * heads, keys, qs, lives, peak, weighted, peaks, exps, gprobs, dq
        )
        own[chunk, :, 0] = (grad_k * SCALE).reshape(2, QUARTER, HD)
        own[chunk, :, 1] = grad_v.reshape(2, QUARTER, HD)
        serve(step, SECOND, services)
        return carry

    lax.fori_loop(0, steps, second, 0)
    grad_k, grad_v = grads(2 * steps * heads, 0, heads, rk[...], qs, lives, peak, weighted, peaks, exps, gprobs, dq)
    drk[...] = grad_k * SCALE
    drv[...] = grad_v
    hand_over(2)
    moves_out = [
        pltpu.make_async_copy(src, dst, local_s.at[6 + i])
        for i, (src, dst) in enumerate((
            (drk, drk_hbm), (drv, drv_hbm), (dq_out, dq_hbm), (dpk, dpk_hbm), (dpv, dpv_hbm)
        ))
    ]
    moves_out[0].start()
    moves_out[1].start()
    to_owner().wait_recv()
    for h in range(heads):
        dq_out[:, h * HD : (h + 1) * HD] = (dq[h] + wide(dq_in[h])).T * SCALE
    moves_out[2].start()
    hand_over(1)
    relay_back()
    relay(0)
    sums_now = total(0)
    dpk[:, columns(tensor)] = sums_now[0]
    dpv[:, columns(tensor)] = sums_now[1]
    for n in reversed(range(1, ROUNDS)):
        received(to_holder(n))
        cols = columns((tensor + TURN[n]) % 4)
        dpk[:, cols] = wide(z_in[n, 0])
        dpv[:, cols] = wide(z_in[n, 1])
    moves_out[3].start()
    moves_out[4].start()
    sent = to_relay() + [tell(0), tell(1), to_owner()]
    for n in range(ROUNDS):
        sent += [to_half(n, 0), to_half(n, 1), to_ring(n, 0), to_ring(n, 1)]
        if n:
            sent += to_holder(n)
    for copy in sent:
        copy.wait_send()
    for move in moves_out:
        move.wait()


def copy_kernel(*refs):
    sems = refs[-1]
    count = (len(refs) - 1) // 3
    ins, outs, rooms = refs[:count], refs[count : 2 * count], refs[2 * count : 3 * count]
    here = [pltpu.make_async_copy(ins[i], rooms[i], sems.at[0, i]) for i in range(count)]
    away = [pltpu.make_async_copy(rooms[i], outs[i], sems.at[1, i]) for i in range(count)]
    for move in here:
        move.start()
    for i in range(count):
        here[i].wait()
        away[i].start()
    for move in away:
        move.wait()


def local(prompt_k, prompt_v, resp_q, resp_k, resp_v, resp_grad, lengths):
    heads = resp_q.shape[1] // HD
    blocks = (2 * len(SECOND) + 1) * heads
    anywhere = pl.BlockSpec(memory_space=pl.ANY)
    f32, bf16 = jnp.float32, jnp.bfloat16
    stat = pltpu.VMEM((2 * heads, 8, ROWS), f32)
    piece = (2, QUARTER, HD)

    def sems(*shape):
        return [pltpu.SemaphoreType.DMA(shape)] * 2

    outs = tuple(jax.ShapeDtypeStruct(x.shape, f32) for x in (resp_q, resp_k, resp_v, prompt_k, prompt_v))
    flops = 10 * blocks * CHUNK * ROWS * HD
    results = pl.pallas_call(
        kernel,
        out_shape=outs,
        in_specs=[pl.BlockSpec(memory_space=pltpu.SMEM)] + [anywhere] * 6,
        out_specs=[anywhere] * 5,
        scratch_shapes=[
            *(pltpu.VMEM(x.shape, bf16) for x in (resp_q, prompt_k, prompt_v, resp_k, resp_v, resp_grad)),
            *(pltpu.VMEM(x.shape, f32) for x in outs),
            pltpu.VMEM((2 * heads, ROWS, HD), bf16),
            pltpu.VMEM((2 * heads, ROWS, HD), bf16),
            stat,
            stat,
            stat,
            pltpu.VMEM((blocks, 8, ROWS), f32),
            pltpu.VMEM((blocks, CHUNK, ROWS), f32),
            pltpu.VMEM((blocks, CHUNK, ROWS), f32),
            pltpu.VMEM((2 * heads, HD, ROWS), f32),
            pltpu.VMEM((heads, HD, ROWS), bf16),
            pltpu.VMEM((heads, HD, ROWS), bf16),
            pltpu.VMEM((2, 3, 8, ROWS), f32),
            pltpu.VMEM((2, 3, 8, ROWS), f32),
            pltpu.VMEM((ROUNDS,) + piece, bf16),
            pltpu.VMEM(piece, bf16),
            pltpu.VMEM(piece, bf16),
            pltpu.VMEM((2 * ROUNDS, 2) + piece, bf16),
            pltpu.VMEM((2 * ROUNDS, 2) + piece, f32),
            pltpu.VMEM((ROUNDS,) + piece, bf16),
            pltpu.VMEM((ROUNDS,) + piece, bf16),
            pltpu.VMEM((ROUNDS, 2) + piece, bf16),
            pltpu.VMEM((ROUNDS, 2) + piece, bf16),
            pltpu.VMEM((ROUNDS,) + piece, bf16),
            pltpu.VMEM((ROUNDS,) + piece, bf16),
            pltpu.SemaphoreType.DMA((11,)),
            *sems(2),
            *sems(2),
            *sems(1),
            *sems(ROUNDS, 6, 2),
            *sems(ROUNDS, 2),
            *sems(ROUNDS, 2),
            *sems(ROUNDS, 2),
        ],
        compiler_params=pltpu.CompilerParams(
            vmem_limit_bytes=61 * 1024 * 1024, collective_id=0, has_side_effects=True
        ),
        cost_estimate=pl.CostEstimate(flops=flops, bytes_accessed=3 << 20, transcendentals=0),
    )(lengths, resp_q, prompt_k, prompt_v, resp_k, resp_v, resp_grad)
    return pl.pallas_call(
        copy_kernel,
        out_shape=outs,
        in_specs=[anywhere] * 5,
        out_specs=[anywhere] * 5,
        scratch_shapes=[pltpu.VMEM(x.shape, f32) for x in outs] + [pltpu.SemaphoreType.DMA((2, 5))],
        compiler_params=pltpu.CompilerParams(vmem_limit_bytes=61 * 1024 * 1024),
    )(*results)


def solution(mesh):
    rows = P(("dp", "resp", "tensor"), None)
    both = P(("dp", "resp"), "tensor")
    return jax.shard_map(
        local,
        mesh=mesh,
        in_specs=(rows, rows, both, both, both, both, P(("dp", "resp"))),
        out_specs=(both, both, both, rows, rows),
        check_vma=False,
    )
```

```python
import jax
import jax.numpy as jnp
from jax import lax
from jax.experimental import pallas as pl
from jax.experimental.pallas import tpu as pltpu
from jax.sharding import PartitionSpec as P

HD = 128
SCALE = HD**-0.5
LOG2E = 1.4426950408889634
NEG = -1e30
ROWS = 256
CHUNK = 256

CONTRACT_LAST = (((1,), (1,)), ((), ()))
PLAIN = (((1,), (0,)), ((), ()))


def dot(a, b, dims):
    return lax.dot_general(a, b, dims, preferred_element_type=jnp.float32)


MESH = pl.DeviceIdType.MESH
QUARTER = 128
ROUNDS = 4
TURN = (0, 1, 3, 2)
SPREAD, AHEAD, BEHIND, FAR_K, FAR_V = range(5)

FIRST = ("b0o", "b0t", "c0o", "c0t", "c1o", "c1t", "b1o", "b1t", "b2o", "b2t", "b3t", "d0t", "b3o", "d1t", "d0o", "d1o")
SECOND = ("d1o", "d0o", "d1t", "d0t", "b3o", "b3t", "b2o", "b2t", "b1o", "b1t", "c1t", "c1o", "c0t", "c0o", "b0t", "b0o")
BASE = {"b": 0, "c": 4, "d": 6}


def code(name):
    return (BASE[name[0]] + int(name[1])) * 2 + (name[2] == "t")


def place(letter, n):
    return BASE[letter] + n // 2, n % 2


def pick(step, order):
    chosen = code(order[0])
    for at, name in enumerate(order[1:], 1):
        chosen = jnp.where(step == at, code(name), chosen)
    return chosen // 2, chosen % 2


def attend(base, group, count, keys, vals, causal, qs, lives, peak, denom, weighted, peaks, exps, gprobs):
    for h in range(count):
        at, g = base + h, group + h
        scores = dot(keys, qs[g], CONTRACT_LAST) * (SCALE * LOG2E)
        if causal is not None:
            scores = jnp.where(causal, scores, NEG)
        gprob = dot(vals, lives[g], CONTRACT_LAST)
        scores = scores.reshape(CHUNK // 8, 8, ROWS)
        old = peak[g]
        new = jnp.maximum(old, jnp.max(scores, axis=0))
        raw = jnp.exp2(scores - new[None])
        shrink = jnp.exp2(old - new)
        peak[g] = new
        denom[g] = denom[g] * shrink + jnp.sum(raw, axis=0)
        weighted[g] = weighted[g] * shrink + jnp.sum(raw * gprob.reshape(raw.shape), axis=0)
        peaks[at] = new
        exps[at] = raw.reshape(CHUNK, ROWS)
        gprobs[at] = gprob


def join_sums(group, count, peak, denom, weighted, out):
    for h in range(count):
        top = jnp.max(peak[group + h], axis=0, keepdims=True)
        share = jnp.exp2(peak[group + h] - top)
        out[0, h : h + 1] = top
        out[1, h : h + 1] = jnp.sum(denom[group + h] * share, axis=0, keepdims=True)
        out[2, h : h + 1] = jnp.sum(weighted[group + h] * share, axis=0, keepdims=True)


def finish_stats(group, count, one, two, peak, weighted):
    for h in range(count):
        row = slice(h, h + 1)
        top = jnp.maximum(one[0, row], two[0, row])
        share_one, share_two = jnp.exp2(one[0, row] - top), jnp.exp2(two[0, row] - top)
        total = one[1, row] * share_one + two[1, row] * share_two
        mean = (one[2, row] * share_one + two[2, row] * share_two) / total
        peak[group + h] = jnp.broadcast_to(top + jnp.log2(total), (8, ROWS))
        weighted[group + h] = jnp.broadcast_to(mean, (8, ROWS))


def grads(base, group, count, keys, qs, lives, peak, weighted, peaks, exps, gprobs, dq):
    keys_t = keys.T
    probs, dscores = [], []
    for h in range(count):
        at, g = base + h, group + h
        factor = jnp.exp2(peaks[at] - peak[g])
        prob = exps[at].reshape(CHUNK // 8, 8, ROWS) * factor[None]
        dscore = prob * (gprobs[at].reshape(CHUNK // 8, 8, ROWS) - weighted[g][None])
        probs.append(prob.reshape(CHUNK, ROWS).astype(jnp.bfloat16))
        dscore = dscore.reshape(CHUNK, ROWS).astype(jnp.bfloat16)
        dscores.append(dscore)
        dq[g] += dot(keys_t, dscore, PLAIN)
    rows = pl.ds(group, count)
    grad_v = dot(jnp.concatenate(probs, axis=1), lives[rows].reshape(count * ROWS, HD), PLAIN)
    grad_k = dot(jnp.concatenate(dscores, axis=1), qs[rows].reshape(count * ROWS, HD), PLAIN)
    return grad_k, grad_v


def kernel(lengths, q_hbm, pk_hbm, pv_hbm, rk_hbm, rv_hbm, g_hbm, dq_hbm, drk_hbm, drv_hbm, dpk_hbm, dpv_hbm,
           q, pk, pv, rk, rv, g, dq_out, drk, drv, dpk, dpv,
           qs, lives, peak, denom, weighted, peaks, exps, gprobs, dq, dq_send, dq_in,
           stat_out, stat_in, packed, kv, own, half_out, half_in, ring_out, ring_in, z_out, z_in,
           local_s, swap_s, swap_r, stat_s, stat_r, dq_s, dq_r, get_s, get_r, half_s, half_r, ring_s, ring_r, z_s, z_r):
    heads = q.shape[1] // HD
    resp, tensor = lax.axis_index("resp"), lax.axis_index("tensor")
    chip, core = resp // 2, resp % 2
    up = {"resp": (chip + 1) % 4 * 2 + core}
    down = {"resp": (chip + 3) % 4 * 2 + core}
    twin = {"resp": chip * 2 + 1 - core}

    def along(turn):
        return {"tensor": (tensor + turn) % 4}

    def columns(index):
        return pl.ds(pl.multiple_of(index * HD, HD), HD)

    barrier = pltpu.get_barrier_semaphore()
    for other in (up, down, twin, along(1), along(2), along(3)):
        pl.semaphore_signal(barrier, inc=1, device_id=other, device_id_type=MESH)
    moves_in = [
        pltpu.make_async_copy(src, dst, local_s.at[i])
        for i, (src, dst) in enumerate(
            ((pk_hbm, pk), (pv_hbm, pv), (q_hbm, q), (g_hbm, g), (rk_hbm, rk), (rv_hbm, rv))
        )
    ]
    for move in moves_in:
        move.start()

    def send(src, dst, sems, at, to):
        return pltpu.make_async_remote_copy(
            src_ref=src, dst_ref=dst, send_sem=sems[0].at[at], recv_sem=sems[1].at[at],
            device_id=to, device_id_type=MESH,
        )

    def get(n, kind):
        mine, far = kv.at[*place("c", n)], kv.at[*place("d", n)]
        if kind == SPREAD:
            ends = [(packed.at[n, part], mine.at[part], along(TURN[n])) for part in range(2)]
        elif kind == AHEAD:
            ends = [(mine.at[part], kv.at[n, 0, part], up) for part in range(2)]
        elif kind == BEHIND:
            ends = [(mine.at[part], kv.at[n, 1, part], down) for part in range(2)]
        elif kind == FAR_K:
            ends = [(kv.at[n, 0, 0], far.at[0], up)]
        else:
            ends = [(kv.at[n, 1, 1], far.at[1], down)]
        return [send(src, dst, (get_s, get_r), (n, kind, i), to) for i, (src, dst, to) in enumerate(ends)]

    def start(copies):
        for copy in copies:
            copy.start()

    def received(copies):
        for copy in copies:
            copy.wait_recv()

    def begin(n):
        if n:
            received(get(n, SPREAD))
        start(get(n, AHEAD))
        start(get(n, BEHIND))

    def forward(n):
        received(get(n, AHEAD))
        start(get(n, FAR_K))
        received(get(n, BEHIND))
        start(get(n, FAR_V))

    def swap():
        return [
            send(ref.at[h], ref.at[heads + h], (swap_s, swap_r), (i, h), twin)
            for h in range(heads)
            for i, ref in enumerate((qs, lives))
        ]

    positions = lax.broadcasted_iota(jnp.int32, (ROWS, HD), 0)
    alive = positions < lengths[0]
    moves_in[0].wait()
    moves_in[1].wait()
    kv[4, 0, 0] = pk[:, columns(tensor)]
    kv[4, 0, 1] = pv[:, columns(tensor)]
    for n in range(1, ROUNDS):
        cols = columns((tensor + TURN[n]) % 4)
        packed[n, 0] = pk[:, cols]
        packed[n, 1] = pv[:, cols]
    pl.semaphore_wait(barrier, 6)
    begin(0)
    for n in range(1, ROUNDS):
        start(get(n, SPREAD))
    moves_in[2].wait()
    moves_in[3].wait()
    for h in range(heads):
        cols = slice(h * HD, (h + 1) * HD)
        qs[h] = q[:, cols]
        lives[h] = jnp.where(alive, g[:, cols], jnp.zeros((), jnp.bfloat16))
    start(swap())
    moves_in[4].wait()
    moves_in[5].wait()
    peak[...] = jnp.full(peak.shape, NEG, jnp.float32)
    denom[...] = jnp.zeros(denom.shape, jnp.float32)
    weighted[...] = jnp.zeros(weighted.shape, jnp.float32)
    dq[...] = jnp.zeros(dq.shape, jnp.float32)
    own[...] = jnp.zeros(own.shape, jnp.float32)
    causal = lax.broadcasted_iota(jnp.int32, (CHUNK, ROWS), 0) <= lax.broadcasted_iota(jnp.int32, (CHUNK, ROWS), 1)
    sums = (qs, lives, peak, denom, weighted, peaks, exps, gprobs)
    steps = len(FIRST)
    attend(steps * heads, 0, heads, rk[...], rv[...], causal, *sums)

    def far_received(*rounds):
        for n in rounds:
            received(get(n, FAR_K) + get(n, FAR_V))

    before = {
        "b0o": (lambda: forward(0),),
        "b0t": (lambda: received(swap()),),
        "d0t": (lambda: far_received(0, 1),),
        "d1t": (lambda: far_received(2, 3),),
    }
    after = {
        "b0o": (lambda: begin(1), lambda: begin(2)),
        "c0t": (lambda: begin(3),),
        "c1o": (lambda: forward(1), lambda: forward(2)),
        "b2o": (lambda: forward(3),),
    }

    def serve(step, order, table):
        for name, jobs in table.items():
            @pl.when(step == order.index(name))
            def _():
                for job in jobs:
                    job()

    def first(step, carry):
        chunk, half = pick(step, FIRST)
        serve(step, FIRST, before)
        keys = kv[chunk, :, 0].reshape(CHUNK, HD)
        vals = kv[chunk, :, 1].reshape(CHUNK, HD)
        attend((chunk * 2 + half) * heads, half * heads, heads, keys, vals, None, *sums)
        serve(step, FIRST, after)

        @pl.when(step == FIRST.index("d1t"))
        def _():
            join_sums(heads, heads, peak, denom, weighted, stat_out.at[1])
            tell(1).start()

        return carry

    def tell(half):
        return send(stat_out.at[half], stat_in.at[1 - half], (stat_s, stat_r), 1 - half, twin)

    lax.fori_loop(0, steps, first, 0)
    join_sums(0, heads, peak, denom, weighted, stat_out.at[0])
    tell(0).start()
    tell(1).wait_recv()
    finish_stats(0, heads, stat_out.at[0], stat_in.at[0], peak, weighted)

    def to_half(n, part):
        return send(half_out.at[n, part], half_in.at[n, part], (half_s, half_r), (n, part), (up, down)[part])

    def to_ring(n, way):
        return [
            send(ring_out.at[n, way, part], ring_in.at[n, way, part], (ring_s, ring_r), (n, way, part), (up, down)[way])
            for part in range(2)
        ]

    def to_holder(n):
        return [
            send(z_out.at[n, part], z_in.at[n, part], (z_s, z_r), (n, part), along(4 - TURN[n])) for part in range(2)
        ]

    def to_owner(h):
        return send(dq_send.at[h], dq_in.at[h], (dq_s, dq_r), h, twin)

    def wide(ref):
        return ref.astype(jnp.float32)

    def halves(n):
        half_out[n] = own[place("d", n)].astype(jnp.bfloat16)
        to_half(n, 0).start()
        to_half(n, 1).start()

    def relay(n):
        for way in range(2):
            to_half(n, way).wait_recv()
            part = own[n, 1 - way]
            ring_out[n, way, way] = (part[way] + wide(half_in[n, way])).astype(jnp.bfloat16)
            ring_out[n, way, 1 - way] = part[1 - way].astype(jnp.bfloat16)
            start(to_ring(n, way))

    def total(n):
        received(to_ring(n, 0) + to_ring(n, 1))
        return own[place("c", n)] + wide(ring_in[n, 0]) + wide(ring_in[n, 1])

    def hand_over(n):
        z_out[n] = total(n).astype(jnp.bfloat16)
        start(to_holder(n))

    def learn():
        tell(0).wait_recv()
        finish_stats(heads, heads, stat_out.at[1], stat_in.at[1], peak, weighted)

    def return_queries():
        for h in range(heads):
            dq_send[h] = dq[heads + h].astype(jnp.bfloat16)
            to_owner(h).start()

    services = {
        "d0o": (learn,),
        "d1t": (lambda: halves(3), lambda: halves(2)),
        "d0t": (lambda: halves(1), lambda: halves(0)),
        "b2t": (lambda: relay(3), lambda: relay(2)),
        "b1t": (lambda: relay(1),),
        "c1o": (lambda: hand_over(3), lambda: hand_over(2)),
        "c0o": (lambda: hand_over(1),),
        "b0t": (return_queries,),
        "b0o": (lambda: relay(0),),
    }

    def second(step, carry):
        chunk, half = pick(step, SECOND)
        keys = kv[chunk, :, 0].reshape(CHUNK, HD)
        grad_k, grad_v = grads(
            (chunk * 2 + half) * heads, half * heads, heads, keys, qs, lives, peak, weighted, peaks, exps, gprobs, dq
        )
        grad_k = (grad_k * SCALE).reshape(2, QUARTER, HD)
        grad_v = grad_v.reshape(2, QUARTER, HD)
        own[chunk, :, 0] += grad_k
        own[chunk, :, 1] += grad_v
        serve(step, SECOND, services)
        return carry

    lax.fori_loop(0, steps, second, 0)
    grad_k, grad_v = grads(steps * heads, 0, heads, rk[...], qs, lives, peak, weighted, peaks, exps, gprobs, dq)
    drk[...] = grad_k * SCALE
    drv[...] = grad_v
    moves_out = [
        pltpu.make_async_copy(src, dst, local_s.at[6 + i])
        for i, (src, dst) in enumerate((
            (drk, drk_hbm), (drv, drv_hbm), (dq_out, dq_hbm), (dpk, dpk_hbm), (dpv, dpv_hbm)
        ))
    ]
    moves_out[0].start()
    moves_out[1].start()
    for h in range(heads):
        to_owner(h).wait_recv()
        dq_out[:, h * HD : (h + 1) * HD] = (dq[h] + wide(dq_in[h])).T * SCALE
    moves_out[2].start()
    sums_now = total(0)
    dpk[:, columns(tensor)] = sums_now[0]
    dpv[:, columns(tensor)] = sums_now[1]
    for n in reversed(range(1, ROUNDS)):
        received(to_holder(n))
        cols = columns((tensor + TURN[n]) % 4)
        dpk[:, cols] = wide(z_in[n, 0])
        dpv[:, cols] = wide(z_in[n, 1])
    moves_out[3].start()
    moves_out[4].start()
    sent = swap() + [tell(0), tell(1)] + [to_owner(h) for h in range(heads)]
    for n in range(ROUNDS):
        for kind in range(SPREAD if n else AHEAD, FAR_V + 1):
            sent += get(n, kind)
        sent += [to_half(n, 0), to_half(n, 1)] + to_ring(n, 0) + to_ring(n, 1)
        if n:
            sent += to_holder(n)
    for copy in sent:
        copy.wait_send()
    for move in moves_out:
        move.wait()


def copy_kernel(*refs):
    sems = refs[-1]
    count = (len(refs) - 1) // 3
    ins, outs, rooms = refs[:count], refs[count : 2 * count], refs[2 * count : 3 * count]
    here = [pltpu.make_async_copy(ins[i], rooms[i], sems.at[0, i]) for i in range(count)]
    away = [pltpu.make_async_copy(rooms[i], outs[i], sems.at[1, i]) for i in range(count)]
    for move in here:
        move.start()
    for i in range(count):
        here[i].wait()
        away[i].start()
    for move in away:
        move.wait()


def local(prompt_k, prompt_v, resp_q, resp_k, resp_v, resp_grad, lengths):
    heads = resp_q.shape[1] // HD
    blocks = (len(FIRST) + 1) * heads
    anywhere = pl.BlockSpec(memory_space=pl.ANY)
    f32, bf16 = jnp.float32, jnp.bfloat16
    stat = pltpu.VMEM((2 * heads, 8, ROWS), f32)
    piece = (2, QUARTER, HD)

    def sems(*shape):
        return [pltpu.SemaphoreType.DMA(shape)] * 2

    outs = tuple(jax.ShapeDtypeStruct(x.shape, f32) for x in (resp_q, resp_k, resp_v, prompt_k, prompt_v))
    flops = 10 * blocks * CHUNK * ROWS * HD
    results = pl.pallas_call(
        kernel,
        out_shape=outs,
        in_specs=[pl.BlockSpec(memory_space=pltpu.SMEM)] + [anywhere] * 6,
        out_specs=[anywhere] * 5,
        scratch_shapes=[
            *(pltpu.VMEM(x.shape, bf16) for x in (resp_q, prompt_k, prompt_v, resp_k, resp_v, resp_grad)),
            *(pltpu.VMEM(x.shape, f32) for x in outs),
            pltpu.VMEM((2 * heads, ROWS, HD), bf16),
            pltpu.VMEM((2 * heads, ROWS, HD), bf16),
            stat,
            stat,
            stat,
            pltpu.VMEM((blocks, 8, ROWS), f32),
            pltpu.VMEM((blocks, CHUNK, ROWS), f32),
            pltpu.VMEM((blocks, CHUNK, ROWS), f32),
            pltpu.VMEM((2 * heads, HD, ROWS), f32),
            pltpu.VMEM((heads, HD, ROWS), bf16),
            pltpu.VMEM((heads, HD, ROWS), bf16),
            pltpu.VMEM((2, 3, 8, ROWS), f32),
            pltpu.VMEM((2, 3, 8, ROWS), f32),
            pltpu.VMEM((ROUNDS,) + piece, bf16),
            pltpu.VMEM((2 * ROUNDS, 2) + piece, bf16),
            pltpu.VMEM((2 * ROUNDS, 2) + piece, f32),
            pltpu.VMEM((ROUNDS,) + piece, bf16),
            pltpu.VMEM((ROUNDS,) + piece, bf16),
            pltpu.VMEM((ROUNDS, 2) + piece, bf16),
            pltpu.VMEM((ROUNDS, 2) + piece, bf16),
            pltpu.VMEM((ROUNDS,) + piece, bf16),
            pltpu.VMEM((ROUNDS,) + piece, bf16),
            pltpu.SemaphoreType.DMA((11,)),
            *sems(2, heads),
            *sems(2),
            *sems(heads),
            *sems(ROUNDS, 5, 2),
            *sems(ROUNDS, 2),
            *sems(ROUNDS, 2, 2),
            *sems(ROUNDS, 2),
        ],
        compiler_params=pltpu.CompilerParams(
            vmem_limit_bytes=61 * 1024 * 1024, collective_id=0, has_side_effects=True
        ),
        cost_estimate=pl.CostEstimate(flops=flops, bytes_accessed=3 << 20, transcendentals=0),
    )(lengths, resp_q, prompt_k, prompt_v, resp_k, resp_v, resp_grad)
    return pl.pallas_call(
        copy_kernel,
        out_shape=outs,
        in_specs=[anywhere] * 5,
        out_specs=[anywhere] * 5,
        scratch_shapes=[pltpu.VMEM(x.shape, f32) for x in outs] + [pltpu.SemaphoreType.DMA((2, 5))],
        compiler_params=pltpu.CompilerParams(vmem_limit_bytes=61 * 1024 * 1024),
    )(*results)


def solution(mesh):
    rows = P(("dp", "resp", "tensor"), None)
    both = P(("dp", "resp"), "tensor")
    return jax.shard_map(
        local,
        mesh=mesh,
        in_specs=(rows, rows, both, both, both, both, P(("dp", "resp"))),
        out_specs=(both, both, both, rows, rows),
        check_vma=False,
    )
```

```python
import jax
import jax.numpy as jnp
from jax import lax
from jax.experimental import pallas as pl
from jax.experimental.pallas import tpu as pltpu
from jax.sharding import PartitionSpec as P

HD = 128
SCALE = HD**-0.5
LOG2E = 1.4426950408889634
NEG = -1e30
ROWS = 256
CHUNK = 256

CONTRACT_LAST = (((1,), (1,)), ((), ()))
PLAIN = (((1,), (0,)), ((), ()))


def dot(a, b, dims):
    return lax.dot_general(a, b, dims, preferred_element_type=jnp.float32)


MESH = pl.DeviceIdType.MESH
QUARTER = 128
ROUNDS = 4
TURN = (0, 1, 3, 2)
SPREAD, AHEAD, BEHIND, FAR_K, FAR_V = range(5)

FIRST = ("b0o", "b0t", "c0o", "c0t", "b1o", "b1t", "b2o", "b2t", "d0o", "d0t", "c1o", "c1t", "b3t", "b3o", "d1t", "d1o")
SECOND = ("d1o", "d0o", "d1t", "d0t", "b3o", "b3t", "b2o", "b2t", "b1o", "b1t", "c1t", "c1o", "c0t", "c0o", "b0t", "b0o")
BASE = {"b": 0, "c": 4, "d": 6}


def code(name):
    return (BASE[name[0]] + int(name[1])) * 2 + (name[2] == "t")


def place(letter, n):
    return BASE[letter] + n // 2, n % 2


def pick(step, order):
    chosen = code(order[0])
    for at, name in enumerate(order[1:], 1):
        chosen = jnp.where(step == at, code(name), chosen)
    return chosen // 2, chosen % 2


def attend(base, group, count, keys, vals, causal, qs, lives, peak, denom, weighted, peaks, exps, gprobs):
    for h in range(count):
        at, g = base + h, group + h
        scores = dot(keys, qs[g], CONTRACT_LAST) * (SCALE * LOG2E)
        if causal is not None:
            scores = jnp.where(causal, scores, NEG)
        gprob = dot(vals, lives[g], CONTRACT_LAST)
        scores = scores.reshape(CHUNK // 8, 8, ROWS)
        old = peak[g]
        new = jnp.maximum(old, jnp.max(scores, axis=0))
        raw = jnp.exp2(scores - new[None])
        shrink = jnp.exp2(old - new)
        peak[g] = new
        denom[g] = denom[g] * shrink + jnp.sum(raw, axis=0)
        weighted[g] = weighted[g] * shrink + jnp.sum(raw * gprob.reshape(raw.shape), axis=0)
        peaks[at] = new
        exps[at] = raw.reshape(CHUNK, ROWS)
        gprobs[at] = gprob


def join_sums(group, count, peak, denom, weighted, out):
    for h in range(count):
        top = jnp.max(peak[group + h], axis=0, keepdims=True)
        share = jnp.exp2(peak[group + h] - top)
        out[0, h : h + 1] = top
        out[1, h : h + 1] = jnp.sum(denom[group + h] * share, axis=0, keepdims=True)
        out[2, h : h + 1] = jnp.sum(weighted[group + h] * share, axis=0, keepdims=True)


def finish_stats(group, count, one, two, peak, weighted):
    for h in range(count):
        row = slice(h, h + 1)
        top = jnp.maximum(one[0, row], two[0, row])
        share_one, share_two = jnp.exp2(one[0, row] - top), jnp.exp2(two[0, row] - top)
        total = one[1, row] * share_one + two[1, row] * share_two
        mean = (one[2, row] * share_one + two[2, row] * share_two) / total
        peak[group + h] = jnp.broadcast_to(top + jnp.log2(total), (8, ROWS))
        weighted[group + h] = jnp.broadcast_to(mean, (8, ROWS))


def grads(base, group, count, keys, qs, lives, peak, weighted, peaks, exps, gprobs, dq):
    keys_t = keys.T
    probs, dscores = [], []
    for h in range(count):
        at, g = base + h, group + h
        factor = jnp.exp2(peaks[at] - peak[g])
        prob = exps[at].reshape(CHUNK // 8, 8, ROWS) * factor[None]
        dscore = prob * (gprobs[at].reshape(CHUNK // 8, 8, ROWS) - weighted[g][None])
        probs.append(prob.reshape(CHUNK, ROWS).astype(jnp.bfloat16))
        dscore = dscore.reshape(CHUNK, ROWS).astype(jnp.bfloat16)
        dscores.append(dscore)
        dq[g] += dot(keys_t, dscore, PLAIN)
    rows = pl.ds(group, count)
    grad_v = dot(jnp.concatenate(probs, axis=1), lives[rows].reshape(count * ROWS, HD), PLAIN)
    grad_k = dot(jnp.concatenate(dscores, axis=1), qs[rows].reshape(count * ROWS, HD), PLAIN)
    return grad_k, grad_v


def kernel(lengths, q_hbm, pk_hbm, pv_hbm, rk_hbm, rv_hbm, g_hbm, dq_hbm, drk_hbm, drv_hbm, dpk_hbm, dpv_hbm,
           q, pk, pv, rk, rv, g, dq_out, drk, drv, dpk, dpv,
           qs, lives, peak, denom, weighted, peaks, exps, gprobs, dq, dq_send, dq_in,
           stat_out, stat_in, packed, kv, own, half_out, half_in, ring_out, ring_in, z_out, z_in,
           local_s, swap_s, swap_r, stat_s, stat_r, dq_s, dq_r, get_s, get_r, half_s, half_r, ring_s, ring_r, z_s, z_r):
    heads = q.shape[1] // HD
    resp, tensor = lax.axis_index("resp"), lax.axis_index("tensor")
    chip, core = resp // 2, resp % 2
    up = {"resp": (chip + 1) % 4 * 2 + core}
    down = {"resp": (chip + 3) % 4 * 2 + core}
    twin = {"resp": chip * 2 + 1 - core}

    def along(turn):
        return {"tensor": (tensor + turn) % 4}

    def columns(index):
        return pl.ds(pl.multiple_of(index * HD, HD), HD)

    barrier = pltpu.get_barrier_semaphore()
    for other in (up, down, twin, along(1), along(2), along(3)):
        pl.semaphore_signal(barrier, inc=1, device_id=other, device_id_type=MESH)
    moves_in = [
        pltpu.make_async_copy(src, dst, local_s.at[i])
        for i, (src, dst) in enumerate(
            ((pk_hbm, pk), (pv_hbm, pv), (q_hbm, q), (g_hbm, g), (rk_hbm, rk), (rv_hbm, rv))
        )
    ]
    for move in moves_in:
        move.start()

    def send(src, dst, sems, at, to):
        return pltpu.make_async_remote_copy(
            src_ref=src, dst_ref=dst, send_sem=sems[0].at[at], recv_sem=sems[1].at[at],
            device_id=to, device_id_type=MESH,
        )

    def get(n, kind):
        mine, far = kv.at[*place("c", n)], kv.at[*place("d", n)]
        if kind == SPREAD:
            ends = [(packed.at[n, part], mine.at[part], along(TURN[n])) for part in range(2)]
        elif kind == AHEAD:
            ends = [(mine.at[part], kv.at[n, 0, part], up) for part in range(2)]
        elif kind == BEHIND:
            ends = [(mine.at[part], kv.at[n, 1, part], down) for part in range(2)]
        elif kind == FAR_K:
            ends = [(kv.at[n, 0, 0], far.at[0], up)]
        else:
            ends = [(kv.at[n, 1, 1], far.at[1], down)]
        return [send(src, dst, (get_s, get_r), (n, kind, i), to) for i, (src, dst, to) in enumerate(ends)]

    def start(copies):
        for copy in copies:
            copy.start()

    def received(copies):
        for copy in copies:
            copy.wait_recv()

    def begin(n):
        if n:
            received(get(n, SPREAD))
        start(get(n, AHEAD))
        start(get(n, BEHIND))

    def forward(n):
        received(get(n, AHEAD))
        start(get(n, FAR_K))
        received(get(n, BEHIND))
        start(get(n, FAR_V))

    def swap():
        return [
            send(ref.at[h], ref.at[heads + h], (swap_s, swap_r), (i, h), twin)
            for h in range(heads)
            for i, ref in enumerate((qs, lives))
        ]

    positions = lax.broadcasted_iota(jnp.int32, (ROWS, HD), 0)
    alive = positions < lengths[0]
    moves_in[0].wait()
    moves_in[1].wait()
    kv[4, 0, 0] = pk[:, columns(tensor)]
    kv[4, 0, 1] = pv[:, columns(tensor)]
    for n in range(1, ROUNDS):
        cols = columns((tensor + TURN[n]) % 4)
        packed[n, 0] = pk[:, cols]
        packed[n, 1] = pv[:, cols]
    pl.semaphore_wait(barrier, 6)
    begin(0)
    for n in range(1, ROUNDS):
        start(get(n, SPREAD))
    moves_in[2].wait()
    moves_in[3].wait()
    for h in range(heads):
        cols = slice(h * HD, (h + 1) * HD)
        qs[h] = q[:, cols]
        lives[h] = jnp.where(alive, g[:, cols], jnp.zeros((), jnp.bfloat16))
    start(swap())
    moves_in[4].wait()
    moves_in[5].wait()
    peak[...] = jnp.full(peak.shape, NEG, jnp.float32)
    denom[...] = jnp.zeros(denom.shape, jnp.float32)
    weighted[...] = jnp.zeros(weighted.shape, jnp.float32)
    dq[...] = jnp.zeros(dq.shape, jnp.float32)
    own[...] = jnp.zeros(own.shape, jnp.float32)
    causal = lax.broadcasted_iota(jnp.int32, (CHUNK, ROWS), 0) <= lax.broadcasted_iota(jnp.int32, (CHUNK, ROWS), 1)
    sums = (qs, lives, peak, denom, weighted, peaks, exps, gprobs)
    steps = len(FIRST)
    attend(steps * heads, 0, heads, rk[...], rv[...], causal, *sums)

    def far_received(*rounds):
        for n in rounds:
            received(get(n, FAR_K) + get(n, FAR_V))

    before = {
        "b0o": (lambda: forward(0),),
        "b0t": (lambda: received(swap()),),
        "b1o": (lambda: forward(1),),
        "b2o": (lambda: forward(2),),
        "d0o": (lambda: far_received(0, 1),),
        "b3t": (lambda: forward(3),),
        "d1t": (lambda: far_received(2, 3),),
    }
    after = {
        "b0o": (lambda: begin(1), lambda: begin(2)),
        "b2t": (lambda: begin(3),),
    }

    def serve(step, order, table):
        for name, jobs in table.items():
            @pl.when(step == order.index(name))
            def _():
                for job in jobs:
                    job()

    def first(step, carry):
        chunk, half = pick(step, FIRST)
        serve(step, FIRST, before)
        keys = kv[chunk, :, 0].reshape(CHUNK, HD)
        vals = kv[chunk, :, 1].reshape(CHUNK, HD)
        attend((chunk * 2 + half) * heads, half * heads, heads, keys, vals, None, *sums)
        serve(step, FIRST, after)

        @pl.when(step == FIRST.index("d1t"))
        def _():
            join_sums(heads, heads, peak, denom, weighted, stat_out.at[1])
            tell(1).start()

        return carry

    def tell(half):
        return send(stat_out.at[half], stat_in.at[1 - half], (stat_s, stat_r), 1 - half, twin)

    lax.fori_loop(0, steps, first, 0)
    join_sums(0, heads, peak, denom, weighted, stat_out.at[0])
    tell(0).start()
    tell(1).wait_recv()
    finish_stats(0, heads, stat_out.at[0], stat_in.at[0], peak, weighted)

    def to_half(n, part):
        return send(half_out.at[n, part], half_in.at[n, part], (half_s, half_r), (n, part), (up, down)[part])

    def to_ring(n, way):
        return [
            send(ring_out.at[n, way, part], ring_in.at[n, way, part], (ring_s, ring_r), (n, way, part), (up, down)[way])
            for part in range(2)
        ]

    def to_holder(n):
        return [
            send(z_out.at[n, part], z_in.at[n, part], (z_s, z_r), (n, part), along(4 - TURN[n])) for part in range(2)
        ]

    def to_owner(h):
        return send(dq_send.at[h], dq_in.at[h], (dq_s, dq_r), h, twin)

    def wide(ref):
        return ref.astype(jnp.float32)

    def halves(n):
        half_out[n] = own[place("d", n)].astype(jnp.bfloat16)
        to_half(n, 0).start()
        to_half(n, 1).start()

    def relay(n):
        for way in range(2):
            to_half(n, way).wait_recv()
            part = own[n, 1 - way]
            ring_out[n, way, way] = (part[way] + wide(half_in[n, way])).astype(jnp.bfloat16)
            ring_out[n, way, 1 - way] = part[1 - way].astype(jnp.bfloat16)
            start(to_ring(n, way))

    def total(n):
        received(to_ring(n, 0) + to_ring(n, 1))
        return own[place("c", n)] + wide(ring_in[n, 0]) + wide(ring_in[n, 1])

    def hand_over(n):
        z_out[n] = total(n).astype(jnp.bfloat16)
        start(to_holder(n))

    def learn():
        tell(0).wait_recv()
        finish_stats(heads, heads, stat_out.at[1], stat_in.at[1], peak, weighted)

    def return_queries():
        for h in range(heads):
            dq_send[h] = dq[heads + h].astype(jnp.bfloat16)
            to_owner(h).start()

    services = {
        "d0o": (learn,),
        "d1t": (lambda: halves(3), lambda: halves(2)),
        "d0t": (lambda: halves(1), lambda: halves(0)),
        "b2t": (lambda: relay(3), lambda: relay(2)),
        "b1t": (lambda: relay(1),),
        "c1o": (lambda: hand_over(3), lambda: hand_over(2)),
        "c0o": (lambda: hand_over(1),),
        "b0t": (return_queries,),
        "b0o": (lambda: relay(0),),
    }

    def second(step, carry):
        chunk, half = pick(step, SECOND)
        keys = kv[chunk, :, 0].reshape(CHUNK, HD)
        grad_k, grad_v = grads(
            (chunk * 2 + half) * heads, half * heads, heads, keys, qs, lives, peak, weighted, peaks, exps, gprobs, dq
        )
        grad_k = (grad_k * SCALE).reshape(2, QUARTER, HD)
        grad_v = grad_v.reshape(2, QUARTER, HD)
        own[chunk, :, 0] += grad_k
        own[chunk, :, 1] += grad_v
        serve(step, SECOND, services)
        return carry

    lax.fori_loop(0, steps, second, 0)
    grad_k, grad_v = grads(steps * heads, 0, heads, rk[...], qs, lives, peak, weighted, peaks, exps, gprobs, dq)
    drk[...] = grad_k * SCALE
    drv[...] = grad_v
    moves_out = [
        pltpu.make_async_copy(src, dst, local_s.at[6 + i])
        for i, (src, dst) in enumerate((
            (drk, drk_hbm), (drv, drv_hbm), (dq_out, dq_hbm), (dpk, dpk_hbm), (dpv, dpv_hbm)
        ))
    ]
    moves_out[0].start()
    moves_out[1].start()
    for h in range(heads):
        to_owner(h).wait_recv()
        dq_out[:, h * HD : (h + 1) * HD] = (dq[h] + wide(dq_in[h])).T * SCALE
    moves_out[2].start()
    sums_now = total(0)
    dpk[:, columns(tensor)] = sums_now[0]
    dpv[:, columns(tensor)] = sums_now[1]
    for n in reversed(range(1, ROUNDS)):
        received(to_holder(n))
        cols = columns((tensor + TURN[n]) % 4)
        dpk[:, cols] = wide(z_in[n, 0])
        dpv[:, cols] = wide(z_in[n, 1])
    moves_out[3].start()
    moves_out[4].start()
    sent = swap() + [tell(0), tell(1)] + [to_owner(h) for h in range(heads)]
    for n in range(ROUNDS):
        for kind in range(SPREAD if n else AHEAD, FAR_V + 1):
            sent += get(n, kind)
        sent += [to_half(n, 0), to_half(n, 1)] + to_ring(n, 0) + to_ring(n, 1)
        if n:
            sent += to_holder(n)
    for copy in sent:
        copy.wait_send()
    for move in moves_out:
        move.wait()


def copy_kernel(*refs):
    sems = refs[-1]
    count = (len(refs) - 1) // 3
    ins, outs, rooms = refs[:count], refs[count : 2 * count], refs[2 * count : 3 * count]
    here = [pltpu.make_async_copy(ins[i], rooms[i], sems.at[0, i]) for i in range(count)]
    away = [pltpu.make_async_copy(rooms[i], outs[i], sems.at[1, i]) for i in range(count)]
    for move in here:
        move.start()
    for i in range(count):
        here[i].wait()
        away[i].start()
    for move in away:
        move.wait()


def local(prompt_k, prompt_v, resp_q, resp_k, resp_v, resp_grad, lengths):
    heads = resp_q.shape[1] // HD
    blocks = (len(FIRST) + 1) * heads
    anywhere = pl.BlockSpec(memory_space=pl.ANY)
    f32, bf16 = jnp.float32, jnp.bfloat16
    stat = pltpu.VMEM((2 * heads, 8, ROWS), f32)
    piece = (2, QUARTER, HD)

    def sems(*shape):
        return [pltpu.SemaphoreType.DMA(shape)] * 2

    outs = tuple(jax.ShapeDtypeStruct(x.shape, f32) for x in (resp_q, resp_k, resp_v, prompt_k, prompt_v))
    flops = 10 * blocks * CHUNK * ROWS * HD
    results = pl.pallas_call(
        kernel,
        out_shape=outs,
        in_specs=[pl.BlockSpec(memory_space=pltpu.SMEM)] + [anywhere] * 6,
        out_specs=[anywhere] * 5,
        scratch_shapes=[
            *(pltpu.VMEM(x.shape, bf16) for x in (resp_q, prompt_k, prompt_v, resp_k, resp_v, resp_grad)),
            *(pltpu.VMEM(x.shape, f32) for x in outs),
            pltpu.VMEM((2 * heads, ROWS, HD), bf16),
            pltpu.VMEM((2 * heads, ROWS, HD), bf16),
            stat,
            stat,
            stat,
            pltpu.VMEM((blocks, 8, ROWS), f32),
            pltpu.VMEM((blocks, CHUNK, ROWS), f32),
            pltpu.VMEM((blocks, CHUNK, ROWS), f32),
            pltpu.VMEM((2 * heads, HD, ROWS), f32),
            pltpu.VMEM((heads, HD, ROWS), bf16),
            pltpu.VMEM((heads, HD, ROWS), bf16),
            pltpu.VMEM((2, 3, 8, ROWS), f32),
            pltpu.VMEM((2, 3, 8, ROWS), f32),
            pltpu.VMEM((ROUNDS,) + piece, bf16),
            pltpu.VMEM((2 * ROUNDS, 2) + piece, bf16),
            pltpu.VMEM((2 * ROUNDS, 2) + piece, f32),
            pltpu.VMEM((ROUNDS,) + piece, bf16),
            pltpu.VMEM((ROUNDS,) + piece, bf16),
            pltpu.VMEM((ROUNDS, 2) + piece, bf16),
            pltpu.VMEM((ROUNDS, 2) + piece, bf16),
            pltpu.VMEM((ROUNDS,) + piece, bf16),
            pltpu.VMEM((ROUNDS,) + piece, bf16),
            pltpu.SemaphoreType.DMA((11,)),
            *sems(2, heads),
            *sems(2),
            *sems(heads),
            *sems(ROUNDS, 5, 2),
            *sems(ROUNDS, 2),
            *sems(ROUNDS, 2, 2),
            *sems(ROUNDS, 2),
        ],
        compiler_params=pltpu.CompilerParams(
            vmem_limit_bytes=61 * 1024 * 1024, collective_id=0, has_side_effects=True
        ),
        cost_estimate=pl.CostEstimate(flops=flops, bytes_accessed=3 << 20, transcendentals=0),
    )(lengths, resp_q, prompt_k, prompt_v, resp_k, resp_v, resp_grad)
    return pl.pallas_call(
        copy_kernel,
        out_shape=outs,
        in_specs=[anywhere] * 5,
        out_specs=[anywhere] * 5,
        scratch_shapes=[pltpu.VMEM(x.shape, f32) for x in outs] + [pltpu.SemaphoreType.DMA((2, 5))],
        compiler_params=pltpu.CompilerParams(vmem_limit_bytes=61 * 1024 * 1024),
    )(*results)


def solution(mesh):
    rows = P(("dp", "resp", "tensor"), None)
    both = P(("dp", "resp"), "tensor")
    return jax.shard_map(
        local,
        mesh=mesh,
        in_specs=(rows, rows, both, both, both, both, P(("dp", "resp"))),
        out_specs=(both, both, both, rows, rows),
        check_vma=False,
    )
```

```python
import jax
import jax.numpy as jnp
from jax import lax
from jax.experimental import pallas as pl
from jax.experimental.pallas import tpu as pltpu
from jax.sharding import PartitionSpec as P

HD = 128
SCALE = HD**-0.5
LOG2E = 1.4426950408889634
NEG = -1e30
ROWS = 256
CHUNK = 256

CONTRACT_LAST = (((1,), (1,)), ((), ()))
PLAIN = (((1,), (0,)), ((), ()))


def dot(a, b, dims):
    return lax.dot_general(a, b, dims, preferred_element_type=jnp.float32)


MESH = pl.DeviceIdType.MESH
QUARTER = 128
ROUNDS = 4
TURN = (0, 1, 3, 2)
SPREAD, AHEAD, BEHIND, ACROSS = range(4)

FIRST = ("b0o", "c0o", "b0t", "c0t", "c1o", "c1t", "b1o", "b1t", "b2o", "b2t", "b3t", "d0t", "b3o", "d1t", "d0o", "d1o")
SECOND = ("d1o", "d0o", "d1t", "d0t", "b3o", "b3t", "b2o", "b2t", "b1o", "b1t", "c1t", "c1o", "c0t", "c0o", "b0t", "b0o")
BASE = {"b": 0, "c": 4, "d": 6}


def code(name):
    return (BASE[name[0]] + int(name[1])) * 2 + (name[2] == "t")


def place(letter, n):
    return BASE[letter] + n // 2, n % 2


def pick(step, order):
    chosen = code(order[0])
    for at, name in enumerate(order[1:], 1):
        chosen = jnp.where(step == at, code(name), chosen)
    return chosen // 2, chosen % 2


def attend(base, group, count, keys, vals, causal, qs, lives, peak, denom, weighted, peaks, exps, gprobs):
    for h in range(count):
        at, g = base + h, group + h
        scores = dot(keys, qs[g], CONTRACT_LAST) * (SCALE * LOG2E)
        if causal is not None:
            scores = jnp.where(causal, scores, NEG)
        gprob = dot(vals, lives[g], CONTRACT_LAST)
        scores = scores.reshape(CHUNK // 8, 8, ROWS)
        old = peak[g]
        new = jnp.maximum(old, jnp.max(scores, axis=0))
        raw = jnp.exp2(scores - new[None])
        shrink = jnp.exp2(old - new)
        peak[g] = new
        denom[g] = denom[g] * shrink + jnp.sum(raw, axis=0)
        weighted[g] = weighted[g] * shrink + jnp.sum(raw * gprob.reshape(raw.shape), axis=0)
        peaks[at] = new
        exps[at] = raw.reshape(CHUNK, ROWS)
        gprobs[at] = gprob


def join_sums(group, count, peak, denom, weighted, out):
    for h in range(count):
        top = jnp.max(peak[group + h], axis=0, keepdims=True)
        share = jnp.exp2(peak[group + h] - top)
        out[0, h : h + 1] = top
        out[1, h : h + 1] = jnp.sum(denom[group + h] * share, axis=0, keepdims=True)
        out[2, h : h + 1] = jnp.sum(weighted[group + h] * share, axis=0, keepdims=True)


def finish_stats(group, count, one, two, peak, weighted):
    for h in range(count):
        row = slice(h, h + 1)
        top = jnp.maximum(one[0, row], two[0, row])
        share_one, share_two = jnp.exp2(one[0, row] - top), jnp.exp2(two[0, row] - top)
        total = one[1, row] * share_one + two[1, row] * share_two
        mean = (one[2, row] * share_one + two[2, row] * share_two) / total
        peak[group + h] = jnp.broadcast_to(top + jnp.log2(total), (8, ROWS))
        weighted[group + h] = jnp.broadcast_to(mean, (8, ROWS))


def grads(base, group, count, keys, qs, lives, peak, weighted, peaks, exps, gprobs, dq):
    keys_t = keys.T
    probs, dscores = [], []
    for h in range(count):
        at, g = base + h, group + h
        factor = jnp.exp2(peaks[at] - peak[g])
        prob = exps[at].reshape(CHUNK // 8, 8, ROWS) * factor[None]
        dscore = prob * (gprobs[at].reshape(CHUNK // 8, 8, ROWS) - weighted[g][None])
        probs.append(prob.reshape(CHUNK, ROWS).astype(jnp.bfloat16))
        dscore = dscore.reshape(CHUNK, ROWS).astype(jnp.bfloat16)
        dscores.append(dscore)
        dq[g] += dot(keys_t, dscore, PLAIN)
    rows = pl.ds(group, count)
    grad_v = dot(jnp.concatenate(probs, axis=1), lives[rows].reshape(count * ROWS, HD), PLAIN)
    grad_k = dot(jnp.concatenate(dscores, axis=1), qs[rows].reshape(count * ROWS, HD), PLAIN)
    return grad_k, grad_v


def kernel(lengths, q_hbm, pk_hbm, pv_hbm, rk_hbm, rv_hbm, g_hbm, dq_hbm, drk_hbm, drv_hbm, dpk_hbm, dpv_hbm,
           q, pk, pv, rk, rv, g, dq_out, drk, drv, dpk, dpv,
           qs, lives, peak, denom, weighted, peaks, exps, gprobs, dq, dq_send, dq_in,
           stat_out, stat_in, packed, kv, own, ring_out, ring_in, z_out, z_in,
           local_s, swap_s, swap_r, stat_s, stat_r, dq_s, dq_r, get_s, get_r, ring_s, ring_r, z_s, z_r):
    heads = q.shape[1] // HD
    resp, tensor = lax.axis_index("resp"), lax.axis_index("tensor")
    chip, core = resp // 2, resp % 2
    up = {"resp": (chip + 1) % 4 * 2 + core}
    down = {"resp": (chip + 3) % 4 * 2 + core}
    across = {"resp": (chip + 2) % 4 * 2 + core}
    twin = {"resp": chip * 2 + 1 - core}

    def along(turn):
        return {"tensor": (tensor + turn) % 4}

    def columns(index):
        return pl.ds(pl.multiple_of(index * HD, HD), HD)

    barrier = pltpu.get_barrier_semaphore()
    for other in (up, down, across, twin, along(1), along(2), along(3)):
        pl.semaphore_signal(barrier, inc=1, device_id=other, device_id_type=MESH)
    moves_in = [
        pltpu.make_async_copy(src, dst, local_s.at[i])
        for i, (src, dst) in enumerate(
            ((pk_hbm, pk), (pv_hbm, pv), (q_hbm, q), (g_hbm, g), (rk_hbm, rk), (rv_hbm, rv))
        )
    ]
    for move in moves_in:
        move.start()

    def send(src, dst, sems, at, to):
        return pltpu.make_async_remote_copy(
            src_ref=src, dst_ref=dst, send_sem=sems[0].at[at], recv_sem=sems[1].at[at],
            device_id=to, device_id_type=MESH,
        )

    def get(n, kind):
        mine, far = kv.at[*place("c", n)], kv.at[*place("d", n)]
        if kind == SPREAD:
            ends = [(packed.at[n, part], mine.at[part], along(TURN[n])) for part in range(2)]
        elif kind == AHEAD:
            ends = [(mine.at[part], kv.at[n, 0, part], up) for part in range(2)]
        elif kind == BEHIND:
            ends = [(mine.at[part], kv.at[n, 1, part], down) for part in range(2)]
        else:
            ends = [(mine.at[part], far.at[part], across) for part in range(2)]
        return [send(src, dst, (get_s, get_r), (n, kind, i), to) for i, (src, dst, to) in enumerate(ends)]

    def start(copies):
        for copy in copies:
            copy.start()

    def received(copies):
        for copy in copies:
            copy.wait_recv()

    def begin(n):
        if n:
            received(get(n, SPREAD))
        for kind in (AHEAD, BEHIND, ACROSS):
            start(get(n, kind))

    def near_received(n):
        received(get(n, AHEAD) + get(n, BEHIND))

    def swap():
        return [
            send(ref.at[h], ref.at[heads + h], (swap_s, swap_r), (i, h), twin)
            for h in range(heads)
            for i, ref in enumerate((qs, lives))
        ]

    positions = lax.broadcasted_iota(jnp.int32, (ROWS, HD), 0)
    alive = positions < lengths[0]
    moves_in[0].wait()
    moves_in[1].wait()
    kv[4, 0, 0] = pk[:, columns(tensor)]
    kv[4, 0, 1] = pv[:, columns(tensor)]
    for n in range(1, ROUNDS):
        cols = columns((tensor + TURN[n]) % 4)
        packed[n, 0] = pk[:, cols]
        packed[n, 1] = pv[:, cols]
    pl.semaphore_wait(barrier, 7)
    begin(0)
    for n in range(1, ROUNDS):
        start(get(n, SPREAD))
    moves_in[2].wait()
    moves_in[3].wait()
    for h in range(heads):
        cols = slice(h * HD, (h + 1) * HD)
        qs[h] = q[:, cols]
        lives[h] = jnp.where(alive, g[:, cols], jnp.zeros((), jnp.bfloat16))
    start(swap())
    moves_in[4].wait()
    moves_in[5].wait()
    peak[...] = jnp.full(peak.shape, NEG, jnp.float32)
    denom[...] = jnp.zeros(denom.shape, jnp.float32)
    weighted[...] = jnp.zeros(weighted.shape, jnp.float32)
    dq[...] = jnp.zeros(dq.shape, jnp.float32)
    own[...] = jnp.zeros(own.shape, jnp.float32)
    causal = lax.broadcasted_iota(jnp.int32, (CHUNK, ROWS), 0) <= lax.broadcasted_iota(jnp.int32, (CHUNK, ROWS), 1)
    sums = (qs, lives, peak, denom, weighted, peaks, exps, gprobs)
    steps = len(FIRST)
    attend(steps * heads, 0, heads, rk[...], rv[...], causal, *sums)

    def far_received(*rounds):
        for n in rounds:
            received(get(n, ACROSS))

    before = {
        "b0o": (lambda: near_received(0),),
        "b0t": (lambda: received(swap()),),
        "b1o": (lambda: near_received(1),),
        "b2o": (lambda: near_received(2),),
        "b3t": (lambda: near_received(3),),
        "d0t": (lambda: far_received(0, 1),),
        "d1t": (lambda: far_received(2, 3),),
    }
    after = {
        "b0o": (lambda: begin(1), lambda: begin(2)),
        "c0t": (lambda: begin(3),),
    }

    def serve(step, order, table):
        for name, jobs in table.items():
            @pl.when(step == order.index(name))
            def _():
                for job in jobs:
                    job()

    def first(step, carry):
        chunk, half = pick(step, FIRST)
        serve(step, FIRST, before)
        keys = kv[chunk, :, 0].reshape(CHUNK, HD)
        vals = kv[chunk, :, 1].reshape(CHUNK, HD)
        attend((chunk * 2 + half) * heads, half * heads, heads, keys, vals, None, *sums)
        serve(step, FIRST, after)

        @pl.when(step == FIRST.index("d1t"))
        def _():
            join_sums(heads, heads, peak, denom, weighted, stat_out.at[1])
            tell(1).start()

        return carry

    def tell(half):
        return send(stat_out.at[half], stat_in.at[1 - half], (stat_s, stat_r), 1 - half, twin)

    lax.fori_loop(0, steps, first, 0)
    join_sums(0, heads, peak, denom, weighted, stat_out.at[0])
    tell(0).start()
    tell(1).wait_recv()
    finish_stats(0, heads, stat_out.at[0], stat_in.at[0], peak, weighted)

    def to_ring(n, way):
        to = (up, down, across)[way]
        return [send(ring_out.at[n, way], ring_in.at[n, way], (ring_s, ring_r), (n, way), to)]

    def to_holder(n):
        return [
            send(z_out.at[n, part], z_in.at[n, part], (z_s, z_r), (n, part), along(4 - TURN[n])) for part in range(2)
        ]

    def to_owner(h):
        return send(dq_send.at[h], dq_in.at[h], (dq_s, dq_r), h, twin)

    def wide(ref):
        return ref.astype(jnp.float32)

    def send_far(n):
        ring_out[n, 2] = own[place("d", n)].astype(jnp.bfloat16)
        start(to_ring(n, 2))

    def send_near(n):
        for way in range(2):
            ring_out[n, way] = own[n, 1 - way].astype(jnp.bfloat16)
            start(to_ring(n, way))

    def total(n):
        for way in range(3):
            received(to_ring(n, way))
        return own[place("c", n)] + wide(ring_in[n, 0]) + wide(ring_in[n, 1]) + wide(ring_in[n, 2])

    def hand_over(n):
        z_out[n] = total(n).astype(jnp.bfloat16)
        start(to_holder(n))

    def learn():
        tell(0).wait_recv()
        finish_stats(heads, heads, stat_out.at[1], stat_in.at[1], peak, weighted)

    def return_queries():
        for h in range(heads):
            dq_send[h] = dq[heads + h].astype(jnp.bfloat16)
            to_owner(h).start()

    services = {
        "d0o": (learn,),
        "d1t": (lambda: send_far(3), lambda: send_far(2)),
        "d0t": (lambda: send_far(1), lambda: send_far(0)),
        "b3t": (lambda: send_near(3),),
        "b2t": (lambda: send_near(2),),
        "b1t": (lambda: send_near(1),),
        "c1o": (lambda: hand_over(3), lambda: hand_over(2)),
        "c0o": (lambda: hand_over(1),),
        "b0t": (return_queries,),
        "b0o": (lambda: send_near(0),),
    }

    def second(step, carry):
        chunk, half = pick(step, SECOND)
        keys = kv[chunk, :, 0].reshape(CHUNK, HD)
        grad_k, grad_v = grads(
            (chunk * 2 + half) * heads, half * heads, heads, keys, qs, lives, peak, weighted, peaks, exps, gprobs, dq
        )
        grad_k = (grad_k * SCALE).reshape(2, QUARTER, HD)
        grad_v = grad_v.reshape(2, QUARTER, HD)
        own[chunk, :, 0] += grad_k
        own[chunk, :, 1] += grad_v
        serve(step, SECOND, services)
        return carry

    lax.fori_loop(0, steps, second, 0)
    grad_k, grad_v = grads(steps * heads, 0, heads, rk[...], qs, lives, peak, weighted, peaks, exps, gprobs, dq)
    drk[...] = grad_k * SCALE
    drv[...] = grad_v
    moves_out = [
        pltpu.make_async_copy(src, dst, local_s.at[6 + i])
        for i, (src, dst) in enumerate((
            (drk, drk_hbm), (drv, drv_hbm), (dq_out, dq_hbm), (dpk, dpk_hbm), (dpv, dpv_hbm)
        ))
    ]
    moves_out[0].start()
    moves_out[1].start()
    for h in range(heads):
        to_owner(h).wait_recv()
        dq_out[:, h * HD : (h + 1) * HD] = (dq[h] + wide(dq_in[h])).T * SCALE
    moves_out[2].start()
    sums_now = total(0)
    dpk[:, columns(tensor)] = sums_now[0]
    dpv[:, columns(tensor)] = sums_now[1]
    for n in reversed(range(1, ROUNDS)):
        received(to_holder(n))
        cols = columns((tensor + TURN[n]) % 4)
        dpk[:, cols] = wide(z_in[n, 0])
        dpv[:, cols] = wide(z_in[n, 1])
    moves_out[3].start()
    moves_out[4].start()
    sent = swap() + [tell(0), tell(1)] + [to_owner(h) for h in range(heads)]
    for n in range(ROUNDS):
        for kind in range(SPREAD if n else AHEAD, ACROSS + 1):
            sent += get(n, kind)
        sent += to_ring(n, 0) + to_ring(n, 1) + to_ring(n, 2)
        if n:
            sent += to_holder(n)
    for copy in sent:
        copy.wait_send()
    for move in moves_out:
        move.wait()


def copy_kernel(*refs):
    sems = refs[-1]
    count = (len(refs) - 1) // 3
    ins, outs, rooms = refs[:count], refs[count : 2 * count], refs[2 * count : 3 * count]
    here = [pltpu.make_async_copy(ins[i], rooms[i], sems.at[0, i]) for i in range(count)]
    away = [pltpu.make_async_copy(rooms[i], outs[i], sems.at[1, i]) for i in range(count)]
    for move in here:
        move.start()
    for i in range(count):
        here[i].wait()
        away[i].start()
    for move in away:
        move.wait()


def local(prompt_k, prompt_v, resp_q, resp_k, resp_v, resp_grad, lengths):
    heads = resp_q.shape[1] // HD
    blocks = (len(FIRST) + 1) * heads
    anywhere = pl.BlockSpec(memory_space=pl.ANY)
    f32, bf16 = jnp.float32, jnp.bfloat16
    stat = pltpu.VMEM((2 * heads, 8, ROWS), f32)
    piece = (2, QUARTER, HD)

    def sems(*shape):
        return [pltpu.SemaphoreType.DMA(shape)] * 2

    outs = tuple(jax.ShapeDtypeStruct(x.shape, f32) for x in (resp_q, resp_k, resp_v, prompt_k, prompt_v))
    flops = 10 * blocks * CHUNK * ROWS * HD
    results = pl.pallas_call(
        kernel,
        out_shape=outs,
        in_specs=[pl.BlockSpec(memory_space=pltpu.SMEM)] + [anywhere] * 6,
        out_specs=[anywhere] * 5,
        scratch_shapes=[
            *(pltpu.VMEM(x.shape, bf16) for x in (resp_q, prompt_k, prompt_v, resp_k, resp_v, resp_grad)),
            *(pltpu.VMEM(x.shape, f32) for x in outs),
            pltpu.VMEM((2 * heads, ROWS, HD), bf16),
            pltpu.VMEM((2 * heads, ROWS, HD), bf16),
            stat,
            stat,
            stat,
            pltpu.VMEM((blocks, 8, ROWS), f32),
            pltpu.VMEM((blocks, CHUNK, ROWS), f32),
            pltpu.VMEM((blocks, CHUNK, ROWS), f32),
            pltpu.VMEM((2 * heads, HD, ROWS), f32),
            pltpu.VMEM((heads, HD, ROWS), bf16),
            pltpu.VMEM((heads, HD, ROWS), bf16),
            pltpu.VMEM((2, 3, 8, ROWS), f32),
            pltpu.VMEM((2, 3, 8, ROWS), f32),
            pltpu.VMEM((ROUNDS,) + piece, bf16),
            pltpu.VMEM((2 * ROUNDS, 2) + piece, bf16),
            pltpu.VMEM((2 * ROUNDS, 2) + piece, f32),
            pltpu.VMEM((ROUNDS, 3) + piece, bf16),
            pltpu.VMEM((ROUNDS, 3) + piece, bf16),
            pltpu.VMEM((ROUNDS,) + piece, bf16),
            pltpu.VMEM((ROUNDS,) + piece, bf16),
            pltpu.SemaphoreType.DMA((11,)),
            *sems(2, heads),
            *sems(2),
            *sems(heads),
            *sems(ROUNDS, 4, 2),
            *sems(ROUNDS, 3),
            *sems(ROUNDS, 2),
        ],
        compiler_params=pltpu.CompilerParams(
            vmem_limit_bytes=61 * 1024 * 1024, collective_id=0, has_side_effects=True
        ),
        cost_estimate=pl.CostEstimate(flops=flops, bytes_accessed=3 << 20, transcendentals=0),
    )(lengths, resp_q, prompt_k, prompt_v, resp_k, resp_v, resp_grad)
    return pl.pallas_call(
        copy_kernel,
        out_shape=outs,
        in_specs=[anywhere] * 5,
        out_specs=[anywhere] * 5,
        scratch_shapes=[pltpu.VMEM(x.shape, f32) for x in outs] + [pltpu.SemaphoreType.DMA((2, 5))],
        compiler_params=pltpu.CompilerParams(vmem_limit_bytes=61 * 1024 * 1024),
    )(*results)


def solution(mesh):
    rows = P(("dp", "resp", "tensor"), None)
    both = P(("dp", "resp"), "tensor")
    return jax.shard_map(
        local,
        mesh=mesh,
        in_specs=(rows, rows, both, both, both, both, P(("dp", "resp"))),
        out_specs=(both, both, both, rows, rows),
        check_vma=False,
    )
```

```python
import jax
import jax.numpy as jnp
from jax import lax
from jax.experimental import pallas as pl
from jax.experimental.pallas import tpu as pltpu
from jax.sharding import PartitionSpec as P

HD = 128
SCALE = HD**-0.5
LOG2E = 1.4426950408889634
NEG = -1e30
ROWS = 256
CHUNK = 256

CONTRACT_LAST = (((1,), (1,)), ((), ()))
PLAIN = (((1,), (0,)), ((), ()))


def dot(a, b, dims):
    return lax.dot_general(a, b, dims, preferred_element_type=jnp.float32)


MESH = pl.DeviceIdType.MESH
QUARTER = 128
ROUNDS = 4
PIECES = 4
TURN = (0, 1, 3, 2)
SPREAD, AHEAD, BEHIND, ACROSS = range(4)

FIRST = ("b0o", "c0o", "b0t", "c0t", "c1o", "c1t", "b1o", "b1t", "b2o", "b2t", "b3t", "d0t", "b3o", "d1t", "d0o", "d1o")
SECOND = ("d1o", "d0o", "d1t", "d0t", "b3o", "b3t", "b2o", "b2t", "b1o", "b1t", "c1t", "c1o", "c0t", "c0o", "b0t", "b0o")
BASE = {"b": 0, "c": 4, "d": 6}


def code(name):
    return (BASE[name[0]] + int(name[1])) * 2 + (name[2] == "t")


def place(letter, n):
    return BASE[letter] + n // 2, n % 2


def pick(step, order):
    chosen = code(order[0])
    for at, name in enumerate(order[1:], 1):
        chosen = jnp.where(step == at, code(name), chosen)
    return chosen // 2, chosen % 2


def attend(base, group, count, keys, vals, causal, qs, lives, peak, denom, weighted, peaks, exps, gprobs):
    for h in range(count):
        at, g = base + h, group + h
        scores = dot(keys, qs[g], CONTRACT_LAST) * (SCALE * LOG2E)
        if causal is not None:
            scores = jnp.where(causal, scores, NEG)
        gprob = dot(vals, lives[g], CONTRACT_LAST)
        scores = scores.reshape(CHUNK // 8, 8, ROWS)
        old = peak[g]
        new = jnp.maximum(old, jnp.max(scores, axis=0))
        raw = jnp.exp2(scores - new[None])
        shrink = jnp.exp2(old - new)
        peak[g] = new
        denom[g] = denom[g] * shrink + jnp.sum(raw, axis=0)
        weighted[g] = weighted[g] * shrink + jnp.sum(raw * gprob.reshape(raw.shape), axis=0)
        peaks[at] = new
        exps[at] = raw.reshape(CHUNK, ROWS)
        gprobs[at] = gprob


def join_sums(group, count, peak, denom, weighted, out):
    for h in range(count):
        top = jnp.max(peak[group + h], axis=0, keepdims=True)
        share = jnp.exp2(peak[group + h] - top)
        out[0, h : h + 1] = top
        out[1, h : h + 1] = jnp.sum(denom[group + h] * share, axis=0, keepdims=True)
        out[2, h : h + 1] = jnp.sum(weighted[group + h] * share, axis=0, keepdims=True)


def finish_stats(group, count, one, two, peak, weighted):
    for h in range(count):
        row = slice(h, h + 1)
        top = jnp.maximum(one[0, row], two[0, row])
        share_one, share_two = jnp.exp2(one[0, row] - top), jnp.exp2(two[0, row] - top)
        total = one[1, row] * share_one + two[1, row] * share_two
        mean = (one[2, row] * share_one + two[2, row] * share_two) / total
        peak[group + h] = jnp.broadcast_to(top + jnp.log2(total), (8, ROWS))
        weighted[group + h] = jnp.broadcast_to(mean, (8, ROWS))


def grads(base, group, count, keys, qs, lives, peak, weighted, peaks, exps, gprobs, dq):
    keys_t = keys.T
    probs, dscores = [], []
    for h in range(count):
        at, g = base + h, group + h
        factor = jnp.exp2(peaks[at] - peak[g])
        prob = exps[at].reshape(CHUNK // 8, 8, ROWS) * factor[None]
        dscore = prob * (gprobs[at].reshape(CHUNK // 8, 8, ROWS) - weighted[g][None])
        probs.append(prob.reshape(CHUNK, ROWS).astype(jnp.bfloat16))
        dscore = dscore.reshape(CHUNK, ROWS).astype(jnp.bfloat16)
        dscores.append(dscore)
        dq[g] += dot(keys_t, dscore, PLAIN)
    rows = pl.ds(group, count)
    grad_v = dot(jnp.concatenate(probs, axis=1), lives[rows].reshape(count * ROWS, HD), PLAIN)
    grad_k = dot(jnp.concatenate(dscores, axis=1), qs[rows].reshape(count * ROWS, HD), PLAIN)
    return grad_k, grad_v


def kernel(lengths, q_hbm, pk_hbm, pv_hbm, rk_hbm, rv_hbm, g_hbm, dq_hbm, drk_hbm, drv_hbm, dpk_hbm, dpv_hbm,
           q, pk, pv, rk, rv, g, dq_out, drk, drv, dpk, dpv,
           qs, lives, peak, denom, weighted, peaks, exps, gprobs, dq, dq_send, dq_in,
           stat_out, stat_in, packed, kv, own, ring_out, ring_in, z_out, z_in,
           local_s, swap_s, swap_r, stat_s, stat_r, dq_s, dq_r, get_s, get_r, ring_s, ring_r, z_s, z_r):
    heads = q.shape[1] // HD
    resp, tensor = lax.axis_index("resp"), lax.axis_index("tensor")
    chip, core = resp // 2, resp % 2
    up = {"resp": (chip + 1) % 4 * 2 + core}
    down = {"resp": (chip + 3) % 4 * 2 + core}
    across = {"resp": (chip + 2) % 4 * 2 + core}
    twin = {"resp": chip * 2 + 1 - core}

    def along(turn):
        return {"tensor": (tensor + turn) % 4}

    def columns(index):
        return pl.ds(pl.multiple_of(index * HD, HD), HD)

    barrier = pltpu.get_barrier_semaphore()
    for other in (up, down, across, twin, along(1), along(2), along(3)):
        pl.semaphore_signal(barrier, inc=1, device_id=other, device_id_type=MESH)
    moves_in = [
        pltpu.make_async_copy(src, dst, local_s.at[i])
        for i, (src, dst) in enumerate(
            ((pk_hbm, pk), (pv_hbm, pv), (q_hbm, q), (g_hbm, g), (rk_hbm, rk), (rv_hbm, rv))
        )
    ]
    for move in moves_in:
        move.start()

    def send(src, dst, sems, at, to):
        return pltpu.make_async_remote_copy(
            src_ref=src, dst_ref=dst, send_sem=sems[0].at[at], recv_sem=sems[1].at[at],
            device_id=to, device_id_type=MESH,
        )

    def get(n, kind):
        mine, far = kv.at[*place("c", n)], kv.at[*place("d", n)]
        if kind == SPREAD:
            ends = [(packed.at[n, part], mine.at[part], along(TURN[n])) for part in range(2)]
        elif kind == AHEAD:
            ends = [(mine.at[part], kv.at[n, 0, part], up) for part in range(2)]
        elif kind == BEHIND:
            ends = [(mine.at[part], kv.at[n, 1, part], down) for part in range(2)]
        else:
            ends = [(mine.at[part], far.at[part], across) for part in range(2)]
        return [send(src, dst, (get_s, get_r), (n, kind, i), to) for i, (src, dst, to) in enumerate(ends)]

    def start(copies):
        for copy in copies:
            copy.start()

    def received(copies):
        for copy in copies:
            copy.wait_recv()

    def begin(n):
        if n:
            received(get(n, SPREAD))
        for kind in (AHEAD, BEHIND, ACROSS):
            start(get(n, kind))

    def near_received(n):
        received(get(n, AHEAD) + get(n, BEHIND))

    def swap():
        return [
            send(ref.at[h], ref.at[heads + h], (swap_s, swap_r), (i, h), twin)
            for h in range(heads)
            for i, ref in enumerate((qs, lives))
        ]

    positions = lax.broadcasted_iota(jnp.int32, (ROWS, HD), 0)
    alive = positions < lengths[0]
    moves_in[0].wait()
    moves_in[1].wait()
    kv[4, 0, 0] = pk[:, columns(tensor)]
    kv[4, 0, 1] = pv[:, columns(tensor)]
    for n in range(1, ROUNDS):
        cols = columns((tensor + TURN[n]) % 4)
        packed[n, 0] = pk[:, cols]
        packed[n, 1] = pv[:, cols]
    pl.semaphore_wait(barrier, 7)
    begin(0)
    for n in range(1, ROUNDS):
        start(get(n, SPREAD))
    moves_in[2].wait()
    moves_in[3].wait()
    for h in range(heads):
        cols = slice(h * HD, (h + 1) * HD)
        qs[h] = q[:, cols]
        lives[h] = jnp.where(alive, g[:, cols], jnp.zeros((), jnp.bfloat16))
    start(swap())
    moves_in[4].wait()
    moves_in[5].wait()
    peak[...] = jnp.full(peak.shape, NEG, jnp.float32)
    denom[...] = jnp.zeros(denom.shape, jnp.float32)
    weighted[...] = jnp.zeros(weighted.shape, jnp.float32)
    dq[...] = jnp.zeros(dq.shape, jnp.float32)
    own[...] = jnp.zeros(own.shape, jnp.float32)
    causal = lax.broadcasted_iota(jnp.int32, (CHUNK, ROWS), 0) <= lax.broadcasted_iota(jnp.int32, (CHUNK, ROWS), 1)
    sums = (qs, lives, peak, denom, weighted, peaks, exps, gprobs)
    steps = len(FIRST)
    attend(steps * heads, 0, heads, rk[...], rv[...], causal, *sums)

    def far_received(*rounds):
        for n in rounds:
            received(get(n, ACROSS))

    before = {
        "b0o": (lambda: near_received(0),),
        "b0t": (lambda: received(swap()),),
        "b1o": (lambda: near_received(1),),
        "b2o": (lambda: near_received(2),),
        "b3t": (lambda: near_received(3),),
        "d0t": (lambda: far_received(0, 1),),
        "d1t": (lambda: far_received(2, 3),),
    }
    after = {
        "b0o": (lambda: begin(1), lambda: begin(2)),
        "c0t": (lambda: begin(3),),
    }

    def serve(step, order, table):
        for name, jobs in table.items():
            @pl.when(step == order.index(name))
            def _():
                for job in jobs:
                    job()

    def first(step, carry):
        chunk, half = pick(step, FIRST)
        serve(step, FIRST, before)
        keys = kv[chunk, :, 0].reshape(CHUNK, HD)
        vals = kv[chunk, :, 1].reshape(CHUNK, HD)
        attend((chunk * 2 + half) * heads, half * heads, heads, keys, vals, None, *sums)
        serve(step, FIRST, after)

        @pl.when(step == FIRST.index("d1t"))
        def _():
            join_sums(heads, heads, peak, denom, weighted, stat_out.at[1])
            tell(1).start()

        return carry

    def tell(half):
        return send(stat_out.at[half], stat_in.at[1 - half], (stat_s, stat_r), 1 - half, twin)

    lax.fori_loop(0, steps, first, 0)
    join_sums(0, heads, peak, denom, weighted, stat_out.at[0])
    tell(0).start()
    tell(1).wait_recv()
    finish_stats(0, heads, stat_out.at[0], stat_in.at[0], peak, weighted)

    def to_ring(n, way):
        to = (up, down, across)[way]
        return [send(ring_out.at[n, way], ring_in.at[n, way], (ring_s, ring_r), (n, way), to)]

    def to_holder(n):
        return [
            send(z_out.at[n, part], z_in.at[n, part], (z_s, z_r), (n, part), along(4 - TURN[n])) for part in range(2)
        ]

    def to_owner(h):
        return send(dq_send.at[h], dq_in.at[h], (dq_s, dq_r), h, twin)

    def wide(ref):
        return ref.astype(jnp.float32)

    def send_far(n):
        ring_out[n, 2] = own[place("d", n)].astype(jnp.bfloat16)
        start(to_ring(n, 2))

    def send_near(n):
        for way in range(2):
            ring_out[n, way] = own[n, 1 - way].astype(jnp.bfloat16)
            start(to_ring(n, way))

    def total(n):
        for way in range(3):
            received(to_ring(n, way))
        return own[place("c", n)] + wide(ring_in[n, 0]) + wide(ring_in[n, 1]) + wide(ring_in[n, 2])

    def hand_over(n):
        z_out[n] = total(n).astype(jnp.bfloat16)
        start(to_holder(n))

    def learn():
        tell(0).wait_recv()
        finish_stats(heads, heads, stat_out.at[1], stat_in.at[1], peak, weighted)

    def return_queries():
        for h in range(heads):
            dq_send[h] = dq[heads + h].astype(jnp.bfloat16)
            to_owner(h).start()

    services = {
        "d0o": (learn,),
        "d1t": (lambda: send_far(3), lambda: send_far(2)),
        "d0t": (lambda: send_far(1), lambda: send_far(0)),
        "b3t": (lambda: send_near(3),),
        "b2t": (lambda: send_near(2),),
        "b1t": (lambda: send_near(1),),
        "c1o": (lambda: hand_over(3), lambda: hand_over(2)),
        "c0o": (lambda: hand_over(1),),
        "b0t": (return_queries,),
        "b0o": (lambda: send_near(0),),
    }

    def second(step, carry):
        chunk, half = pick(step, SECOND)
        keys = kv[chunk, :, 0].reshape(CHUNK, HD)
        grad_k, grad_v = grads(
            (chunk * 2 + half) * heads, half * heads, heads, keys, qs, lives, peak, weighted, peaks, exps, gprobs, dq
        )
        grad_k = (grad_k * SCALE).reshape(2, QUARTER, HD)
        grad_v = grad_v.reshape(2, QUARTER, HD)
        own[chunk, :, 0] += grad_k
        own[chunk, :, 1] += grad_v
        serve(step, SECOND, services)
        return carry

    lax.fori_loop(0, steps, second, 0)
    grad_k, grad_v = grads(steps * heads, 0, heads, rk[...], qs, lives, peak, weighted, peaks, exps, gprobs, dq)
    drk[...] = grad_k * SCALE
    drv[...] = grad_v
    moves_out = [
        pltpu.make_async_copy(src, dst, local_s.at[6 + i])
        for i, (src, dst) in enumerate((
            (drk, drk_hbm), (drv, drv_hbm), (dq_out, dq_hbm)
        ))
    ]
    moves_out[0].start()
    moves_out[1].start()
    for h in range(heads):
        to_owner(h).wait_recv()
        dq_out[:, h * HD : (h + 1) * HD] = (dq[h] + wide(dq_in[h])).T * SCALE
    moves_out[2].start()
    sent = swap() + [tell(0), tell(1)]
    for n in range(ROUNDS):
        for kind in range(SPREAD if n else AHEAD, ACROSS + 1):
            sent += get(n, kind)
    for copy in sent:
        copy.wait_send()

    def prompt_out(n, values):
        cols = columns((tensor + TURN[n]) % 4)
        for part, (here, there) in enumerate(((dpk, dpk_hbm), (dpv, dpv_hbm))):
            here[:, cols] = values[part]
            moves_out.append(pltpu.make_async_copy(here.at[:, cols], there.at[:, cols], local_s.at[9 + 2 * n + part]))
            moves_out[-1].start()

    prompt_out(0, total(0))
    for n in reversed(range(1, ROUNDS)):
        received(to_holder(n))
        prompt_out(n, wide(z_in[n]))
    sent = [to_owner(h) for h in range(heads)]
    for n in range(ROUNDS):
        sent += to_ring(n, 0) + to_ring(n, 1) + to_ring(n, 2)
        if n:
            sent += to_holder(n)
    for copy in sent:
        copy.wait_send()
    for move in moves_out:
        move.wait()


def copy_kernel(*refs):
    sems = refs[-1]
    count = (len(refs) - 1) // 3
    here, away = [], []
    for src, dst, room in zip(refs[:count], refs[count : 2 * count], refs[2 * count : 3 * count]):
        step = src.shape[0] // PIECES
        for i in range(PIECES):
            rows, at = pl.ds(i * step, step), len(here)
            here.append(pltpu.make_async_copy(src.at[rows], room.at[rows], sems.at[0, at]))
            away.append(pltpu.make_async_copy(room.at[rows], dst.at[rows], sems.at[1, at]))
    for move in here:
        move.start()
    for move_in, move_out in zip(here, away):
        move_in.wait()
        move_out.start()
    for move in away:
        move.wait()


def local(prompt_k, prompt_v, resp_q, resp_k, resp_v, resp_grad, lengths):
    heads = resp_q.shape[1] // HD
    blocks = (len(FIRST) + 1) * heads
    anywhere = pl.BlockSpec(memory_space=pl.ANY)
    f32, bf16 = jnp.float32, jnp.bfloat16
    stat = pltpu.VMEM((2 * heads, 8, ROWS), f32)
    piece = (2, QUARTER, HD)

    def sems(*shape):
        return [pltpu.SemaphoreType.DMA(shape)] * 2

    outs = tuple(jax.ShapeDtypeStruct(x.shape, f32) for x in (resp_q, resp_k, resp_v, prompt_k, prompt_v))
    flops = 10 * blocks * CHUNK * ROWS * HD
    results = pl.pallas_call(
        kernel,
        out_shape=outs,
        in_specs=[pl.BlockSpec(memory_space=pltpu.SMEM)] + [anywhere] * 6,
        out_specs=[anywhere] * 5,
        scratch_shapes=[
            *(pltpu.VMEM(x.shape, bf16) for x in (resp_q, prompt_k, prompt_v, resp_k, resp_v, resp_grad)),
            *(pltpu.VMEM(x.shape, f32) for x in outs),
            pltpu.VMEM((2 * heads, ROWS, HD), bf16),
            pltpu.VMEM((2 * heads, ROWS, HD), bf16),
            stat,
            stat,
            stat,
            pltpu.VMEM((blocks, 8, ROWS), f32),
            pltpu.VMEM((blocks, CHUNK, ROWS), f32),
            pltpu.VMEM((blocks, CHUNK, ROWS), f32),
            pltpu.VMEM((2 * heads, HD, ROWS), f32),
            pltpu.VMEM((heads, HD, ROWS), bf16),
            pltpu.VMEM((heads, HD, ROWS), bf16),
            pltpu.VMEM((2, 3, 8, ROWS), f32),
            pltpu.VMEM((2, 3, 8, ROWS), f32),
            pltpu.VMEM((ROUNDS,) + piece, bf16),
            pltpu.VMEM((2 * ROUNDS, 2) + piece, bf16),
            pltpu.VMEM((2 * ROUNDS, 2) + piece, f32),
            pltpu.VMEM((ROUNDS, 3) + piece, bf16),
            pltpu.VMEM((ROUNDS, 3) + piece, bf16),
            pltpu.VMEM((ROUNDS,) + piece, bf16),
            pltpu.VMEM((ROUNDS,) + piece, bf16),
            pltpu.SemaphoreType.DMA((17,)),
            *sems(2, heads),
            *sems(2),
            *sems(heads),
            *sems(ROUNDS, 4, 2),
            *sems(ROUNDS, 3),
            *sems(ROUNDS, 2),
        ],
        compiler_params=pltpu.CompilerParams(
            vmem_limit_bytes=61 * 1024 * 1024, collective_id=0, has_side_effects=True
        ),
        cost_estimate=pl.CostEstimate(flops=flops, bytes_accessed=3 << 20, transcendentals=0),
    )(lengths, resp_q, prompt_k, prompt_v, resp_k, resp_v, resp_grad)
    return pl.pallas_call(
        copy_kernel,
        out_shape=outs,
        in_specs=[anywhere] * 5,
        out_specs=[anywhere] * 5,
        scratch_shapes=[pltpu.VMEM(x.shape, f32) for x in outs] + [pltpu.SemaphoreType.DMA((2, 5 * PIECES))],
        compiler_params=pltpu.CompilerParams(vmem_limit_bytes=61 * 1024 * 1024),
    )(*results)


def solution(mesh):
    rows = P(("dp", "resp", "tensor"), None)
    both = P(("dp", "resp"), "tensor")
    return jax.shard_map(
        local,
        mesh=mesh,
        in_specs=(rows, rows, both, both, both, both, P(("dp", "resp"))),
        out_specs=(both, both, both, rows, rows),
        check_vma=False,
    )
```

```python
import jax
import jax.numpy as jnp
from jax import lax
from jax.experimental import pallas as pl
from jax.experimental.pallas import tpu as pltpu
from jax.sharding import PartitionSpec as P

HD = 128
SCALE = HD**-0.5
LOG2E = 1.4426950408889634
NEG = -1e30
ROWS = 256
CHUNK = 256

CONTRACT_LAST = (((1,), (1,)), ((), ()))
PLAIN = (((1,), (0,)), ((), ()))


def dot(a, b, dims):
    return lax.dot_general(a, b, dims, preferred_element_type=jnp.float32)


MESH = pl.DeviceIdType.MESH
QUARTER = 128
ROUNDS = 4
TURN = (0, 1, 3, 2)
SPREAD, AHEAD, BEHIND, ACROSS = range(4)

FIRST = ("b0o", "c0o", "b0t", "c0t", "c1o", "c1t", "b1o", "b1t", "b2o", "b2t", "b3t", "d0t", "b3o", "d1t", "d0o", "d1o")
SECOND = ("d1o", "d0o", "d1t", "d0t", "b3o", "b3t", "b2o", "b2t", "b1o", "b1t", "c1t", "c1o", "c0t", "c0o", "b0t", "b0o")
BASE = {"b": 0, "c": 4, "d": 6}


def code(name):
    return (BASE[name[0]] + int(name[1])) * 2 + (name[2] == "t")


def place(letter, n):
    return BASE[letter] + n // 2, n % 2


def pick(step, order):
    chosen = code(order[0])
    for at, name in enumerate(order[1:], 1):
        chosen = jnp.where(step == at, code(name), chosen)
    return chosen // 2, chosen % 2


def attend(base, group, count, keys, vals, causal, qs, lives, peak, denom, weighted, peaks, exps, gprobs):
    for h in range(count):
        at, g = base + h, group + h
        scores = dot(keys, qs[g], CONTRACT_LAST) * (SCALE * LOG2E)
        if causal is not None:
            scores = jnp.where(causal, scores, NEG)
        gprob = dot(vals, lives[g], CONTRACT_LAST)
        scores = scores.reshape(CHUNK // 8, 8, ROWS)
        old = peak[g]
        new = jnp.maximum(old, jnp.max(scores, axis=0))
        raw = jnp.exp2(scores - new[None])
        shrink = jnp.exp2(old - new)
        peak[g] = new
        denom[g] = denom[g] * shrink + jnp.sum(raw, axis=0)
        weighted[g] = weighted[g] * shrink + jnp.sum(raw * gprob.reshape(raw.shape), axis=0)
        peaks[at] = new
        exps[at] = raw.reshape(CHUNK, ROWS)
        gprobs[at] = gprob


def join_sums(group, count, peak, denom, weighted, out):
    for h in range(count):
        top = jnp.max(peak[group + h], axis=0, keepdims=True)
        share = jnp.exp2(peak[group + h] - top)
        out[0, h : h + 1] = top
        out[1, h : h + 1] = jnp.sum(denom[group + h] * share, axis=0, keepdims=True)
        out[2, h : h + 1] = jnp.sum(weighted[group + h] * share, axis=0, keepdims=True)


def finish_stats(group, count, one, two, peak, weighted):
    for h in range(count):
        row = slice(h, h + 1)
        top = jnp.maximum(one[0, row], two[0, row])
        share_one, share_two = jnp.exp2(one[0, row] - top), jnp.exp2(two[0, row] - top)
        total = one[1, row] * share_one + two[1, row] * share_two
        mean = (one[2, row] * share_one + two[2, row] * share_two) / total
        peak[group + h] = jnp.broadcast_to(top + jnp.log2(total), (8, ROWS))
        weighted[group + h] = jnp.broadcast_to(mean, (8, ROWS))


def grads(base, group, count, keys, qs, lives, peak, weighted, peaks, exps, gprobs, dq):
    keys_t = keys.T
    probs, dscores = [], []
    for h in range(count):
        at, g = base + h, group + h
        factor = jnp.exp2(peaks[at] - peak[g])
        prob = exps[at].reshape(CHUNK // 8, 8, ROWS) * factor[None]
        dscore = prob * (gprobs[at].reshape(CHUNK // 8, 8, ROWS) - weighted[g][None])
        probs.append(prob.reshape(CHUNK, ROWS).astype(jnp.bfloat16))
        dscore = dscore.reshape(CHUNK, ROWS).astype(jnp.bfloat16)
        dscores.append(dscore)
        dq[g] += dot(keys_t, dscore, PLAIN)
    rows = pl.ds(group, count)
    grad_v = dot(jnp.concatenate(probs, axis=1), lives[rows].reshape(count * ROWS, HD), PLAIN)
    grad_k = dot(jnp.concatenate(dscores, axis=1), qs[rows].reshape(count * ROWS, HD), PLAIN)
    return grad_k, grad_v


def kernel(lengths, q_hbm, pk_hbm, pv_hbm, rk_hbm, rv_hbm, g_hbm, dq_hbm, drk_hbm, drv_hbm, dpk_hbm, dpv_hbm,
           q, pk, pv, rk, rv, g, dq_out, drk, drv, dpk, dpv,
           qs, lives, peak, denom, weighted, peaks, exps, gprobs, dq, dq_send, dq_in,
           stat_out, stat_in, packed, kv, own, ring_out, ring_in, z_out, z_in,
           local_s, swap_s, swap_r, stat_s, stat_r, dq_s, dq_r, get_s, get_r, ring_s, ring_r, z_s, z_r):
    heads = q.shape[1] // HD
    resp, tensor = lax.axis_index("resp"), lax.axis_index("tensor")
    chip, core = resp // 2, resp % 2
    up = {"resp": (chip + 1) % 4 * 2 + core}
    down = {"resp": (chip + 3) % 4 * 2 + core}
    across = {"resp": (chip + 2) % 4 * 2 + core}
    twin = {"resp": chip * 2 + 1 - core}

    def along(turn):
        return {"tensor": (tensor + turn) % 4}

    def columns(index):
        return pl.ds(pl.multiple_of(index * HD, HD), HD)

    barrier = pltpu.get_barrier_semaphore()
    for other in (up, down, across, twin, along(1), along(2), along(3)):
        pl.semaphore_signal(barrier, inc=1, device_id=other, device_id_type=MESH)
    moves_in = [
        pltpu.make_async_copy(src, dst, local_s.at[i])
        for i, (src, dst) in enumerate(
            ((pk_hbm, pk), (pv_hbm, pv), (q_hbm, q), (g_hbm, g), (rk_hbm, rk), (rv_hbm, rv))
        )
    ]
    for move in moves_in:
        move.start()

    def send(src, dst, sems, at, to):
        return pltpu.make_async_remote_copy(
            src_ref=src, dst_ref=dst, send_sem=sems[0].at[at], recv_sem=sems[1].at[at],
            device_id=to, device_id_type=MESH,
        )

    def get(n, kind):
        mine, far = kv.at[*place("c", n)], kv.at[*place("d", n)]
        src, dst, to = {
            SPREAD: (packed.at[n], mine, along(TURN[n])),
            AHEAD: (mine, kv.at[n, 0], up),
            BEHIND: (mine, kv.at[n, 1], down),
            ACROSS: (mine, far, across),
        }[kind]
        return [send(src, dst, (get_s, get_r), (n, kind), to)]

    def start(copies):
        for copy in copies:
            copy.start()

    def received(copies):
        for copy in copies:
            copy.wait_recv()

    def begin(n):
        if n:
            received(get(n, SPREAD))
        for kind in (AHEAD, BEHIND, ACROSS):
            start(get(n, kind))

    def near_received(n):
        received(get(n, AHEAD) + get(n, BEHIND))

    def swap():
        here, there = pl.ds(0, heads), pl.ds(heads, heads)
        return [send(ref.at[here], ref.at[there], (swap_s, swap_r), i, twin) for i, ref in enumerate((qs, lives))]

    positions = lax.broadcasted_iota(jnp.int32, (ROWS, HD), 0)
    alive = positions < lengths[0]
    moves_in[0].wait()
    moves_in[1].wait()
    kv[4, 0, 0] = pk[:, columns(tensor)]
    kv[4, 0, 1] = pv[:, columns(tensor)]
    for n in range(1, ROUNDS):
        cols = columns((tensor + TURN[n]) % 4)
        packed[n, 0] = pk[:, cols]
        packed[n, 1] = pv[:, cols]
    pl.semaphore_wait(barrier, 7)
    begin(0)
    for n in range(1, ROUNDS):
        start(get(n, SPREAD))
    moves_in[2].wait()
    moves_in[3].wait()
    for h in range(heads):
        cols = slice(h * HD, (h + 1) * HD)
        qs[h] = q[:, cols]
        lives[h] = jnp.where(alive, g[:, cols], jnp.zeros((), jnp.bfloat16))
    start(swap())
    moves_in[4].wait()
    moves_in[5].wait()
    peak[...] = jnp.full(peak.shape, NEG, jnp.float32)
    denom[...] = jnp.zeros(denom.shape, jnp.float32)
    weighted[...] = jnp.zeros(weighted.shape, jnp.float32)
    dq[...] = jnp.zeros(dq.shape, jnp.float32)
    own[...] = jnp.zeros(own.shape, jnp.float32)
    causal = lax.broadcasted_iota(jnp.int32, (CHUNK, ROWS), 0) <= lax.broadcasted_iota(jnp.int32, (CHUNK, ROWS), 1)
    sums = (qs, lives, peak, denom, weighted, peaks, exps, gprobs)
    steps = len(FIRST)
    attend(steps * heads, 0, heads, rk[...], rv[...], causal, *sums)

    def far_received(*rounds):
        for n in rounds:
            received(get(n, ACROSS))

    before = {
        "b0o": (lambda: near_received(0),),
        "b0t": (lambda: received(swap()),),
        "b1o": (lambda: near_received(1),),
        "b2o": (lambda: near_received(2),),
        "b3t": (lambda: near_received(3),),
        "d0t": (lambda: far_received(0, 1),),
        "d1t": (lambda: far_received(2, 3),),
    }
    after = {
        "b0o": (lambda: begin(1), lambda: begin(2)),
        "c0t": (lambda: begin(3),),
    }

    def serve(step, order, table):
        for name, jobs in table.items():
            @pl.when(step == order.index(name))
            def _():
                for job in jobs:
                    job()

    def first(step, carry):
        chunk, half = pick(step, FIRST)
        serve(step, FIRST, before)
        keys = kv[chunk, :, 0].reshape(CHUNK, HD)
        vals = kv[chunk, :, 1].reshape(CHUNK, HD)
        attend((chunk * 2 + half) * heads, half * heads, heads, keys, vals, None, *sums)
        serve(step, FIRST, after)

        @pl.when(step == FIRST.index("d1t"))
        def _():
            join_sums(heads, heads, peak, denom, weighted, stat_out.at[1])
            tell(1).start()

        return carry

    def tell(half):
        return send(stat_out.at[half], stat_in.at[1 - half], (stat_s, stat_r), 1 - half, twin)

    lax.fori_loop(0, steps, first, 0)
    join_sums(0, heads, peak, denom, weighted, stat_out.at[0])
    tell(0).start()
    tell(1).wait_recv()
    finish_stats(0, heads, stat_out.at[0], stat_in.at[0], peak, weighted)

    def to_ring(n, way):
        to = (up, down, across)[way]
        return [send(ring_out.at[n, way], ring_in.at[n, way], (ring_s, ring_r), (n, way), to)]

    def to_holder(n):
        return [send(z_out.at[n], z_in.at[n], (z_s, z_r), n, along(4 - TURN[n]))]

    def to_owner():
        return send(dq_send, dq_in, (dq_s, dq_r), 0, twin)

    def wide(ref):
        return ref.astype(jnp.float32)

    def send_far(n):
        ring_out[n, 2] = own[place("d", n)].astype(jnp.bfloat16)
        start(to_ring(n, 2))

    def send_near(n):
        for way in range(2):
            ring_out[n, way] = own[n, 1 - way].astype(jnp.bfloat16)
            start(to_ring(n, way))

    def total(n):
        for way in range(3):
            received(to_ring(n, way))
        return own[place("c", n)] + wide(ring_in[n, 0]) + wide(ring_in[n, 1]) + wide(ring_in[n, 2])

    def hand_over(n):
        z_out[n] = total(n).astype(jnp.bfloat16)
        start(to_holder(n))

    def learn():
        tell(0).wait_recv()
        finish_stats(heads, heads, stat_out.at[1], stat_in.at[1], peak, weighted)

    def return_queries():
        for h in range(heads):
            dq_send[h] = dq[heads + h].astype(jnp.bfloat16)
        to_owner().start()

    services = {
        "d0o": (learn,),
        "d1t": (lambda: send_far(3), lambda: send_far(2)),
        "d0t": (lambda: send_far(1), lambda: send_far(0)),
        "b3t": (lambda: send_near(3),),
        "b2t": (lambda: send_near(2),),
        "b1t": (lambda: send_near(1),),
        "c1o": (lambda: hand_over(3), lambda: hand_over(2)),
        "c0o": (lambda: hand_over(1),),
        "b0t": (return_queries,),
        "b0o": (lambda: send_near(0),),
    }

    def second(step, carry):
        chunk, half = pick(step, SECOND)
        keys = kv[chunk, :, 0].reshape(CHUNK, HD)
        grad_k, grad_v = grads(
            (chunk * 2 + half) * heads, half * heads, heads, keys, qs, lives, peak, weighted, peaks, exps, gprobs, dq
        )
        grad_k = (grad_k * SCALE).reshape(2, QUARTER, HD)
        grad_v = grad_v.reshape(2, QUARTER, HD)
        own[chunk, :, 0] += grad_k
        own[chunk, :, 1] += grad_v
        serve(step, SECOND, services)
        return carry

    lax.fori_loop(0, steps, second, 0)
    grad_k, grad_v = grads(steps * heads, 0, heads, rk[...], qs, lives, peak, weighted, peaks, exps, gprobs, dq)
    drk[...] = grad_k * SCALE
    drv[...] = grad_v
    moves_out = [
        pltpu.make_async_copy(src, dst, local_s.at[6 + i])
        for i, (src, dst) in enumerate((
            (drk, drk_hbm), (drv, drv_hbm), (dq_out, dq_hbm), (dpk, dpk_hbm), (dpv, dpv_hbm)
        ))
    ]
    moves_out[0].start()
    moves_out[1].start()
    to_owner().wait_recv()
    for h in range(heads):
        dq_out[:, h * HD : (h + 1) * HD] = (dq[h] + wide(dq_in[h])).T * SCALE
    moves_out[2].start()
    sums_now = total(0)
    dpk[:, columns(tensor)] = sums_now[0]
    dpv[:, columns(tensor)] = sums_now[1]
    for n in reversed(range(1, ROUNDS)):
        received(to_holder(n))
        cols = columns((tensor + TURN[n]) % 4)
        dpk[:, cols] = wide(z_in[n, 0])
        dpv[:, cols] = wide(z_in[n, 1])
    moves_out[3].start()
    moves_out[4].start()
    sent = swap() + [tell(0), tell(1), to_owner()]
    for n in range(ROUNDS):
        for kind in range(SPREAD if n else AHEAD, ACROSS + 1):
            sent += get(n, kind)
        sent += to_ring(n, 0) + to_ring(n, 1) + to_ring(n, 2)
        if n:
            sent += to_holder(n)
    for copy in sent:
        copy.wait_send()
    for move in moves_out:
        move.wait()


def copy_kernel(*refs):
    sems = refs[-1]
    count = (len(refs) - 1) // 3
    ins, outs, rooms = refs[:count], refs[count : 2 * count], refs[2 * count : 3 * count]
    here = [pltpu.make_async_copy(ins[i], rooms[i], sems.at[0, i]) for i in range(count)]
    away = [pltpu.make_async_copy(rooms[i], outs[i], sems.at[1, i]) for i in range(count)]
    for move in here:
        move.start()
    for i in range(count):
        here[i].wait()
        away[i].start()
    for move in away:
        move.wait()


def local(prompt_k, prompt_v, resp_q, resp_k, resp_v, resp_grad, lengths):
    heads = resp_q.shape[1] // HD
    blocks = (len(FIRST) + 1) * heads
    anywhere = pl.BlockSpec(memory_space=pl.ANY)
    f32, bf16 = jnp.float32, jnp.bfloat16
    stat = pltpu.VMEM((2 * heads, 8, ROWS), f32)
    piece = (2, QUARTER, HD)

    def sems(*shape):
        return [pltpu.SemaphoreType.DMA(shape)] * 2

    outs = tuple(jax.ShapeDtypeStruct(x.shape, f32) for x in (resp_q, resp_k, resp_v, prompt_k, prompt_v))
    flops = 10 * blocks * CHUNK * ROWS * HD
    results = pl.pallas_call(
        kernel,
        out_shape=outs,
        in_specs=[pl.BlockSpec(memory_space=pltpu.SMEM)] + [anywhere] * 6,
        out_specs=[anywhere] * 5,
        scratch_shapes=[
            *(pltpu.VMEM(x.shape, bf16) for x in (resp_q, prompt_k, prompt_v, resp_k, resp_v, resp_grad)),
            *(pltpu.VMEM(x.shape, f32) for x in outs),
            pltpu.VMEM((2 * heads, ROWS, HD), bf16),
            pltpu.VMEM((2 * heads, ROWS, HD), bf16),
            stat,
            stat,
            stat,
            pltpu.VMEM((blocks, 8, ROWS), f32),
            pltpu.VMEM((blocks, CHUNK, ROWS), f32),
            pltpu.VMEM((blocks, CHUNK, ROWS), f32),
            pltpu.VMEM((2 * heads, HD, ROWS), f32),
            pltpu.VMEM((heads, HD, ROWS), bf16),
            pltpu.VMEM((heads, HD, ROWS), bf16),
            pltpu.VMEM((2, 3, 8, ROWS), f32),
            pltpu.VMEM((2, 3, 8, ROWS), f32),
            pltpu.VMEM((ROUNDS,) + piece, bf16),
            pltpu.VMEM((2 * ROUNDS, 2) + piece, bf16),
            pltpu.VMEM((2 * ROUNDS, 2) + piece, f32),
            pltpu.VMEM((ROUNDS, 3) + piece, bf16),
            pltpu.VMEM((ROUNDS, 3) + piece, bf16),
            pltpu.VMEM((ROUNDS,) + piece, bf16),
            pltpu.VMEM((ROUNDS,) + piece, bf16),
            pltpu.SemaphoreType.DMA((11,)),
            *sems(2),
            *sems(2),
            *sems(1),
            *sems(ROUNDS, 4),
            *sems(ROUNDS, 3),
            *sems(ROUNDS),
        ],
        compiler_params=pltpu.CompilerParams(
            vmem_limit_bytes=61 * 1024 * 1024, collective_id=0, has_side_effects=True
        ),
        cost_estimate=pl.CostEstimate(flops=flops, bytes_accessed=3 << 20, transcendentals=0),
    )(lengths, resp_q, prompt_k, prompt_v, resp_k, resp_v, resp_grad)
    return pl.pallas_call(
        copy_kernel,
        out_shape=outs,
        in_specs=[anywhere] * 5,
        out_specs=[anywhere] * 5,
        scratch_shapes=[pltpu.VMEM(x.shape, f32) for x in outs] + [pltpu.SemaphoreType.DMA((2, 5))],
        compiler_params=pltpu.CompilerParams(vmem_limit_bytes=61 * 1024 * 1024),
    )(*results)


def solution(mesh):
    rows = P(("dp", "resp", "tensor"), None)
    both = P(("dp", "resp"), "tensor")
    return jax.shard_map(
        local,
        mesh=mesh,
        in_specs=(rows, rows, both, both, both, both, P(("dp", "resp"))),
        out_specs=(both, both, both, rows, rows),
        check_vma=False,
    )
```

```python
import jax
import jax.numpy as jnp
from jax import lax
from jax.experimental import pallas as pl
from jax.experimental.pallas import tpu as pltpu
from jax.sharding import PartitionSpec as P

HD = 128
SCALE = HD**-0.5
LOG2E = 1.4426950408889634
NEG = -1e30
ROWS = 256
CHUNK = 256

CONTRACT_LAST = (((1,), (1,)), ((), ()))
PLAIN = (((1,), (0,)), ((), ()))


def dot(a, b, dims):
    return lax.dot_general(a, b, dims, preferred_element_type=jnp.float32)


MESH = pl.DeviceIdType.MESH
QUARTER = 128
ROUNDS = 4
TURN = (0, 1, 3, 2)
SPREAD, AHEAD, BEHIND, ACROSS = range(4)

FIRST = ("b0o", "c0o", "b0t", "c0t", "c1o", "c1t", "b1o", "b1t", "b2o", "b2t", "b3t", "d0t", "d1t", "b3o", "d0o", "d1o")
SECOND = ("d1o", "d0o", "b3o", "d1t", "d0t", "b3t", "b2o", "b2t", "b1o", "b1t", "c1t", "c1o", "c0t", "c0o", "b0t", "b0o")
BASE = {"b": 0, "c": 4, "d": 6}


def code(name):
    return (BASE[name[0]] + int(name[1])) * 2 + (name[2] == "t")


def place(letter, n):
    return BASE[letter] + n // 2, n % 2


def pick(step, order):
    chosen = code(order[0])
    for at, name in enumerate(order[1:], 1):
        chosen = jnp.where(step == at, code(name), chosen)
    return chosen // 2, chosen % 2


def attend(base, group, count, keys, vals, causal, qs, lives, peak, denom, weighted, peaks, exps, gprobs):
    for h in range(count):
        at, g = base + h, group + h
        scores = dot(keys, qs[g], CONTRACT_LAST) * (SCALE * LOG2E)
        if causal is not None:
            scores = jnp.where(causal, scores, NEG)
        gprob = dot(vals, lives[g], CONTRACT_LAST)
        scores = scores.reshape(CHUNK // 8, 8, ROWS)
        old = peak[g]
        new = jnp.maximum(old, jnp.max(scores, axis=0))
        raw = jnp.exp2(scores - new[None])
        shrink = jnp.exp2(old - new)
        peak[g] = new
        denom[g] = denom[g] * shrink + jnp.sum(raw, axis=0)
        weighted[g] = weighted[g] * shrink + jnp.sum(raw * gprob.reshape(raw.shape), axis=0)
        peaks[at] = new
        exps[at] = raw.reshape(CHUNK, ROWS)
        gprobs[at] = gprob


def join_sums(group, count, peak, denom, weighted, out):
    for h in range(count):
        top = jnp.max(peak[group + h], axis=0, keepdims=True)
        share = jnp.exp2(peak[group + h] - top)
        out[0, h : h + 1] = top
        out[1, h : h + 1] = jnp.sum(denom[group + h] * share, axis=0, keepdims=True)
        out[2, h : h + 1] = jnp.sum(weighted[group + h] * share, axis=0, keepdims=True)


def finish_stats(group, count, one, two, peak, weighted):
    for h in range(count):
        row = slice(h, h + 1)
        top = jnp.maximum(one[0, row], two[0, row])
        share_one, share_two = jnp.exp2(one[0, row] - top), jnp.exp2(two[0, row] - top)
        total = one[1, row] * share_one + two[1, row] * share_two
        mean = (one[2, row] * share_one + two[2, row] * share_two) / total
        peak[group + h] = jnp.broadcast_to(top + jnp.log2(total), (8, ROWS))
        weighted[group + h] = jnp.broadcast_to(mean, (8, ROWS))


def grads(base, group, count, keys, qs, lives, peak, weighted, peaks, exps, gprobs, dq):
    keys_t = keys.T
    probs, dscores = [], []
    for h in range(count):
        at, g = base + h, group + h
        factor = jnp.exp2(peaks[at] - peak[g])
        prob = exps[at].reshape(CHUNK // 8, 8, ROWS) * factor[None]
        dscore = prob * (gprobs[at].reshape(CHUNK // 8, 8, ROWS) - weighted[g][None])
        probs.append(prob.reshape(CHUNK, ROWS).astype(jnp.bfloat16))
        dscore = dscore.reshape(CHUNK, ROWS).astype(jnp.bfloat16)
        dscores.append(dscore)
        dq[g] += dot(keys_t, dscore, PLAIN)
    rows = pl.ds(group, count)
    grad_v = dot(jnp.concatenate(probs, axis=1), lives[rows].reshape(count * ROWS, HD), PLAIN)
    grad_k = dot(jnp.concatenate(dscores, axis=1), qs[rows].reshape(count * ROWS, HD), PLAIN)
    return grad_k, grad_v


def kernel(lengths, q_hbm, pk_hbm, pv_hbm, rk_hbm, rv_hbm, g_hbm, dq_hbm, drk_hbm, drv_hbm, dpk_hbm, dpv_hbm,
           q, pk, pv, rk, rv, g, dq_out, drk, drv, dpk, dpv,
           qs, lives, peak, denom, weighted, peaks, exps, gprobs, dq, dq_send, dq_in,
           stat_out, stat_in, packed, kv, own, ring_out, ring_in, z_out, z_in,
           local_s, swap_s, swap_r, stat_s, stat_r, dq_s, dq_r, get_s, get_r, ring_s, ring_r, z_s, z_r):
    heads = q.shape[1] // HD
    resp, tensor = lax.axis_index("resp"), lax.axis_index("tensor")
    chip, core = resp // 2, resp % 2
    up = {"resp": (chip + 1) % 4 * 2 + core}
    down = {"resp": (chip + 3) % 4 * 2 + core}
    across = {"resp": (chip + 2) % 4 * 2 + core}
    twin = {"resp": chip * 2 + 1 - core}

    def along(turn):
        return {"tensor": (tensor + turn) % 4}

    def columns(index):
        return pl.ds(pl.multiple_of(index * HD, HD), HD)

    barrier = pltpu.get_barrier_semaphore()
    for other in (up, down, across, twin, along(1), along(2), along(3)):
        pl.semaphore_signal(barrier, inc=1, device_id=other, device_id_type=MESH)
    moves_in = [
        pltpu.make_async_copy(src, dst, local_s.at[i])
        for i, (src, dst) in enumerate(
            ((pk_hbm, pk), (pv_hbm, pv), (q_hbm, q), (g_hbm, g), (rk_hbm, rk), (rv_hbm, rv))
        )
    ]
    for move in moves_in:
        move.start()

    def send(src, dst, sems, at, to):
        return pltpu.make_async_remote_copy(
            src_ref=src, dst_ref=dst, send_sem=sems[0].at[at], recv_sem=sems[1].at[at],
            device_id=to, device_id_type=MESH,
        )

    def get(n, kind):
        mine, far = kv.at[*place("c", n)], kv.at[*place("d", n)]
        src, dst, to = {
            SPREAD: (packed.at[n], mine, along(TURN[n])),
            AHEAD: (mine, kv.at[n, 0], up),
            BEHIND: (mine, kv.at[n, 1], down),
            ACROSS: (mine, far, across),
        }[kind]
        return [send(src, dst, (get_s, get_r), (n, kind), to)]

    def start(copies):
        for copy in copies:
            copy.start()

    def received(copies):
        for copy in copies:
            copy.wait_recv()

    def begin(n):
        if n:
            received(get(n, SPREAD))
        for kind in (AHEAD, BEHIND, ACROSS):
            start(get(n, kind))

    def near_received(n):
        received(get(n, AHEAD) + get(n, BEHIND))

    def swap():
        here, there = pl.ds(0, heads), pl.ds(heads, heads)
        return [send(ref.at[here], ref.at[there], (swap_s, swap_r), i, twin) for i, ref in enumerate((qs, lives))]

    positions = lax.broadcasted_iota(jnp.int32, (ROWS, HD), 0)
    alive = positions < lengths[0]
    moves_in[0].wait()
    moves_in[1].wait()
    kv[4, 0, 0] = pk[:, columns(tensor)]
    kv[4, 0, 1] = pv[:, columns(tensor)]
    for n in range(1, ROUNDS):
        cols = columns((tensor + TURN[n]) % 4)
        packed[n, 0] = pk[:, cols]
        packed[n, 1] = pv[:, cols]
    pl.semaphore_wait(barrier, 7)
    begin(0)
    for n in range(1, ROUNDS):
        start(get(n, SPREAD))
    moves_in[2].wait()
    moves_in[3].wait()
    for h in range(heads):
        cols = slice(h * HD, (h + 1) * HD)
        qs[h] = q[:, cols]
        lives[h] = jnp.where(alive, g[:, cols], jnp.zeros((), jnp.bfloat16))
    start(swap())
    moves_in[4].wait()
    moves_in[5].wait()
    peak[...] = jnp.full(peak.shape, NEG, jnp.float32)
    denom[...] = jnp.zeros(denom.shape, jnp.float32)
    weighted[...] = jnp.zeros(weighted.shape, jnp.float32)
    dq[...] = jnp.zeros(dq.shape, jnp.float32)
    own[...] = jnp.zeros(own.shape, jnp.float32)
    causal = lax.broadcasted_iota(jnp.int32, (CHUNK, ROWS), 0) <= lax.broadcasted_iota(jnp.int32, (CHUNK, ROWS), 1)
    sums = (qs, lives, peak, denom, weighted, peaks, exps, gprobs)
    steps = len(FIRST)
    attend(steps * heads, 0, heads, rk[...], rv[...], causal, *sums)

    def far_received(*rounds):
        for n in rounds:
            received(get(n, ACROSS))

    before = {
        "b0o": (lambda: near_received(0),),
        "b0t": (lambda: received(swap()),),
        "b1o": (lambda: near_received(1),),
        "b2o": (lambda: near_received(2),),
        "b3t": (lambda: near_received(3),),
        "d0t": (lambda: far_received(0, 1),),
        "d1t": (lambda: far_received(2, 3),),
    }
    after = {
        "b0o": (lambda: begin(1), lambda: begin(2)),
        "c0t": (lambda: begin(3),),
    }

    def serve(step, order, table):
        for name, jobs in table.items():
            @pl.when(step == order.index(name))
            def _():
                for job in jobs:
                    job()

    def first(step, carry):
        chunk, half = pick(step, FIRST)
        serve(step, FIRST, before)
        keys = kv[chunk, :, 0].reshape(CHUNK, HD)
        vals = kv[chunk, :, 1].reshape(CHUNK, HD)
        attend((chunk * 2 + half) * heads, half * heads, heads, keys, vals, None, *sums)
        serve(step, FIRST, after)

        @pl.when(step == FIRST.index("d1t"))
        def _():
            join_sums(heads, heads, peak, denom, weighted, stat_out.at[1])
            tell(1).start()

        return carry

    def tell(half):
        return send(stat_out.at[half], stat_in.at[1 - half], (stat_s, stat_r), 1 - half, twin)

    lax.fori_loop(0, steps, first, 0)
    join_sums(0, heads, peak, denom, weighted, stat_out.at[0])
    tell(0).start()
    tell(1).wait_recv()
    finish_stats(0, heads, stat_out.at[0], stat_in.at[0], peak, weighted)

    def to_ring(n, way):
        to = (up, down, across)[way]
        return [send(ring_out.at[n, way], ring_in.at[n, way], (ring_s, ring_r), (n, way), to)]

    def to_holder(n):
        return [send(z_out.at[n], z_in.at[n], (z_s, z_r), n, along(4 - TURN[n]))]

    def to_owner():
        return send(dq_send, dq_in, (dq_s, dq_r), 0, twin)

    def wide(ref):
        return ref.astype(jnp.float32)

    def send_far(n):
        ring_out[n, 2] = own[place("d", n)].astype(jnp.bfloat16)
        start(to_ring(n, 2))

    def send_near(n):
        for way in range(2):
            ring_out[n, way] = own[n, 1 - way].astype(jnp.bfloat16)
            start(to_ring(n, way))

    def total(n):
        for way in range(3):
            received(to_ring(n, way))
        return own[place("c", n)] + wide(ring_in[n, 0]) + wide(ring_in[n, 1]) + wide(ring_in[n, 2])

    def hand_over(n):
        z_out[n] = total(n).astype(jnp.bfloat16)
        start(to_holder(n))

    def learn():
        tell(0).wait_recv()
        finish_stats(heads, heads, stat_out.at[1], stat_in.at[1], peak, weighted)

    def return_queries():
        for h in range(heads):
            dq_send[h] = dq[heads + h].astype(jnp.bfloat16)
        to_owner().start()

    services = {
        "b3o": (learn,),
        "d1t": (lambda: send_far(3), lambda: send_far(2)),
        "d0t": (lambda: send_far(1), lambda: send_far(0)),
        "b3t": (lambda: send_near(3),),
        "b2t": (lambda: send_near(2),),
        "b1t": (lambda: send_near(1),),
        "c1o": (lambda: hand_over(3), lambda: hand_over(2)),
        "c0o": (lambda: hand_over(1),),
        "b0t": (return_queries,),
        "b0o": (lambda: send_near(0),),
    }

    def second(step, carry):
        chunk, half = pick(step, SECOND)
        keys = kv[chunk, :, 0].reshape(CHUNK, HD)
        grad_k, grad_v = grads(
            (chunk * 2 + half) * heads, half * heads, heads, keys, qs, lives, peak, weighted, peaks, exps, gprobs, dq
        )
        grad_k = (grad_k * SCALE).reshape(2, QUARTER, HD)
        grad_v = grad_v.reshape(2, QUARTER, HD)
        own[chunk, :, 0] += grad_k
        own[chunk, :, 1] += grad_v
        serve(step, SECOND, services)
        return carry

    lax.fori_loop(0, steps, second, 0)
    grad_k, grad_v = grads(steps * heads, 0, heads, rk[...], qs, lives, peak, weighted, peaks, exps, gprobs, dq)
    drk[...] = grad_k * SCALE
    drv[...] = grad_v
    moves_out = [
        pltpu.make_async_copy(src, dst, local_s.at[6 + i])
        for i, (src, dst) in enumerate((
            (drk, drk_hbm), (drv, drv_hbm), (dq_out, dq_hbm), (dpk, dpk_hbm), (dpv, dpv_hbm)
        ))
    ]
    moves_out[0].start()
    moves_out[1].start()
    to_owner().wait_recv()
    for h in range(heads):
        dq_out[:, h * HD : (h + 1) * HD] = (dq[h] + wide(dq_in[h])).T * SCALE
    moves_out[2].start()
    sums_now = total(0)
    dpk[:, columns(tensor)] = sums_now[0]
    dpv[:, columns(tensor)] = sums_now[1]
    for n in reversed(range(1, ROUNDS)):
        received(to_holder(n))
        cols = columns((tensor + TURN[n]) % 4)
        dpk[:, cols] = wide(z_in[n, 0])
        dpv[:, cols] = wide(z_in[n, 1])
    moves_out[3].start()
    moves_out[4].start()
    sent = swap() + [tell(0), tell(1), to_owner()]
    for n in range(ROUNDS):
        for kind in range(SPREAD if n else AHEAD, ACROSS + 1):
            sent += get(n, kind)
        sent += to_ring(n, 0) + to_ring(n, 1) + to_ring(n, 2)
        if n:
            sent += to_holder(n)
    for copy in sent:
        copy.wait_send()
    for move in moves_out:
        move.wait()


def copy_kernel(*refs):
    sems = refs[-1]
    count = (len(refs) - 1) // 3
    ins, outs, rooms = refs[:count], refs[count : 2 * count], refs[2 * count : 3 * count]
    here = [pltpu.make_async_copy(ins[i], rooms[i], sems.at[0, i]) for i in range(count)]
    away = [pltpu.make_async_copy(rooms[i], outs[i], sems.at[1, i]) for i in range(count)]
    for move in here:
        move.start()
    for i in range(count):
        here[i].wait()
        away[i].start()
    for move in away:
        move.wait()


def local(prompt_k, prompt_v, resp_q, resp_k, resp_v, resp_grad, lengths):
    heads = resp_q.shape[1] // HD
    blocks = (len(FIRST) + 1) * heads
    anywhere = pl.BlockSpec(memory_space=pl.ANY)
    f32, bf16 = jnp.float32, jnp.bfloat16
    stat = pltpu.VMEM((2 * heads, 8, ROWS), f32)
    piece = (2, QUARTER, HD)

    def sems(*shape):
        return [pltpu.SemaphoreType.DMA(shape)] * 2

    outs = tuple(jax.ShapeDtypeStruct(x.shape, f32) for x in (resp_q, resp_k, resp_v, prompt_k, prompt_v))
    flops = 10 * blocks * CHUNK * ROWS * HD
    results = pl.pallas_call(
        kernel,
        out_shape=outs,
        in_specs=[pl.BlockSpec(memory_space=pltpu.SMEM)] + [anywhere] * 6,
        out_specs=[anywhere] * 5,
        scratch_shapes=[
            *(pltpu.VMEM(x.shape, bf16) for x in (resp_q, prompt_k, prompt_v, resp_k, resp_v, resp_grad)),
            *(pltpu.VMEM(x.shape, f32) for x in outs),
            pltpu.VMEM((2 * heads, ROWS, HD), bf16),
            pltpu.VMEM((2 * heads, ROWS, HD), bf16),
            stat,
            stat,
            stat,
            pltpu.VMEM((blocks, 8, ROWS), f32),
            pltpu.VMEM((blocks, CHUNK, ROWS), f32),
            pltpu.VMEM((blocks, CHUNK, ROWS), f32),
            pltpu.VMEM((2 * heads, HD, ROWS), f32),
            pltpu.VMEM((heads, HD, ROWS), bf16),
            pltpu.VMEM((heads, HD, ROWS), bf16),
            pltpu.VMEM((2, 3, 8, ROWS), f32),
            pltpu.VMEM((2, 3, 8, ROWS), f32),
            pltpu.VMEM((ROUNDS,) + piece, bf16),
            pltpu.VMEM((2 * ROUNDS, 2) + piece, bf16),
            pltpu.VMEM((2 * ROUNDS, 2) + piece, f32),
            pltpu.VMEM((ROUNDS, 3) + piece, bf16),
            pltpu.VMEM((ROUNDS, 3) + piece, bf16),
            pltpu.VMEM((ROUNDS,) + piece, bf16),
            pltpu.VMEM((ROUNDS,) + piece, bf16),
            pltpu.SemaphoreType.DMA((11,)),
            *sems(2),
            *sems(2),
            *sems(1),
            *sems(ROUNDS, 4),
            *sems(ROUNDS, 3),
            *sems(ROUNDS),
        ],
        compiler_params=pltpu.CompilerParams(
            vmem_limit_bytes=61 * 1024 * 1024, collective_id=0, has_side_effects=True
        ),
        cost_estimate=pl.CostEstimate(flops=flops, bytes_accessed=3 << 20, transcendentals=0),
    )(lengths, resp_q, prompt_k, prompt_v, resp_k, resp_v, resp_grad)
    return pl.pallas_call(
        copy_kernel,
        out_shape=outs,
        in_specs=[anywhere] * 5,
        out_specs=[anywhere] * 5,
        scratch_shapes=[pltpu.VMEM(x.shape, f32) for x in outs] + [pltpu.SemaphoreType.DMA((2, 5))],
        compiler_params=pltpu.CompilerParams(vmem_limit_bytes=61 * 1024 * 1024),
    )(*results)


def solution(mesh):
    rows = P(("dp", "resp", "tensor"), None)
    both = P(("dp", "resp"), "tensor")
    return jax.shard_map(
        local,
        mesh=mesh,
        in_specs=(rows, rows, both, both, both, both, P(("dp", "resp"))),
        out_specs=(both, both, both, rows, rows),
        check_vma=False,
    )
```

```python
import jax
import jax.numpy as jnp
from jax import lax
from jax.experimental import pallas as pl
from jax.experimental.pallas import tpu as pltpu
from jax.sharding import PartitionSpec as P

HD = 128
SCALE = HD**-0.5
LOG2E = 1.4426950408889634
NEG = -1e30
ROWS = 256
CHUNK = 256

CONTRACT_LAST = (((1,), (1,)), ((), ()))
PLAIN = (((1,), (0,)), ((), ()))


def dot(a, b, dims):
    return lax.dot_general(a, b, dims, preferred_element_type=jnp.float32)


MESH = pl.DeviceIdType.MESH
QUARTER = 128
ROUNDS = 4
TURN = (0, 1, 3, 2)
SPREAD, AHEAD, BEHIND, ACROSS = range(4)

FIRST = ("b0o", "c0o", "b0t", "c0t", "c1o", "c1t", "b1o", "b1t", "b2t", "b3t", "d0t", "d1t", "b2o", "b3o", "d0o", "d1o")
SECOND = ("d1o", "d0o", "b3o", "d1t", "d0t", "b3t", "b2o", "b2t", "b1o", "b1t", "c1t", "c1o", "c0t", "c0o", "b0t", "b0o")
BASE = {"b": 0, "c": 4, "d": 6}


def code(name):
    return (BASE[name[0]] + int(name[1])) * 2 + (name[2] == "t")


def place(letter, n):
    return BASE[letter] + n // 2, n % 2


def pick(step, order):
    chosen = code(order[0])
    for at, name in enumerate(order[1:], 1):
        chosen = jnp.where(step == at, code(name), chosen)
    return chosen // 2, chosen % 2


def attend(base, group, count, keys, vals, causal, qs, lives, peak, denom, weighted, peaks, exps, gprobs):
    for h in range(count):
        at, g = base + h, group + h
        scores = dot(keys, qs[g], CONTRACT_LAST) * (SCALE * LOG2E)
        if causal is not None:
            scores = jnp.where(causal, scores, NEG)
        gprob = dot(vals, lives[g], CONTRACT_LAST)
        scores = scores.reshape(CHUNK // 8, 8, ROWS)
        old = peak[g]
        new = jnp.maximum(old, jnp.max(scores, axis=0))
        raw = jnp.exp2(scores - new[None])
        shrink = jnp.exp2(old - new)
        peak[g] = new
        denom[g] = denom[g] * shrink + jnp.sum(raw, axis=0)
        weighted[g] = weighted[g] * shrink + jnp.sum(raw * gprob.reshape(raw.shape), axis=0)
        peaks[at] = new
        exps[at] = raw.reshape(CHUNK, ROWS)
        gprobs[at] = gprob


def join_sums(group, count, peak, denom, weighted, out):
    for h in range(count):
        top = jnp.max(peak[group + h], axis=0, keepdims=True)
        share = jnp.exp2(peak[group + h] - top)
        out[0, h : h + 1] = top
        out[1, h : h + 1] = jnp.sum(denom[group + h] * share, axis=0, keepdims=True)
        out[2, h : h + 1] = jnp.sum(weighted[group + h] * share, axis=0, keepdims=True)


def finish_stats(group, count, one, two, peak, weighted):
    for h in range(count):
        row = slice(h, h + 1)
        top = jnp.maximum(one[0, row], two[0, row])
        share_one, share_two = jnp.exp2(one[0, row] - top), jnp.exp2(two[0, row] - top)
        total = one[1, row] * share_one + two[1, row] * share_two
        mean = (one[2, row] * share_one + two[2, row] * share_two) / total
        peak[group + h] = jnp.broadcast_to(top + jnp.log2(total), (8, ROWS))
        weighted[group + h] = jnp.broadcast_to(mean, (8, ROWS))


def grads(base, group, count, keys, qs, lives, peak, weighted, peaks, exps, gprobs, dq):
    keys_t = keys.T
    probs, dscores = [], []
    for h in range(count):
        at, g = base + h, group + h
        factor = jnp.exp2(peaks[at] - peak[g])
        prob = exps[at].reshape(CHUNK // 8, 8, ROWS) * factor[None]
        dscore = prob * (gprobs[at].reshape(CHUNK // 8, 8, ROWS) - weighted[g][None])
        probs.append(prob.reshape(CHUNK, ROWS).astype(jnp.bfloat16))
        dscore = dscore.reshape(CHUNK, ROWS).astype(jnp.bfloat16)
        dscores.append(dscore)
        dq[g] += dot(keys_t, dscore, PLAIN)
    rows = pl.ds(group, count)
    grad_v = dot(jnp.concatenate(probs, axis=1), lives[rows].reshape(count * ROWS, HD), PLAIN)
    grad_k = dot(jnp.concatenate(dscores, axis=1), qs[rows].reshape(count * ROWS, HD), PLAIN)
    return grad_k, grad_v


def kernel(lengths, q_hbm, pk_hbm, pv_hbm, rk_hbm, rv_hbm, g_hbm, dq_hbm, drk_hbm, drv_hbm, dpk_hbm, dpv_hbm,
           q, pk, pv, rk, rv, g, dq_out, drk, drv, dpk, dpv,
           qs, lives, peak, denom, weighted, peaks, exps, gprobs, dq, dq_send, dq_in,
           stat_out, stat_in, packed, kv, own, ring_out, ring_in, z_out, z_in,
           local_s, swap_s, swap_r, stat_s, stat_r, dq_s, dq_r, get_s, get_r, ring_s, ring_r, z_s, z_r):
    heads = q.shape[1] // HD
    resp, tensor = lax.axis_index("resp"), lax.axis_index("tensor")
    chip, core = resp // 2, resp % 2
    up = {"resp": (chip + 1) % 4 * 2 + core}
    down = {"resp": (chip + 3) % 4 * 2 + core}
    across = {"resp": (chip + 2) % 4 * 2 + core}
    twin = {"resp": chip * 2 + 1 - core}

    def along(turn):
        return {"tensor": (tensor + turn) % 4}

    def columns(index):
        return pl.ds(pl.multiple_of(index * HD, HD), HD)

    barrier = pltpu.get_barrier_semaphore()
    for other in (up, down, across, twin, along(1), along(2), along(3)):
        pl.semaphore_signal(barrier, inc=1, device_id=other, device_id_type=MESH)
    moves_in = [
        pltpu.make_async_copy(src, dst, local_s.at[i])
        for i, (src, dst) in enumerate(
            ((pk_hbm, pk), (pv_hbm, pv), (q_hbm, q), (g_hbm, g), (rk_hbm, rk), (rv_hbm, rv))
        )
    ]
    for move in moves_in:
        move.start()

    def send(src, dst, sems, at, to):
        return pltpu.make_async_remote_copy(
            src_ref=src, dst_ref=dst, send_sem=sems[0].at[at], recv_sem=sems[1].at[at],
            device_id=to, device_id_type=MESH,
        )

    def get(n, kind):
        mine, far = kv.at[*place("c", n)], kv.at[*place("d", n)]
        src, dst, to = {
            SPREAD: (packed.at[n], mine, along(TURN[n])),
            AHEAD: (mine, kv.at[n, 0], up),
            BEHIND: (mine, kv.at[n, 1], down),
            ACROSS: (mine, far, across),
        }[kind]
        return [send(src, dst, (get_s, get_r), (n, kind), to)]

    def start(copies):
        for copy in copies:
            copy.start()

    def received(copies):
        for copy in copies:
            copy.wait_recv()

    def begin(n):
        if n:
            received(get(n, SPREAD))
        for kind in (AHEAD, BEHIND, ACROSS):
            start(get(n, kind))

    def near_received(n):
        received(get(n, AHEAD) + get(n, BEHIND))

    def swap():
        here, there = pl.ds(0, heads), pl.ds(heads, heads)
        return [send(ref.at[here], ref.at[there], (swap_s, swap_r), i, twin) for i, ref in enumerate((qs, lives))]

    positions = lax.broadcasted_iota(jnp.int32, (ROWS, HD), 0)
    alive = positions < lengths[0]
    moves_in[0].wait()
    moves_in[1].wait()
    kv[4, 0, 0] = pk[:, columns(tensor)]
    kv[4, 0, 1] = pv[:, columns(tensor)]
    for n in range(1, ROUNDS):
        cols = columns((tensor + TURN[n]) % 4)
        packed[n, 0] = pk[:, cols]
        packed[n, 1] = pv[:, cols]
    pl.semaphore_wait(barrier, 7)
    for n in range(1, ROUNDS):
        start(get(n, SPREAD))
    begin(0)
    moves_in[2].wait()
    moves_in[3].wait()
    for h in range(heads):
        cols = slice(h * HD, (h + 1) * HD)
        qs[h] = q[:, cols]
        lives[h] = jnp.where(alive, g[:, cols], jnp.zeros((), jnp.bfloat16))
    start(swap())
    moves_in[4].wait()
    moves_in[5].wait()
    peak[...] = jnp.full(peak.shape, NEG, jnp.float32)
    denom[...] = jnp.zeros(denom.shape, jnp.float32)
    weighted[...] = jnp.zeros(weighted.shape, jnp.float32)
    dq[...] = jnp.zeros(dq.shape, jnp.float32)
    own[...] = jnp.zeros(own.shape, jnp.float32)
    causal = lax.broadcasted_iota(jnp.int32, (CHUNK, ROWS), 0) <= lax.broadcasted_iota(jnp.int32, (CHUNK, ROWS), 1)
    sums = (qs, lives, peak, denom, weighted, peaks, exps, gprobs)
    steps = len(FIRST)
    attend(steps * heads, 0, heads, rk[...], rv[...], causal, *sums)

    def far_received(*rounds):
        for n in rounds:
            received(get(n, ACROSS))

    before = {
        "b0o": (lambda: near_received(0),),
        "b0t": (lambda: received(swap()),),
        "b1o": (lambda: near_received(1),),
        "b2t": (lambda: near_received(2),),
        "b3t": (lambda: near_received(3),),
        "d0t": (lambda: far_received(0, 1),),
        "d1t": (lambda: far_received(2, 3),),
    }
    after = {
        "b0o": (lambda: begin(1), lambda: begin(2)),
        "c0t": (lambda: begin(3),),
    }

    def serve(step, order, table):
        for name, jobs in table.items():
            @pl.when(step == order.index(name))
            def _():
                for job in jobs:
                    job()

    def first(step, carry):
        chunk, half = pick(step, FIRST)
        serve(step, FIRST, before)
        keys = kv[chunk, :, 0].reshape(CHUNK, HD)
        vals = kv[chunk, :, 1].reshape(CHUNK, HD)
        attend((chunk * 2 + half) * heads, half * heads, heads, keys, vals, None, *sums)
        serve(step, FIRST, after)

        @pl.when(step == FIRST.index("d1t"))
        def _():
            join_sums(heads, heads, peak, denom, weighted, stat_out.at[1])
            tell(1).start()

        return carry

    def tell(half):
        return send(stat_out.at[half], stat_in.at[1 - half], (stat_s, stat_r), 1 - half, twin)

    lax.fori_loop(0, steps, first, 0)
    join_sums(0, heads, peak, denom, weighted, stat_out.at[0])
    tell(0).start()
    tell(1).wait_recv()
    finish_stats(0, heads, stat_out.at[0], stat_in.at[0], peak, weighted)

    def to_ring(n, way):
        to = (up, down, across)[way]
        return [send(ring_out.at[n, way], ring_in.at[n, way], (ring_s, ring_r), (n, way), to)]

    def to_holder(n):
        return [send(z_out.at[n], z_in.at[n], (z_s, z_r), n, along(4 - TURN[n]))]

    def to_owner():
        return send(dq_send, dq_in, (dq_s, dq_r), 0, twin)

    def wide(ref):
        return ref.astype(jnp.float32)

    def send_far(n):
        ring_out[n, 2] = own[place("d", n)].astype(jnp.bfloat16)
        start(to_ring(n, 2))

    def send_near(n):
        for way in range(2):
            ring_out[n, way] = own[n, 1 - way].astype(jnp.bfloat16)
            start(to_ring(n, way))

    def total(n):
        for way in range(3):
            received(to_ring(n, way))
        return own[place("c", n)] + wide(ring_in[n, 0]) + wide(ring_in[n, 1]) + wide(ring_in[n, 2])

    def hand_over(n):
        z_out[n] = total(n).astype(jnp.bfloat16)
        start(to_holder(n))

    def learn():
        tell(0).wait_recv()
        finish_stats(heads, heads, stat_out.at[1], stat_in.at[1], peak, weighted)

    def return_queries():
        for h in range(heads):
            dq_send[h] = dq[heads + h].astype(jnp.bfloat16)
        to_owner().start()

    services = {
        "b3o": (learn,),
        "d1t": (lambda: send_far(3), lambda: send_far(2)),
        "d0t": (lambda: send_far(1), lambda: send_far(0)),
        "b3t": (lambda: send_near(3),),
        "b2t": (lambda: send_near(2),),
        "b1t": (lambda: send_near(1),),
        "c1o": (lambda: hand_over(3), lambda: hand_over(2)),
        "c0o": (lambda: hand_over(1),),
        "b0t": (return_queries,),
        "b0o": (lambda: send_near(0),),
    }

    def second(step, carry):
        chunk, half = pick(step, SECOND)
        keys = kv[chunk, :, 0].reshape(CHUNK, HD)
        grad_k, grad_v = grads(
            (chunk * 2 + half) * heads, half * heads, heads, keys, qs, lives, peak, weighted, peaks, exps, gprobs, dq
        )
        grad_k = (grad_k * SCALE).reshape(2, QUARTER, HD)
        grad_v = grad_v.reshape(2, QUARTER, HD)
        own[chunk, :, 0] += grad_k
        own[chunk, :, 1] += grad_v
        serve(step, SECOND, services)
        return carry

    lax.fori_loop(0, steps, second, 0)
    grad_k, grad_v = grads(steps * heads, 0, heads, rk[...], qs, lives, peak, weighted, peaks, exps, gprobs, dq)
    drk[...] = grad_k * SCALE
    drv[...] = grad_v
    moves_out = [
        pltpu.make_async_copy(src, dst, local_s.at[6 + i])
        for i, (src, dst) in enumerate((
            (drk, drk_hbm), (drv, drv_hbm), (dq_out, dq_hbm), (dpk, dpk_hbm), (dpv, dpv_hbm)
        ))
    ]
    moves_out[0].start()
    moves_out[1].start()
    to_owner().wait_recv()
    for h in range(heads):
        dq_out[:, h * HD : (h + 1) * HD] = (dq[h] + wide(dq_in[h])).T * SCALE
    moves_out[2].start()
    sums_now = total(0)
    dpk[:, columns(tensor)] = sums_now[0]
    dpv[:, columns(tensor)] = sums_now[1]
    for n in reversed(range(1, ROUNDS)):
        received(to_holder(n))
        cols = columns((tensor + TURN[n]) % 4)
        dpk[:, cols] = wide(z_in[n, 0])
        dpv[:, cols] = wide(z_in[n, 1])
    moves_out[3].start()
    moves_out[4].start()
    sent = swap() + [tell(0), tell(1), to_owner()]
    for n in range(ROUNDS):
        for kind in range(SPREAD if n else AHEAD, ACROSS + 1):
            sent += get(n, kind)
        sent += to_ring(n, 0) + to_ring(n, 1) + to_ring(n, 2)
        if n:
            sent += to_holder(n)
    for copy in sent:
        copy.wait_send()
    for move in moves_out:
        move.wait()


def copy_kernel(*refs):
    sems = refs[-1]
    count = (len(refs) - 1) // 3
    ins, outs, rooms = refs[:count], refs[count : 2 * count], refs[2 * count : 3 * count]
    here = [pltpu.make_async_copy(ins[i], rooms[i], sems.at[0, i]) for i in range(count)]
    away = [pltpu.make_async_copy(rooms[i], outs[i], sems.at[1, i]) for i in range(count)]
    for move in here:
        move.start()
    for i in range(count):
        here[i].wait()
        away[i].start()
    for move in away:
        move.wait()


def local(prompt_k, prompt_v, resp_q, resp_k, resp_v, resp_grad, lengths):
    heads = resp_q.shape[1] // HD
    blocks = (len(FIRST) + 1) * heads
    anywhere = pl.BlockSpec(memory_space=pl.ANY)
    f32, bf16 = jnp.float32, jnp.bfloat16
    stat = pltpu.VMEM((2 * heads, 8, ROWS), f32)
    piece = (2, QUARTER, HD)

    def sems(*shape):
        return [pltpu.SemaphoreType.DMA(shape)] * 2

    outs = tuple(jax.ShapeDtypeStruct(x.shape, f32) for x in (resp_q, resp_k, resp_v, prompt_k, prompt_v))
    flops = 10 * blocks * CHUNK * ROWS * HD
    results = pl.pallas_call(
        kernel,
        out_shape=outs,
        in_specs=[pl.BlockSpec(memory_space=pltpu.SMEM)] + [anywhere] * 6,
        out_specs=[anywhere] * 5,
        scratch_shapes=[
            *(pltpu.VMEM(x.shape, bf16) for x in (resp_q, prompt_k, prompt_v, resp_k, resp_v, resp_grad)),
            *(pltpu.VMEM(x.shape, f32) for x in outs),
            pltpu.VMEM((2 * heads, ROWS, HD), bf16),
            pltpu.VMEM((2 * heads, ROWS, HD), bf16),
            stat,
            stat,
            stat,
            pltpu.VMEM((blocks, 8, ROWS), f32),
            pltpu.VMEM((blocks, CHUNK, ROWS), f32),
            pltpu.VMEM((blocks, CHUNK, ROWS), f32),
            pltpu.VMEM((2 * heads, HD, ROWS), f32),
            pltpu.VMEM((heads, HD, ROWS), bf16),
            pltpu.VMEM((heads, HD, ROWS), bf16),
            pltpu.VMEM((2, 3, 8, ROWS), f32),
            pltpu.VMEM((2, 3, 8, ROWS), f32),
            pltpu.VMEM((ROUNDS,) + piece, bf16),
            pltpu.VMEM((2 * ROUNDS, 2) + piece, bf16),
            pltpu.VMEM((2 * ROUNDS, 2) + piece, f32),
            pltpu.VMEM((ROUNDS, 3) + piece, bf16),
            pltpu.VMEM((ROUNDS, 3) + piece, bf16),
            pltpu.VMEM((ROUNDS,) + piece, bf16),
            pltpu.VMEM((ROUNDS,) + piece, bf16),
            pltpu.SemaphoreType.DMA((11,)),
            *sems(2),
            *sems(2),
            *sems(1),
            *sems(ROUNDS, 4),
            *sems(ROUNDS, 3),
            *sems(ROUNDS),
        ],
        compiler_params=pltpu.CompilerParams(
            vmem_limit_bytes=61 * 1024 * 1024, collective_id=0, has_side_effects=True
        ),
        cost_estimate=pl.CostEstimate(flops=flops, bytes_accessed=3 << 20, transcendentals=0),
    )(lengths, resp_q, prompt_k, prompt_v, resp_k, resp_v, resp_grad)
    return pl.pallas_call(
        copy_kernel,
        out_shape=outs,
        in_specs=[anywhere] * 5,
        out_specs=[anywhere] * 5,
        scratch_shapes=[pltpu.VMEM(x.shape, f32) for x in outs] + [pltpu.SemaphoreType.DMA((2, 5))],
        compiler_params=pltpu.CompilerParams(vmem_limit_bytes=61 * 1024 * 1024),
    )(*results)


def solution(mesh):
    rows = P(("dp", "resp", "tensor"), None)
    both = P(("dp", "resp"), "tensor")
    return jax.shard_map(
        local,
        mesh=mesh,
        in_specs=(rows, rows, both, both, both, both, P(("dp", "resp"))),
        out_specs=(both, both, both, rows, rows),
        check_vma=False,
    )
```
